32 devices in a mesh: section: 2 (over x), group: 4 (over y, core), replica: 4 (over z).
Axes of the slice: x: 2, y: 2, z: 4, core: 2. Of those that a mesh axis runs over, the one named last changes fastest.
Arguments:
- chars: bfloat16 [16384, 768], P(('group', 'replica')), may hold values from -6 to 6
- char_codes: int32 [16384], P(('group', 'replica')), may hold values from 0 to 44127, as said below
- mol_cotangent: bfloat16 [4096, 768], P(('group', 'replica')), may hold values from -6 to 6
- attn_norm_gain: bfloat16 [768], P('group'), may hold values from 0.5 to 1.5
- attn_norm_bias: bfloat16 [768], P('group'), may hold values from -1.75 to 1.75
- qkv_weight: bfloat16 [768, 2304], P('group'), may hold values from -0.21875 to 0.21875
- qv_bias: bfloat16 [1536], P('group'), may hold values from -3 to 3
- out_weight: bfloat16 [768, 768], P('group'), may hold values from -0.625 to 0.625
- out_bias: bfloat16 [768], P('group'), may hold values from -1.75 to 1.75
- ffn_norm_gain: bfloat16 [768], P('group'), may hold values from 0.5 to 1.5
- ffn_norm_bias: bfloat16 [768], P('group'), may hold values from -1.75 to 1.75
- ffn_in_weight: bfloat16 [768, 3072], P('group'), may hold values from -0.21875 to 0.21875
- ffn_in_bias: bfloat16 [3072], P('group'), may hold values from -3 to 3
- ffn_out_weight: bfloat16 [3072, 768], P('group'), may hold values from -0.109375 to 0.109375
- ffn_out_bias: bfloat16 [768], P('group'), may hold values from -1.75 to 1.75
- conv_weight: bfloat16 [3072, 768], P('group'), may hold values from -0.109375 to 0.109375
- conv_bias: bfloat16 [768], P('group'), may hold values from -3 to 3
- down_norm_gain: bfloat16 [768], P('group'), may hold values from 0.5 to 1.5
- down_norm_bias: bfloat16 [768], P('group'), may hold values from -1.75 to 1.75
Outputs:
- molecules: bfloat16 [4096, 768], P(('group', 'replica'), 'section')
- chars_grad: bfloat16 [16384, 768], P(('group', 'replica'), 'section')
- grad_attn_norm_gain: float32 [768], P('group')
- grad_attn_norm_bias: float32 [768], P('group')
- grad_qkv_weight: float32 [768, 2304], P('group')
- grad_qv_bias: float32 [1536], P('group')
- grad_out_weight: float32 [768, 768], P('group')
- grad_out_bias: float32 [768], P('group')
- grad_ffn_norm_gain: float32 [768], P('group')
- grad_ffn_norm_bias: float32 [768], P('group')
- grad_ffn_in_weight: float32 [768, 3072], P('group')
- grad_ffn_in_bias: float32 [3072], P('group')
- grad_ffn_out_weight: float32 [3072, 768], P('group')
- grad_ffn_out_bias: float32 [768], P('group')
- grad_conv_weight: float32 [3072, 768], P('group')
- grad_conv_bias: float32 [768], P('group')
- grad_down_norm_gain: float32 [768], P('group')
- grad_down_norm_bias: float32 [768], P('group')
The draws below stay inside these ranges and needn't reach their ends.
Inputs may be any that keep to these rules, and one draw needn't show every extreme that they name: `char_codes`: each row of 2048 characters holds nonzero codepoints up to its length and 0 after it; every row ends in padding.
All inputs are finite; a program needn't handle non-finite values.
Results may differ from the reference program's by a relative error of at most 0.02.
Values may be sent and summed in bfloat16 or wider, within the bound.
A program may use at most 320 MiB of HBM per device.

```python
import jax
import jax.numpy as jnp
from jax import lax

D = 768
HEADS = 12
HEAD_DIM = 64
FF = 3072
WIN = 128
KERNEL = 4
ROW_LEN = 2048
TOKENS = 16384


def draw_char_codes(key, part):
    key = jax.random.fold_in(key, 11)
    length_key, script_key, offset_key = jax.random.split(key, 3)
    row_count = TOKENS // ROW_LEN
    lengths = jax.random.randint(length_key, (row_count, 1), ROW_LEN // 4, ROW_LEN)
    script_starts = jnp.array([32, 1024, 2304, 12352, 19968, 44032], jnp.int32)
    script = jax.random.randint(script_key, (row_count, ROW_LEN), 0, 6)
    offset = jax.random.randint(offset_key, (row_count, ROW_LEN), 0, 96)
    code_values = script_starts[script] + offset
    position = jnp.arange(ROW_LEN, dtype=jnp.int32)[None, :]
    row_index = jnp.arange(row_count, dtype=jnp.int32)[:, None]
    code_values = jnp.where((row_index == 0) & (position == 0), 44127, code_values)
    code_values = jnp.where(position < lengths, code_values, 0)
    return code_values.reshape(TOKENS).astype(jnp.int32)


def level_of(own_key, dims, shards, smallest, largest):
    def one(dim, blocks):
        steps = jax.random.uniform(jax.random.fold_in(jax.random.fold_in(own_key, 6), dim), (blocks,), jnp.float32, smallest / len(shards), largest / len(shards))
        return jnp.repeat(jnp.exp(steps), dims[dim] // blocks).reshape((-1,) + (1,) * (len(dims) - dim - 1))

    loudness = one(*shards[0])
    for cut in shards[1:]:
        loudness = loudness * one(*cut)
    return loudness


def noise(own_key, extent, deviation, bound, cuts=(), kind=jnp.bfloat16):
    drawn = deviation * jax.random.normal(own_key, extent, jnp.float32)
    if cuts:
        drawn = drawn * level_of(own_key, extent, cuts, -0.22, 0.18)
    return jnp.clip(drawn, -bound, bound).astype(kind)


def setup_inputs(seed: int = 0) -> dict:
    key_list = jax.random.split(jax.random.key(seed), 20)
    return {
        "chars": noise(key_list[0], (TOKENS, D), 1.0, 6.0, ((0, 16),)),
        "char_codes": draw_char_codes(jax.random.fold_in(key_list[19], 71), 0),
        "mol_cotangent": noise(key_list[2], (TOKENS // KERNEL, D), 1.0, 6.0, ((0, 16),)),
        "attn_norm_gain": jnp.clip(1.0 + 0.1 * jax.random.normal(key_list[3], (D,), jnp.float32), 0.5, 1.5).astype(jnp.bfloat16),
        "attn_norm_bias": noise(key_list[4], (D,), 0.3, 1.75, ((0, 4),)),
        "qkv_weight": noise(key_list[5], (D, 3 * D), D ** -0.5, 0.21875, ((0, 4),)),
        "qv_bias": noise(key_list[6], (2 * D,), 0.5, 3.0, ((0, 4),)),
        "out_weight": noise(key_list[7], (D, D), (D // 8) ** -0.5, 0.625, ((0, 4),)),
        "out_bias": noise(key_list[8], (D,), 0.3, 1.75, ((0, 4),)),
        "ffn_norm_gain": jnp.clip(1.0 + 0.1 * jax.random.normal(key_list[9], (D,), jnp.float32), 0.5, 1.5).astype(jnp.bfloat16),
        "ffn_norm_bias": noise(key_list[10], (D,), 0.3, 1.75, ((0, 4),)),
        "ffn_in_weight": noise(key_list[11], (D, FF), D ** -0.5, 0.21875, ((0, 4),)),
        "ffn_in_bias": noise(key_list[12], (FF,), 0.5, 3.0, ((0, 4),)),
        "ffn_out_weight": noise(key_list[13], (FF, D), FF ** -0.5, 0.109375, ((0, 4),)),
        "ffn_out_bias": noise(key_list[14], (D,), 0.3, 1.75, ((0, 4),)),
        "conv_weight": noise(key_list[15], (KERNEL * D, D), (KERNEL * D) ** -0.5, 0.109375, ((0, 4),)),
        "conv_bias": noise(key_list[16], (D,), 0.5, 3.0, ((0, 4),)),
        "down_norm_gain": jnp.clip(1.0 + 0.1 * jax.random.normal(key_list[17], (D,), jnp.float32), 0.5, 1.5).astype(jnp.bfloat16),
        "down_norm_bias": noise(key_list[18], (D,), 0.3, 1.75, ((0, 4),)),
    }


@jax.custom_vjp
def low(v):
    return lax.optimization_barrier(v.astype(jnp.bfloat16)).astype(jnp.float32)

@jax.custom_vjp
def low_back(v):
    return v

def low_keep(v):
    return (low(v), None)

def low_pass(kept, grad):
    return (grad,)

def back_keep(v):
    return (v, None)

def back_low(kept, grad):
    return (low(grad),)
low.defvjp(low_keep, low_pass)
low_back.defvjp(back_keep, back_low)
norm_eps = 1e-06
mask_value = -10000.0
highest = lax.Precision.HIGHEST

def layer_norm(values, norm_gain, norm_shift):
    center = values - lax.optimization_barrier(jnp.mean(values, axis=-1, keepdims=True))
    spread = lax.optimization_barrier(jnp.mean(center * center, axis=-1, keepdims=True))
    return center * lax.rsqrt(spread + norm_eps) * norm_gain + norm_shift

def matmul(left_side, right_side):
    return jnp.dot(left_side, right_side, precision=highest, preferred_element_type=jnp.float32)

def gelu_exact(values):
    return jax.nn.gelu(values, approximate=False)

def forward_block(params, block_chars, key_bias):
    attn_norm_gain, attn_norm_bias, qkv_weight, qv_bias, out_weight, out_bias, ffn_norm_gain, ffn_norm_bias, ffn_in_weight, ffn_in_bias, ffn_out_weight, ffn_out_bias, conv_weight, conv_bias, down_norm_gain, down_norm_bias = params
    row_count = block_chars.shape[0]
    windows = row_count // WIN
    normed = low(layer_norm(block_chars, attn_norm_gain, attn_norm_bias))
    bias_row = jnp.concatenate([qv_bias[:D], jnp.zeros((D,), jnp.float32), qv_bias[D:]])
    projected = low_back(low(matmul(normed, qkv_weight) + bias_row))
    heads_split = projected.reshape(windows, WIN, 3, HEADS, HEAD_DIM)
    queries = heads_split[:, :, 0]
    keys_all = heads_split[:, :, 1]
    values_all = heads_split[:, :, 2]
    scores = jnp.einsum('wqhd,wkhd->whqk', queries, keys_all, precision=highest) * HEAD_DIM ** (-0.5)
    scores = low_back(scores + key_bias)
    prob_weights = low(jax.nn.softmax(scores, axis=-1))
    context = jnp.einsum('whqk,wkhd->wqhd', prob_weights, values_all, precision=highest)
    context = low_back(low(context.reshape(row_count, D)))
    attended = low_back(matmul(context, out_weight) + out_bias)
    hidden = block_chars + attended
    normed_ffn = low(layer_norm(hidden, ffn_norm_gain, ffn_norm_bias))
    inner_act = low_back(matmul(normed_ffn, ffn_in_weight) + ffn_in_bias)
    active = low(gelu_exact(inner_act))
    layer_out = low_back(low(hidden + matmul(active, ffn_out_weight) + ffn_out_bias))
    stacked = layer_out.reshape(row_count // KERNEL, KERNEL * D)
    conv_out = low_back(matmul(stacked, conv_weight) + conv_bias)
    return layer_norm(gelu_exact(conv_out), down_norm_gain, down_norm_bias)

def reference(chars, char_codes, mol_cotangent, attn_norm_gain, attn_norm_bias, qkv_weight, qv_bias, out_weight, out_bias, ffn_norm_gain, ffn_norm_bias, ffn_in_weight, ffn_in_bias, ffn_out_weight, ffn_out_bias, conv_weight, conv_bias, down_norm_gain, down_norm_bias):
    params = tuple((weight.astype(jnp.float32) for weight in (attn_norm_gain, attn_norm_bias, qkv_weight, qv_bias, out_weight, out_bias, ffn_norm_gain, ffn_norm_bias, ffn_in_weight, ffn_in_bias, ffn_out_weight, ffn_out_bias, conv_weight, conv_bias, down_norm_gain, down_norm_bias)))
    block_count = TOKENS // ROW_LEN
    chars_blocks = chars.astype(jnp.float32).reshape(block_count, ROW_LEN, D)
    bias_blocks = jnp.where(char_codes != 0, 0.0, mask_value).astype(jnp.float32)
    bias_blocks = bias_blocks.reshape(block_count, ROW_LEN // WIN, 1, 1, WIN)
    cot_blocks = mol_cotangent.astype(jnp.float32).reshape(block_count, ROW_LEN // KERNEL, D)

    def block_step(totals, pieces):
        block_chars, key_bias, block_cot = pieces

        def forward(weights, inputs):
            return forward_block(weights, inputs, key_bias)
        outputs, pullback = jax.vjp(forward, params, block_chars)
        weight_grads, input_grad = pullback(block_cot)
        totals = jax.tree.map(jnp.add, totals, weight_grads)
        return (totals, (outputs.astype(jnp.bfloat16), input_grad.astype(jnp.bfloat16)))
    initial = tuple((jnp.zeros_like(weight) for weight in params))
    totals, (mol_blocks, grad_blocks) = lax.scan(block_step, initial, (chars_blocks, bias_blocks, cot_blocks))
    return (mol_blocks.reshape(TOKENS // KERNEL, D), grad_blocks.reshape(TOKENS, D), totals[0], totals[1], totals[2], totals[3], totals[4], totals[5], totals[6], totals[7], totals[8], totals[9], totals[10], totals[11], totals[12], totals[13], totals[14], totals[15])
```

```python
import jax
import jax.numpy as jnp
from jax import lax
from jax.experimental import pallas as pl
from jax.experimental.pallas import tpu as pltpu
from jax.sharding import PartitionSpec as P

D = 768
HEADS = 12
HEAD_DIM = 64
FF = 3072
WIN = 128
KERNEL = 4


norm_eps = 1e-06
mask_value = -10000.0


def layer_norm(values, norm_gain, norm_shift):
    center = values - jnp.mean(values, axis=-1, keepdims=True)
    spread = jnp.mean(center * center, axis=-1, keepdims=True)
    return center * lax.rsqrt(spread + norm_eps) * norm_gain + norm_shift


def gelu_exact(values):
    return jax.nn.gelu(values, approximate=False)


def project(left_side, right_side):
    return jnp.dot(left_side, right_side, preferred_element_type=jnp.float32)


def contract_rows(left_side, right_side):
    return lax.dot_general(
        left_side, right_side, (((0,), (0,)), ((), ())), preferred_element_type=jnp.float32
    )


def times_transpose(left_side, right_side):
    return lax.dot_general(
        left_side, right_side, (((1,), (1,)), ((), ())), preferred_element_type=jnp.float32
    )


def norm_back(values, norm_gain, norm_shift, grad_out):
    outputs, pullback = jax.vjp(layer_norm, values, norm_gain, norm_shift)
    return pullback(grad_out)


def window_bias(row_codes):
    windows = row_codes.shape[0] // WIN
    return (
        jnp.where(row_codes != 0, 0.0, mask_value).astype(jnp.float32).reshape(windows, 1, 1, WIN)
    )


def attention_scores(queries, keys_all, key_bias):
    raw_scores = jnp.einsum(
        "wqhd,wkhd->whqk", queries, keys_all, preferred_element_type=jnp.float32
    )
    return raw_scores * HEAD_DIM ** (-0.5) + key_bias


def first_forward(weights, row_chars, row_codes):
    (
        attn_norm_gain,
        attn_norm_bias,
        qkv_weight,
        qv_bias,
        out_weight,
        out_bias,
        ffn_norm_gain,
        ffn_norm_bias,
        ffn_in_weight,
        ffn_in_bias,
        ffn_out_weight,
        ffn_out_bias,
    ) = weights[:12]
    row_count = row_chars.shape[0]
    windows = row_count // WIN
    chars_wide = row_chars.astype(jnp.float32)
    normed = layer_norm(
        chars_wide, attn_norm_gain.astype(jnp.float32), attn_norm_bias.astype(jnp.float32)
    ).astype(jnp.bfloat16)
    bias_row = jnp.concatenate([qv_bias[:D], jnp.zeros((D,), jnp.bfloat16), qv_bias[D:]]).astype(
        jnp.float32
    )
    projected = (project(normed, qkv_weight) + bias_row).astype(jnp.bfloat16)
    heads_split = projected.reshape(windows, WIN, 3, HEADS, HEAD_DIM)
    scores = attention_scores(heads_split[:, :, 0], heads_split[:, :, 1], window_bias(row_codes))
    top_score = jnp.max(scores, axis=-1, keepdims=True)
    log_total = top_score + jnp.log(jnp.sum(jnp.exp(scores - top_score), axis=-1, keepdims=True))
    prob_weights = jnp.exp(scores - log_total).astype(jnp.bfloat16)
    context = jnp.einsum(
        "whqk,wkhd->wqhd", prob_weights, heads_split[:, :, 2], preferred_element_type=jnp.float32
    )
    context = context.reshape(row_count, D).astype(jnp.bfloat16)
    hidden = chars_wide + project(context, out_weight) + out_bias.astype(jnp.float32)
    normed_ffn = layer_norm(
        hidden, ffn_norm_gain.astype(jnp.float32), ffn_norm_bias.astype(jnp.float32)
    ).astype(jnp.bfloat16)
    inner_act = project(normed_ffn, ffn_in_weight) + ffn_in_bias.astype(jnp.float32)
    active = gelu_exact(inner_act).astype(jnp.bfloat16)
    layer_out = hidden + project(active, ffn_out_weight) + ffn_out_bias.astype(jnp.float32)
    kept = (normed, projected, log_total, context, hidden, normed_ffn, inner_act, active)
    return (layer_out.astype(jnp.bfloat16), kept)


def first_backward(weights, row_chars, row_codes, kept, grad_out):
    (
        attn_norm_gain,
        attn_norm_bias,
        qkv_weight,
        qv_bias,
        out_weight,
        out_bias,
        ffn_norm_gain,
        ffn_norm_bias,
        ffn_in_weight,
        ffn_in_bias,
        ffn_out_weight,
        ffn_out_bias,
    ) = weights[:12]
    normed, projected, log_total, context, hidden, normed_ffn, inner_act, active = kept
    row_count = row_chars.shape[0]
    windows = row_count // WIN
    grad_layer = grad_out.astype(jnp.float32)
    grad_ffn_out_weight = contract_rows(active, grad_out)
    grad_ffn_out_bias = jnp.sum(grad_layer, axis=0)
    grad_active = times_transpose(grad_out, ffn_out_weight)
    gelu_value, gelu_pull = jax.vjp(gelu_exact, inner_act)
    grad_inner = gelu_pull(grad_active)[0].astype(jnp.bfloat16)
    grad_ffn_in_weight = contract_rows(normed_ffn, grad_inner)
    grad_ffn_in_bias = jnp.sum(grad_inner.astype(jnp.float32), axis=0)
    grad_hidden_norm, grad_ffn_norm_gain, grad_ffn_norm_bias = norm_back(
        hidden,
        ffn_norm_gain.astype(jnp.float32),
        ffn_norm_bias.astype(jnp.float32),
        times_transpose(grad_inner, ffn_in_weight),
    )
    grad_hidden = grad_layer + grad_hidden_norm
    grad_attended = grad_hidden.astype(jnp.bfloat16)
    grad_out_weight = contract_rows(context, grad_attended)
    grad_out_bias = jnp.sum(grad_attended.astype(jnp.float32), axis=0)
    grad_context = times_transpose(grad_attended, out_weight).astype(jnp.bfloat16)
    grad_context = grad_context.reshape(windows, WIN, HEADS, HEAD_DIM)
    heads_split = projected.reshape(windows, WIN, 3, HEADS, HEAD_DIM)
    queries = heads_split[:, :, 0]
    keys_all = heads_split[:, :, 1]
    values_all = heads_split[:, :, 2]
    scores = attention_scores(queries, keys_all, window_bias(row_codes))
    prob_exact = jnp.exp(scores - log_total)
    prob_weights = prob_exact.astype(jnp.bfloat16)
    grad_probs = jnp.einsum(
        "wqhd,wkhd->whqk", grad_context, values_all, preferred_element_type=jnp.float32
    )
    grad_values = jnp.einsum(
        "whqk,wqhd->wkhd", prob_weights, grad_context, preferred_element_type=jnp.float32
    )
    row_inner = jnp.sum(prob_exact * grad_probs, axis=-1, keepdims=True)
    grad_scores = (prob_exact * (grad_probs - row_inner)).astype(jnp.bfloat16)
    scale_factor = HEAD_DIM ** (-0.5)
    grad_queries = (
        jnp.einsum("whqk,wkhd->wqhd", grad_scores, keys_all, preferred_element_type=jnp.float32)
        * scale_factor
    )
    grad_keys = (
        jnp.einsum("whqk,wqhd->wkhd", grad_scores, queries, preferred_element_type=jnp.float32)
        * scale_factor
    )
    grad_projected = jnp.stack([grad_queries, grad_keys, grad_values], axis=2).astype(jnp.bfloat16)
    grad_projected = grad_projected.reshape(row_count, 3 * D)
    grad_qkv_weight = contract_rows(normed, grad_projected)
    column_sums = jnp.sum(grad_projected.astype(jnp.float32), axis=0)
    grad_qv_bias = jnp.concatenate([column_sums[:D], column_sums[2 * D :]])
    grad_chars_norm, grad_attn_norm_gain, grad_attn_norm_bias = norm_back(
        row_chars.astype(jnp.float32),
        attn_norm_gain.astype(jnp.float32),
        attn_norm_bias.astype(jnp.float32),
        times_transpose(grad_projected, qkv_weight),
    )
    grad_chars = grad_hidden + grad_chars_norm
    return (
        grad_chars,
        (
            grad_attn_norm_gain,
            grad_attn_norm_bias,
            grad_qkv_weight,
            grad_qv_bias,
            grad_out_weight,
            grad_out_bias,
            grad_ffn_norm_gain,
            grad_ffn_norm_bias,
            grad_ffn_in_weight,
            grad_ffn_in_bias,
            grad_ffn_out_weight,
            grad_ffn_out_bias,
        ),
    )


def second_layer(weights, handed, cotangent):
    conv_weight, conv_bias, down_norm_gain, down_norm_bias = weights[12:]
    row_count = handed.shape[0]
    stacked = handed.reshape(row_count // KERNEL, KERNEL * D)
    conv_out = project(stacked, conv_weight) + conv_bias.astype(jnp.float32)

    def tail_part(values, norm_gain, norm_shift):
        return layer_norm(gelu_exact(values), norm_gain, norm_shift)

    mol_values, pullback = jax.vjp(
        tail_part, conv_out, down_norm_gain.astype(jnp.float32), down_norm_bias.astype(jnp.float32)
    )
    grad_conv, grad_down_norm_gain, grad_down_norm_bias = pullback(cotangent.astype(jnp.float32))
    grad_conv = grad_conv.astype(jnp.bfloat16)
    grad_conv_weight = contract_rows(stacked, grad_conv)
    grad_conv_bias = jnp.sum(grad_conv.astype(jnp.float32), axis=0)
    grad_handed = times_transpose(grad_conv, conv_weight).astype(jnp.bfloat16).reshape(row_count, D)
    return (
        mol_values.astype(jnp.bfloat16),
        grad_handed,
        (grad_conv_weight, grad_conv_bias, grad_down_norm_gain, grad_down_norm_bias),
    )


MESH = pl.DeviceIdType.MESH
GROUPS = 4
RING = 4
SHARD = D // GROUPS
PIECE = SHARD // RING
WIDE = 512
SIDE = D - WIDE
HALF = SHARD // 2
CHUNKS = (
    [(0, "col", j) for j in range(3)]
    + [(1, "col", 0)]
    + [(2, "col", j) for j in range(4)]
    + [(3, "row", j) for j in range(4)]
    + [(4, "row", j) for j in range(4)]
)
COUNT = len(CHUNKS)
FULL_SHAPES = [(D, 3 * D), (D, D), (D, FF), (FF, D), (KERNEL * D, D)]
SHARD_SHAPES = [(rows // GROUPS, cols) for rows, cols in FULL_SHAPES]
VEC = (16, 256)


def at16(value):
    return pl.multiple_of(value, 16)


def whole_block(refs, chunk, shard, first, rows):
    mat, kind, j = CHUNKS[chunk]
    if kind == "col":
        return refs[mat].at[pl.ds(at16(shard * SHARD + first), rows), pl.ds(j * D, D)]
    return refs[mat].at[pl.ds(at16(shard * D + j * SHARD + first), rows), :]


def shard_block(refs, chunk, first, rows, col=0, cols=D):
    mat, kind, j = CHUNKS[chunk]
    if kind == "col":
        return refs[mat].at[pl.ds(at16(first), rows), pl.ds(j * D + col, cols)]
    return refs[mat].at[pl.ds(at16(j * SHARD + first), rows), pl.ds(col, cols)]


def places():
    s, g, r = lax.axis_index("section"), lax.axis_index("group"), lax.axis_index("replica")
    near = {
        "c": (s, g ^ 1, r),
        "y": (s, g ^ 2, r),
        "x": (1 - s, g, r),
        "z1": (s, g, r ^ 1),
        "z3": (s, g, r ^ 3),
    }
    return s, g, r, near


def greet(targets):
    barrier = pltpu.get_barrier_semaphore()
    for target in targets:
        pl.semaphore_signal(barrier, inc=1, device_id=target, device_id_type=MESH)
    pl.semaphore_wait(barrier, len(targets))


def remote(src, dst, send, recv, target):
    return pltpu.make_async_remote_copy(
        src_ref=src,
        dst_ref=dst,
        send_sem=send,
        recv_sem=recv,
        device_id=target,
        device_id_type=MESH,
    )


def gather_kernel(*refs):
    shards, vec, full, vecs = refs[:5], refs[5], refs[6:11], refs[11]
    send, recv, own, vec_send, vec_recv = refs[12:]
    s, g, r, near = places()
    greet(list(near.values()) + [(s, g ^ 3, r)])
    kinds = ("y", "x", "z1", "z3")
    mine = lax.rem(r + 2 * s, RING)
    piece = {
        "y": mine,
        "x": lax.rem(mine + 2, RING),
        "z1": lax.rem((r ^ 1) + 2 * s, RING),
        "z3": lax.rem((r ^ 3) + 2 * s, RING),
    }
    other = g ^ 2
    started = []

    def go(copy):
        copy.start()
        started.append(copy)

    def block(chunk, shard, p):
        return whole_block(full, chunk, shard, p * PIECE, PIECE)

    for k in range(COUNT):
        go(
            remote(
                shard_block(shards, k, mine * PIECE, PIECE),
                block(k, g, mine),
                send.at[0, k],
                recv.at[0, k],
                near["y"],
            )
        )
    vec_copies = [
        remote(vec, vecs.at[g], vec_send.at[i], vec_recv.at[i], (s, g ^ i, r)) for i in (1, 2, 3)
    ]
    for copy in vec_copies:
        go(copy)
    locals_ = [pltpu.make_async_copy(vec, vecs.at[g], vec_send.at[0])]
    locals_[0].start()
    for k in range(COUNT):
        copy = pltpu.make_async_copy(
            shard_block(shards, k, 0, SHARD), whole_block(full, k, g, 0, SHARD), own.at[k]
        )
        copy.start()
        locals_.append(copy)
        go(
            remote(
                shard_block(shards, k, 0, SHARD),
                whole_block(full, k, g, 0, SHARD),
                send.at[4, k],
                recv.at[4, k],
                near["c"],
            )
        )

    def arrived(i, k):
        p = piece[kinds[i]]
        here = block(k, other, p)
        remote(here, here, send.at[i, k], recv.at[i, k], near[kinds[i]]).wait_recv()
        return here

    for k in range(COUNT + 1):
        if k < COUNT:
            here = arrived(0, k)
            for i in (1, 2, 3):
                go(remote(here, here, send.at[i, k], recv.at[i, k], near[kinds[i]]))
            remote(here, here, send.at[5, k], recv.at[5, k], near["c"]).start()
        if k >= 1:
            for i in (1, 2, 3):
                here = arrived(i, k - 1)
                remote(here, here, send.at[5, k - 1], recv.at[5, k - 1], near["c"]).start()
    for copy in started:
        copy.wait_send()
    for k in range(COUNT):
        theirs = whole_block(full, k, g ^ 1, 0, SHARD)
        remote(theirs, theirs, send.at[4, k], recv.at[4, k], near["c"]).wait_recv()
        sent = whole_block(full, k, other, 0, SHARD)
        remote(sent, sent, send.at[5, k], recv.at[5, k], near["c"]).wait_send()
        theirs = whole_block(full, k, g ^ 3, 0, SHARD)
        remote(theirs, theirs, send.at[5, k], recv.at[5, k], near["c"]).wait_recv()
    for copy in vec_copies:
        copy.wait_recv()
    for copy in locals_:
        copy.wait()


def gather_weights(shards, vec):
    anywhere = pl.BlockSpec(memory_space=pl.ANY)
    dma = pltpu.SemaphoreType.DMA
    out = pl.pallas_call(
        gather_kernel,
        name="gather_weights",
        out_shape=[jax.ShapeDtypeStruct(shape, jnp.bfloat16) for shape in FULL_SHAPES]
        + [jax.ShapeDtypeStruct((GROUPS,) + VEC, jnp.bfloat16)],
        in_specs=[anywhere] * 6,
        out_specs=[anywhere] * 6,
        scratch_shapes=[dma((6, COUNT)), dma((6, COUNT)), dma((COUNT,)), dma((4,)), dma((4,))],
        compiler_params=pltpu.CompilerParams(collective_id=0, has_side_effects=True),
    )(*shards, vec)
    return out[:5], out[5]


def add_into(dst, row, rows, col, cols, src, src_row=0):
    @pl.loop(0, rows // 16)
    def _(i):
        here = pl.ds(at16(row + i * 16), 16)
        there = pl.ds(at16(src_row + i * 16), 16)
        columns = pl.ds(pl.multiple_of(col, 128), cols)
        dst[here, columns] = dst[here, columns] + src[there, :]


STAGES = 8


def reduce_kernel(extra, *refs):
    grads, vec, out, vec_out = refs[:5], refs[5], refs[6:11], refs[11]
    (held, core_in, y_in, z1_in, z3_in, x_in, e3_in, e1_in, ex_in, ey_in, more_in) = refs[12:23]
    vec_held, vec_in = refs[23:25]
    (load, send, recv, more_send, more_recv, more_free, done, vec_send, vec_recv) = refs[25:]
    s, g, r, near = places()
    far = [(s, g, r ^ (RING << i)) for i in range(extra)]
    greet(list(near.values()) + far)
    y, c = g // 2, lax.rem(g, 2)
    bit0, bit1 = lax.rem(r, 2), lax.rem(r // 2, 2)
    first = lax.rem(bit0 + bit1, 2)
    second = bit1
    side_first, side_second = bit1, bit0
    mine, other = 2 * y + c, 2 * (1 - y) + c

    def spot(k, q):
        return pl.multiple_of(k * D + q * SHARD, 16)

    loads = {}
    for k in range(COUNT):
        loads[k] = []
        for q in range(GROUPS):
            copy = pltpu.make_async_copy(
                whole_block(grads, k, q, 0, SHARD),
                held.at[pl.ds(k * D + q * SHARD, SHARD)],
                load.at[k, q],
            )
            copy.start()
            loads[k].append(copy)

    started = []

    def go(k, i, src, dst, way):
        copy = remote(src, dst, send.at[i, k], recv.at[i, k], near[way])
        copy.start()
        started.append(copy)
        return copy

    flight = {}

    def cut(k, q, row, rows, col, cols):
        return held.at[pl.ds(at16(spot(k, q) + row), rows), pl.ds(pl.multiple_of(col, 128), cols)]

    b_row1 = first * HALF
    b_row2 = b_row1 + second * PIECE
    b_col = s * (WIDE // 2)
    e_row1 = side_first * HALF
    e_row2 = e_row1 + side_second * PIECE
    e_col = WIDE + s * (SIDE // 2)

    def final(k, row, rows, col, cols):
        return shard_block(out, k, row, rows, pl.multiple_of(col, 128), cols)

    def stage(n, k):
        if n == 0:
            for copy in loads[k]:
                copy.wait()
            flight[k] = [
                go(
                    k,
                    i,
                    held.at[pl.ds(spot(k, 2 * i + 1 - c), SHARD)],
                    core_in.at[k, i],
                    "c",
                )
                for i in range(2)
            ]
            return
        for copy in flight[k]:
            copy.wait_recv()
        if n == 1:
            for i in range(2):
                add_into(held, spot(k, 2 * i + c), SHARD, 0, D, core_in.at[k, i])
            flight[k] = [
                go(k, 2, cut(k, other, 0, SHARD, 0, WIDE), y_in.at[k], "y"),
                go(k, 3, cut(k, c, (1 - side_first) * HALF, HALF, WIDE, SIDE), e3_in.at[k, 0], "z3"),
                go(
                    k,
                    4,
                    cut(k, 2 + c, (1 - side_first) * HALF, HALF, WIDE, SIDE),
                    e3_in.at[k, 1],
                    "z3",
                ),
            ]
        if n == 2:
            add_into(held, spot(k, mine), SHARD, 0, WIDE, y_in.at[k])
            send_row = (1 - first) * HALF
            flight[k] = [go(k, 5, cut(k, mine, send_row, HALF, 0, WIDE), z1_in.at[k], "z1")]
            for i in range(2):
                add_into(held, spot(k, 2 * i + c) + e_row1, HALF, WIDE, SIDE, e3_in.at[k, i])
                flight[k].append(
                    go(
                        k,
                        6 + i,
                        cut(k, 2 * i + c, e_row1 + (1 - side_second) * PIECE, PIECE, WIDE, SIDE),
                        e1_in.at[k, i],
                        "z1",
                    )
                )
        if n == 3:
            add_into(held, spot(k, mine) + b_row1, HALF, 0, WIDE, z1_in.at[k])
            send_row = b_row1 + (1 - second) * PIECE
            flight[k] = [go(k, 8, cut(k, mine, send_row, PIECE, 0, WIDE), z3_in.at[k], "z3")]
            for i in range(2):
                add_into(held, spot(k, 2 * i + c) + e_row2, PIECE, WIDE, SIDE, e1_in.at[k, i])
                flight[k].append(
                    go(
                        k,
                        9 + i,
                        cut(k, 2 * i + c, e_row2, PIECE, WIDE + (1 - s) * (SIDE // 2), SIDE // 2),
                        ex_in.at[k, i],
                        "x",
                    )
                )
        if n == 4:
            add_into(held, spot(k, mine) + b_row2, PIECE, 0, WIDE, z3_in.at[k])
            flight[k] = [
                go(
                    k,
                    11,
                    cut(k, mine, b_row2, PIECE, (1 - s) * (WIDE // 2), WIDE // 2),
                    x_in.at[k],
                    "x",
                )
            ]
            for i in range(2):
                add_into(
                    held, spot(k, 2 * i + c) + e_row2, PIECE, e_col, SIDE // 2, ex_in.at[k, i]
                )
            flight[k].append(
                go(k, 12, cut(k, other, e_row2, PIECE, e_col, SIDE // 2), ey_in.at[k], "y")
            )
        if n == 5:
            add_into(held, spot(k, mine) + b_row2, PIECE, b_col, WIDE // 2, x_in.at[k])
            add_into(held, spot(k, mine) + e_row2, PIECE, e_col, SIDE // 2, ey_in.at[k])
            for i in range(extra):
                for part, (row, col, cols) in enumerate(
                    ((b_row2, b_col, WIDE // 2), (e_row2, e_col, SIDE // 2))
                ):
                    there = more_in.at[k, i, :, pl.ds(part * (WIDE // 2), cols)]
                    copy = remote(
                        cut(k, mine, row, PIECE, col, cols),
                        there,
                        more_send.at[part],
                        more_recv.at[k, i, part],
                        far[i],
                    )
                    copy.start()
                    copy.wait()
                    add_into(held, spot(k, mine) + row, PIECE, col, cols, there)
            b_now, e_now = (
                cut(k, mine, b_row2, PIECE, b_col, WIDE // 2),
                cut(k, mine, e_row2, PIECE, e_col, SIDE // 2),
            )
            b_there = final(k, b_row2, PIECE, b_col, WIDE // 2)
            e_there = final(k, e_row2, PIECE, e_col, SIDE // 2)
            flight[k] = [go(k, 13, b_now, b_there, "z3"), go(k, 14, e_now, e_there, "z1")]
            for i, (now, there) in enumerate(((b_now, b_there), (e_now, e_there))):
                copy = pltpu.make_async_copy(now, there, done.at[i, k])
                copy.start()
                flight[k, i] = copy
        if n == 6:
            for i in range(2):
                flight[k, i].wait()
            b_now = final(k, b_row1, HALF, b_col, WIDE // 2)
            e_now = final(k, e_row1, HALF, e_col, SIDE // 2)
            flight[k] = [go(k, 15, b_now, b_now, "z1"), go(k, 16, e_now, e_now, "z3")]
        if n == 7:
            b_now = final(k, 0, SHARD, b_col, WIDE // 2)
            e_now = final(k, 0, SHARD, e_col, SIDE // 2)
            flight[k] = [go(k, 17, b_now, b_now, "x"), go(k, 18, e_now, e_now, "x")]

    vec_load = pltpu.make_async_copy(vec, vec_held, vec_send.at[0])
    vec_load.start()
    vec_load.wait()
    vec_copies = [
        remote(
            vec_held.at[2 * i + 1 - c],
            vec_in.at[i],
            vec_send.at[1 + i],
            vec_recv.at[i],
            near["c"],
        )
        for i in range(2)
    ]
    for copy in vec_copies:
        copy.start()

    def vec_stage(n):
        if n == 0:
            for i in range(2):
                vec_copies[i].wait()
                vec_held[2 * i + c] = vec_held[2 * i + c] + vec_in[i]
            src = vec_held.at[other]
        else:
            vec_copies[-1].wait()
            vec_held[mine] = vec_held[mine] + vec_in[1 + n]
            src = vec_held.at[mine]
        ways = [near["y"], near["z1"], near["z3"], near["x"]] + far
        if n < len(ways):
            copy = remote(src, vec_in.at[2 + n], vec_send.at[3 + n], vec_recv.at[2 + n], ways[n])
            copy.start()
            vec_copies.append(copy)
        else:
            copy = pltpu.make_async_copy(vec_held.at[mine], vec_out, vec_send.at[0])
            copy.start()
            copy.wait()

    vec_steps = 5 + extra
    for i in range(COUNT + STAGES - 1):
        for n in reversed(range(STAGES)):
            k = i - n
            if 0 <= k < COUNT:
                stage(n, k)
        if 2 <= i < 2 + vec_steps:
            vec_stage(i - 2)
    for k in range(COUNT):
        for copy in flight[k]:
            copy.wait_recv()
    for copy in started:
        copy.wait_send()


def reduce_grads(grads, vec, extra):
    anywhere = pl.BlockSpec(memory_space=pl.ANY)
    dma = pltpu.SemaphoreType.DMA
    low = jnp.bfloat16
    vmem = pltpu.VMEM
    out = pl.pallas_call(
        lambda *refs: reduce_kernel(extra, *refs),
        name="reduce_grads",
        out_shape=[jax.ShapeDtypeStruct(shape, low) for shape in SHARD_SHAPES]
        + [jax.ShapeDtypeStruct(VEC, jnp.float32)],
        in_specs=[anywhere] * 6,
        out_specs=[anywhere] * 6,
        scratch_shapes=[
            vmem((COUNT * D, D), low),
            vmem((COUNT, 2, SHARD, D), low),
            vmem((COUNT, SHARD, WIDE), low),
            vmem((COUNT, HALF, WIDE), low),
            vmem((COUNT, PIECE, WIDE), low),
            vmem((COUNT, PIECE, WIDE // 2), low),
            vmem((COUNT, 2, HALF, SIDE), low),
            vmem((COUNT, 2, PIECE, SIDE), low),
            vmem((COUNT, 2, PIECE, SIDE // 2), low),
            vmem((COUNT, PIECE, SIDE // 2), low),
            vmem((COUNT, max(extra, 1), PIECE, D // 2), low),
            vmem((GROUPS,) + VEC, jnp.float32),
            vmem((6 + extra,) + VEC, jnp.float32),
            dma((COUNT, GROUPS)),
            dma((19, COUNT)),
            dma((19, COUNT)),
            dma((2,)),
            dma((COUNT, max(extra, 1), 2)),
            pltpu.SemaphoreType.REGULAR,
            dma((2, COUNT)),
            dma((7 + extra,)),
            dma((6 + extra,)),
        ],
        compiler_params=pltpu.CompilerParams(
            collective_id=1, has_side_effects=True, vmem_limit_bytes=56 << 20
        ),
    )(*grads, vec)
    return out[:5], out[5]


VEC_WIDTHS = [D, D, 2 * D, D, D, D, FF, D, D, D, D]


def pack_vectors(vectors, lead):
    rows = [v.reshape(lead + (-1, SHARD)) for v in vectors]
    stacked = jnp.concatenate(rows, axis=-2)
    pad = [(0, 0)] * len(lead) + [(0, VEC[0] - stacked.shape[-2]), (0, VEC[1] - SHARD)]
    return jnp.pad(stacked, pad)


def unpack_vectors(block):
    parts = []
    row = 0
    for width in VEC_WIDTHS:
        count = width // D
        parts.append(block[..., row : row + count, :SHARD].reshape(-1))
        row += count
    return parts


def body(
    chars,
    char_codes,
    mol_cotangent,
    attn_norm_gain,
    attn_norm_bias,
    qkv_weight,
    qv_bias,
    out_weight,
    out_bias,
    ffn_norm_gain,
    ffn_norm_bias,
    ffn_in_weight,
    ffn_in_bias,
    ffn_out_weight,
    ffn_out_bias,
    conv_weight,
    conv_bias,
    down_norm_gain,
    down_norm_bias,
):
    section = lax.axis_index("section")
    vectors = [
        attn_norm_gain,
        attn_norm_bias,
        qv_bias,
        out_bias,
        ffn_norm_gain,
        ffn_norm_bias,
        ffn_in_bias,
        ffn_out_bias,
        conv_bias,
        down_norm_gain,
        down_norm_bias,
    ]
    (qkv, outw, ffin, ffout, conv), vecs = gather_weights(
        [qkv_weight, out_weight, ffn_in_weight, ffn_out_weight, conv_weight],
        pack_vectors(vectors, ()),
    )
    (an_g, an_b, qv, ob, fn_g, fn_b, fib, fob, cb, dn_g, dn_b) = unpack_vectors(vecs)
    weights = (
        an_g, an_b, qkv, qv, outw, ob, fn_g, fn_b, ffin, fib, ffout, fob, conv, cb, dn_g, dn_b,
    )
    rows = chars.shape[0] // 2
    mols = rows // KERNEL
    my_chars = lax.dynamic_slice_in_dim(chars, section * rows, rows, 0)
    my_codes = lax.dynamic_slice_in_dim(char_codes, section * rows, rows, 0)
    my_cot = lax.dynamic_slice_in_dim(mol_cotangent, section * mols, mols, 0)
    layer_out, kept = first_forward(weights, my_chars, my_codes)
    mol, grad_handed, last = second_layer(weights, layer_out, my_cot)
    grad_chars, first = first_backward(weights, my_chars, my_codes, kept, grad_handed)
    half = D // 2

    def meet(whole):
        keep = lax.dynamic_slice_in_dim(whole, section * half, half, 1)
        give = lax.dynamic_slice_in_dim(whole, (1 - section) * half, half, 1)
        got = lax.ppermute(give, "section", [(0, 1), (1, 0)])
        return jnp.where(
            section == 0,
            jnp.concatenate([keep, got], axis=0),
            jnp.concatenate([got, keep], axis=0),
        )

    molecules = meet(mol)
    chars_grad = meet(grad_chars.astype(jnp.bfloat16))
    g_an_g, g_an_b, g_qkv, g_qv, g_out, g_ob, g_fn_g, g_fn_b, g_in, g_fib, g_ffo, g_fob = first
    g_conv, g_cb, g_dn_g, g_dn_b = last
    vec_grads = [g_an_g, g_an_b, g_qv, g_ob, g_fn_g, g_fn_b, g_fib, g_fob, g_cb, g_dn_g, g_dn_b]
    packed = pack_vectors([v.reshape(GROUPS, -1) for v in vec_grads], (GROUPS,))
    sums, vec_sum = reduce_grads(
        [w.astype(jnp.bfloat16) for w in (g_qkv, g_out, g_in, g_ffo, g_conv)],
        packed,
        (lax.axis_size("replica") // RING).bit_length() - 1,
    )
    t_qkv, t_out, t_in, t_ffo, t_conv = [w.astype(jnp.float32) for w in sums]
    v = unpack_vectors(vec_sum)
    return (
        molecules,
        chars_grad,
        v[0], v[1], t_qkv, v[2], t_out, v[3], v[4], v[5], t_in, v[6], t_ffo, v[7], t_conv,
        v[8], v[9], v[10],
    )


def solution(mesh):
    return jax.shard_map(
        body,
        mesh=mesh,
        in_specs=(
            P(("group", "replica"), None),
            P(("group", "replica")),
            P(("group", "replica"), None),
            P("group"),
            P("group"),
            P("group", None),
            P("group"),
            P("group", None),
            P("group"),
            P("group"),
            P("group"),
            P("group", None),
            P("group"),
            P("group", None),
            P("group"),
            P("group", None),
            P("group"),
            P("group"),
            P("group"),
        ),
        out_specs=(
            P(("group", "replica"), "section"),
            P(("group", "replica"), "section"),
            P("group"),
            P("group"),
            P("group", None),
            P("group"),
            P("group", None),
            P("group"),
            P("group"),
            P("group"),
            P("group", None),
            P("group"),
            P("group", None),
            P("group"),
            P("group", None),
            P("group"),
            P("group"),
            P("group"),
        ),
        check_vma=False,
    )
```

```python
import functools

import jax
import jax.numpy as jnp
from jax import lax
from jax.experimental import pallas as pl
from jax.experimental.pallas import tpu as pltpu
from jax.sharding import PartitionSpec as P

D = 768
HEADS = 12
HEAD_DIM = 64
FF = 3072
WIN = 128
KERNEL = 4
GROUPS = 4
RING = 4
SHARD = D // GROUPS
THIRD = SHARD // 3
HALF = D // 2
TILE = 256
PAIR = 2 * HEAD_DIM
PAIRS = HEADS // 2
RUN = WIN // KERNEL
BLOCKS = FF // D
VEC = (16, 256)
norm_eps = 1e-06
mask_value = -10000.0
MESH = pl.DeviceIdType.MESH
F32 = jnp.float32
LOW = jnp.bfloat16

CHUNKS = (
    [(0, "col", j) for j in range(3)]
    + [(1, "col", 0)]
    + [(2, "col", j) for j in range(4)]
    + [(3, "row", j) for j in range(4)]
    + [(4, "row", j) for j in range(4)]
)
COUNT = len(CHUNKS)
QKV, OUT, FIN, FOUT, CONV = BASES = (0, 3, 4, 8, 12)
SHARD_SHAPES = [(SHARD, 3 * D), (SHARD, D), (SHARD, FF), (FF // GROUPS, D), (D, D)]

A_GAIN, A_BIAS, Q_BIAS, V_BIAS, O_BIAS, F_GAIN, F_BIAS = range(7)
IN_BIAS, FO_BIAS, C_BIAS, D_GAIN, D_BIAS = 7, 11, 12, 13, 14


def segments():
    table = {}
    for row, at in zip((A_GAIN, A_BIAS, O_BIAS, F_GAIN, F_BIAS), (0, 1, 4, 5, 6)):
        table[row] = [(q, at) for q in range(GROUPS)]
    table[Q_BIAS] = [(0, 2), (0, 3), (1, 2), (1, 3)]
    table[V_BIAS] = [(2, 2), (2, 3), (3, 2), (3, 3)]
    for n in range(BLOCKS):
        table[IN_BIAS + n] = [(n, 7 + i) for i in range(4)]
    for row, at in zip((FO_BIAS, C_BIAS, D_GAIN, D_BIAS), (11, 12, 13, 14)):
        table[row] = [(q, at) for q in range(GROUPS)]
    return table


SEGMENTS = segments()


def at16(value):
    return pl.multiple_of(value, 16)


def at128(value):
    return pl.multiple_of(value, 128)


def spot(chunk, shard, first=0):
    mat, kind, j = CHUNKS[chunk]
    if kind == "col":
        return at16((BASES[mat] + j) * D + shard * SHARD + first)
    return at16((BASES[mat] + shard) * D + j * SHARD + first)


def shard_block(refs, chunk, first, rows, col=0, cols=D):
    mat, kind, j = CHUNKS[chunk]
    if kind == "col":
        return refs[mat].at[pl.ds(at16(first), rows), pl.ds(at128(j * D + col), cols)]
    return refs[mat].at[pl.ds(at16(j * SHARD + first), rows), pl.ds(at128(col), cols)]


def remote(src, dst, send, recv, target):
    return pltpu.make_async_remote_copy(
        src_ref=src,
        dst_ref=dst,
        send_sem=send,
        recv_sem=recv,
        device_id=target,
        device_id_type=MESH,
    )


def add_into(dst, row, rows, col, cols, src):
    @pl.loop(0, rows // 16)
    def _(i):
        here = pl.ds(at16(row + i * 16), 16)
        columns = pl.ds(at128(col), cols)
        dst[here, columns] = dst[here, columns] + src[pl.ds(at16(i * 16), 16), :]


def dot(left, right):
    return jnp.dot(left, right, preferred_element_type=F32)


def dot_rows(left, right):
    return lax.dot_general(left, right, (((0,), (0,)), ((), ())), preferred_element_type=F32)


def dot_turned(left, right):
    return lax.dot_general(left, right, (((1,), (1,)), ((), ())), preferred_element_type=F32)


def normalized(values):
    center = values - jnp.mean(values, axis=-1, keepdims=True)
    scale = lax.rsqrt(jnp.mean(center * center, axis=-1, keepdims=True) + norm_eps)
    return center * scale, scale


def norm_back(unit, scale, gain, grad):
    grad_unit = grad * gain
    mean_grad = jnp.mean(grad_unit, axis=-1, keepdims=True)
    mean_both = jnp.mean(grad_unit * unit, axis=-1, keepdims=True)
    return scale * (grad_unit - mean_grad - unit * mean_both)


def gelu_parts(values):
    half = 0.5 * lax.erf(values * (0.5**0.5)) + 0.5
    bell = jnp.exp(-0.5 * values * values) * 0.3989422804014327
    return values * half, half + values * bell


def column_sum(values):
    return jnp.sum(values, axis=0, keepdims=True)


def program_kernel(rows, extra, *refs):
    (chars, codes, cotangent, vec) = refs[:4]
    shards = refs[4:9]
    mols_out, chars_out, vec_out = refs[9:12]
    out = refs[12:17]
    more_in = refs[17] if extra else None
    refs = refs[:17] + refs[17 + (extra > 0) :]
    (
        held,
        core_in,
        y_in,
        x_in,
        e_in,
        m_in,
        vecs,
        vec_segs,
        rows_f32,
        vec_grads,
        vec_in,
        chars_v,
        cot_v,
        normed,
        projected,
        probs,
        context,
        hidden,
        normed_ffn,
        slope,
        active,
        layer,
        stacked,
        low_grad,
        total,
        mol_v,
    ) = refs[17:43]
    (
        w_send,
        w_recv,
        w_own,
        g_send,
        g_recv,
        g_own,
        more_send,
        more_recv,
        v_send,
        v_recv,
        io_sem,
        swap_send,
        swap_recv,
    ) = refs[43:]
    windows = rows // WIN
    mols = rows // KERNEL
    s, g, r = lax.axis_index("section"), lax.axis_index("group"), lax.axis_index("replica")
    near = {
        "c": (s, g ^ 1, r),
        "y": (s, g ^ 2, r),
        "x": (1 - s, g, r),
        "e": (s, g, r ^ 1),
        "m": (s, g, r ^ 3),
        "d": (s, g ^ 3, r),
        "w": (s, g, r ^ 2),
    }
    far = [(s, g, r ^ (RING << i)) for i in range(extra)]
    place = lax.rem(r, RING)
    even = lax.rem(r, 2) == 0
    middle = jnp.logical_or(place == 1, place == 2)
    border = jnp.logical_not(middle)

    loads = [
        pltpu.make_async_copy(chars.at[pl.ds(at16(s * rows), rows)], chars_v, io_sem.at[0]),
        pltpu.make_async_copy(cotangent.at[pl.ds(at16(s * mols), mols)], cot_v, io_sem.at[1]),
        pltpu.make_async_copy(vec, vecs.at[g], io_sem.at[2]),
    ]
    for copy in loads:
        copy.start()
    for k in range(COUNT):
        own_block = held.at[pl.ds(spot(k, g), SHARD)]
        pltpu.make_async_copy(shard_block(shards, k, 0, SHARD), own_block, w_own.at[k]).start()

    barrier = pltpu.get_barrier_semaphore()
    greeted = list(near.values()) + far
    for target in greeted:
        pl.semaphore_signal(barrier, inc=1, device_id=target, device_id_type=MESH)
    pl.semaphore_wait(barrier, len(greeted))

    y_third = jnp.where(even, s, 2)
    z_third = jnp.where(even, 2, s)
    x_third = 1 - s
    other = g ^ 2

    vec_copies = [
        remote(vec, vecs.at[g], v_send.at[i], v_recv.at[i], near[way])
        for i, way in enumerate("cyd")
    ]
    for copy in vec_copies:
        copy.start()

    def hop(i, k, third, way):
        here = held.at[pl.ds(spot(k, other, third * THIRD), THIRD)]
        return remote(here, here, w_send.at[i, k], w_recv.at[i, k], near[way])

    def first_hop(k):
        return remote(
            shard_block(shards, k, y_third * THIRD, THIRD),
            held.at[pl.ds(spot(k, g, y_third * THIRD), THIRD)],
            w_send.at[0, k],
            w_recv.at[0, k],
            near["y"],
        )

    def core_own(k):
        return remote(
            shard_block(shards, k, 0, SHARD),
            held.at[pl.ds(spot(k, g), SHARD)],
            w_send.at[3, k],
            w_recv.at[3, k],
            near["c"],
        )

    def core_hop(k, third):
        hop(4, k, third, "c").start()

    def core_wait(k):
        here = held.at[pl.ds(spot(k, other), SHARD)]
        return remote(here, here, w_send.at[4, k], w_recv.at[4, k], near["c"])

    for k in range(COUNT):
        first_hop(k).start()
    for k in range(COUNT):
        core_own(k).start()

    z_lag, x_lag = 2, 4

    def gather_step(k):
        if k < COUNT:
            hop(0, k, y_third, "y").wait_recv()
            hop(2, k, y_third, "e").start()

            @pl.when(even)
            def _():
                hop(1, k, s, "x").start()

            core_hop(k, y_third)
        j = k - z_lag
        if 0 <= j < COUNT:
            hop(2, j, z_third, "e").wait_recv()

            @pl.when(jnp.logical_not(even))
            def _():
                hop(1, j, s, "x").start()

            core_hop(j, z_third)
        j = k - x_lag
        if 0 <= j < COUNT:
            hop(1, j, x_third, "x").wait_recv()
            core_hop(j, x_third)

    def weight_ready(k):
        own_block = held.at[pl.ds(spot(k, g), SHARD)]
        pltpu.make_async_copy(shard_block(shards, k, 0, SHARD), own_block, w_own.at[k]).wait()
        theirs = held.at[pl.ds(spot(k, g ^ 1), SHARD)]
        remote(theirs, theirs, w_send.at[3, k], w_recv.at[3, k], near["c"]).wait_recv()
        theirs = held.at[pl.ds(spot(k, g ^ 3), SHARD)]
        remote(theirs, theirs, w_send.at[4, k], w_recv.at[4, k], near["c"]).wait_recv()

    def gather_done():
        for k in range(COUNT):
            first_hop(k).wait_send()
            hop(2, k, y_third, "e").wait_send()
            hop(1, k, s, "x").wait_send()
            core_own(k).wait_send()
            core_wait(k).wait_send()

    def spread_matrix(seg):
        i = lax.broadcasted_iota(jnp.int32, (VEC[1], D), 0)
        j = lax.broadcasted_iota(jnp.int32, (VEC[1], D), 1)
        hit = jnp.logical_and(j == i + seg * SHARD, i < SHARD)
        return jnp.where(hit, 1.0, 0.0).astype(LOW)

    def vectors_ready():
        loads[2].wait()
        for copy in vec_copies:
            copy.wait()
        vec_segs[...] = jnp.zeros_like(vec_segs)
        for row, parts in SEGMENTS.items():
            for seg, (q, at) in enumerate(parts):
                vec_segs[seg, row : row + 1, :] = vecs[q, at : at + 1, :]
        full = jnp.zeros((VEC[0], D), F32)
        for seg in range(GROUPS):
            full = full + dot(vec_segs[seg].astype(LOW), spread_matrix(seg))
        rows_f32[...] = full

    def vector(row):
        return rows_f32[row : row + 1, :]

    def vector_tile(row, j):
        return rows_f32[row : row + 1, pl.ds(at128(j * TILE), TILE)]

    def block(n, j=None):
        start = n * D
        if not isinstance(n, int):
            start = at16(start)
        if j is None:
            return held[pl.ds(start, D), :]
        return held[pl.ds(start, D), pl.ds(at128(j * TILE), TILE)]

    def row_tiles(body):
        @pl.loop(0, rows // WIN)
        def _(i):
            body(pl.ds(at128(i * WIN), WIN), i)

    def col_tiles(body):
        @pl.loop(0, D // TILE)
        def _(j):
            body(pl.ds(at128(j * TILE), TILE), j)

    def norm_first():
        loads[0].wait()

        def one(here, i):
            unit, _ = normalized(chars_v[here, :].astype(F32))
            normed[here, :] = (unit * vector(A_GAIN) + vector(A_BIAS)).astype(LOW)

        row_tiles(one)

    def project_block(n):
        def one(here, j):
            value = dot(normed[...], block(QKV + n, j))
            if n == 0:
                value = value + vector_tile(Q_BIAS, j)
            if n == 2:
                value = value + vector_tile(V_BIAS, j)
            projected[n, :, here] = value.astype(LOW)

        col_tiles(one)

    def key_bias(w):
        code = codes[pl.ds(s * windows + w, 1), :]
        return jnp.where(code != 0, 0.0, mask_value).astype(F32)

    def lanes():
        return lax.broadcasted_iota(jnp.int32, (WIN, PAIR), 1) < HEAD_DIM

    def two_heads(values):
        first = lanes()
        zero = jnp.zeros_like(values)
        return jnp.concatenate(
            [jnp.where(first, values, zero), jnp.where(first, zero, values)], axis=0
        )

    def one_pair(values):
        return jnp.where(lanes(), values[:WIN], values[WIN:])

    scale_factor = HEAD_DIM ** (-0.5)

    def attend():
        def one(here, w):
            bias = key_bias(w)
            for p in range(PAIRS):
                cols = pl.ds(p * PAIR, PAIR)
                queries = two_heads(projected[0, here, cols])
                scores = dot_turned(queries, projected[1, here, cols]) * scale_factor + bias
                top = jnp.max(scores, axis=-1, keepdims=True)
                weight = jnp.exp(scores - top)
                weight = weight / jnp.sum(weight, axis=-1, keepdims=True)
                prob = weight.astype(LOW)
                probs[w, p] = prob
                context[here, cols] = one_pair(dot(prob, projected[2, here, cols])).astype(LOW)

        row_tiles(one)

    def attend_out():
        def one(here, j):
            value = dot(context[...], block(OUT, j)) + vector_tile(O_BIAS, j)
            hidden[:, here] = chars_v[:, here].astype(F32) + value

        col_tiles(one)

        def norm(here, i):
            unit, _ = normalized(hidden[here, :])
            normed_ffn[here, :] = (unit * vector(F_GAIN) + vector(F_BIAS)).astype(LOW)

        row_tiles(norm)

    def inner_block(n):
        def one(here, j):
            value = dot(normed_ffn[...], block(FIN + n, j)) + vector_tile(IN_BIAS + n, j)
            gelu, grad = gelu_parts(value)
            active[n, :, here] = gelu.astype(LOW)
            slope[n, :, here] = grad.astype(LOW)

        col_tiles(one)

    def by_place():
        i = lax.broadcasted_iota(jnp.int32, (WIN, WIN), 0)
        j = lax.broadcasted_iota(jnp.int32, (WIN, WIN), 1)
        return jnp.where(j == KERNEL * lax.rem(i, RUN) + i // RUN, 1.0, 0.0).astype(LOW)

    def layer_end():
        def one(here, j):
            value = hidden[:, here] + vector_tile(FO_BIAS, j)
            for n in range(BLOCKS):
                value = value + dot(active[n], block(FOUT + n, j))
            low_grad[:, here] = value.astype(LOW)

        col_tiles(one)
        order = by_place()

        def sort(here, w):
            moved = dot(order, low_grad[here, :]).astype(LOW)
            for k in range(KERNEL):
                stacked[k, pl.ds(at16(w * RUN), RUN), :] = moved[k * RUN : (k + 1) * RUN]

        row_tiles(sort)

    def note(row, value):
        vec_grads[row : row + 1, :] = value

    def note_more(row, value):
        vec_grads[row : row + 1, :] = vec_grads[row : row + 1, :] + value

    def convolve():
        loads[1].wait()
        value = jnp.zeros((mols, D), F32) + vector(C_BIAS)
        for k in range(KERNEL):
            value = value + dot(stacked[k], block(CONV + k))
        gelu, grad = gelu_parts(value)
        unit, scale = normalized(gelu)
        mol_v[...] = (unit * vector(D_GAIN) + vector(D_BIAS)).astype(LOW)
        wide = cot_v[...].astype(F32)
        note(D_GAIN, column_sum(wide * unit))
        note(D_BIAS, column_sum(wide))
        grad_conv = (norm_back(unit, scale, vector(D_GAIN), wide) * grad).astype(LOW)
        cot_v[...] = grad_conv
        note(C_BIAS, column_sum(grad_conv.astype(F32)))

    def convolve_back():
        for k in range(KERNEL):
            total[k * mols : (k + 1) * mols, :] = dot_turned(cot_v[...], block(CONV + k))

        for k in range(KERNEL):

            def one(here, j):
                value = dot_rows(stacked[k, :, here], cot_v[...])
                held[pl.ds(at128((CONV + k) * D + j * TILE), TILE), :] = value.astype(LOW)

            col_tiles(one)

        order = by_place()

        def sort(here, w):
            parts = [total[pl.ds(at16(k * mols + w * RUN), RUN), :] for k in range(KERNEL)]
            value = dot_rows(order, jnp.concatenate(parts, axis=0).astype(LOW))
            layer[here, :] = value
            low_grad[here, :] = value.astype(LOW)
            note_more(FO_BIAS, column_sum(value))

        row_tiles(sort)

    def weight_grad(n, left, right):
        def one(here, j):
            value = dot_rows(left[:, here], right[...])
            held[pl.ds(at128(n * D + j * TILE), TILE), :] = value.astype(LOW)

        col_tiles(one)

    def active_back(n):
        def one(here, j):
            value = dot_turned(
                low_grad[...], held[pl.ds(at128((FOUT + n) * D + j * TILE), TILE), :]
            )
            inner = (value * slope[n, :, here].astype(F32)).astype(LOW)
            slope[n, :, here] = inner
            vec_grads[IN_BIAS + n : IN_BIAS + n + 1, here] = column_sum(inner.astype(F32))

        col_tiles(one)
        weight_grad(FOUT + n, active.at[n], low_grad)

    def inner_sum():
        def one(here, j):
            value = jnp.zeros((rows, TILE), F32)
            for n in range(BLOCKS):
                value = value + dot_turned(
                    slope[n], held[pl.ds(at128((FIN + n) * D + j * TILE), TILE), :]
                )
            total[:, here] = value

        col_tiles(one)

    def hidden_back():
        def one(here, i):
            unit, scale = normalized(hidden[here, :])
            grad = total[here, :]
            note_more(F_GAIN, column_sum(grad * unit))
            note_more(F_BIAS, column_sum(grad))
            value = layer[here, :] + norm_back(unit, scale, vector(F_GAIN), grad)
            layer[here, :] = value
            low = value.astype(LOW)
            low_grad[here, :] = low
            note_more(O_BIAS, column_sum(low.astype(F32)))

        row_tiles(one)

    def context_back():
        def one(here, j):
            value = dot_turned(low_grad[...], held[pl.ds(at128(OUT * D + j * TILE), TILE), :])
            normed_ffn[:, here] = value.astype(LOW)

        col_tiles(one)
        weight_grad(OUT, context, low_grad)

    def attend_back():
        def one(here, w):
            for p in range(PAIRS):
                cols = pl.ds(p * PAIR, PAIR)
                grad_out = two_heads(normed_ffn[here, cols])
                prob = probs[w, p]
                wide = prob.astype(F32)
                grad_prob = dot_turned(grad_out, projected[2, here, cols])
                inner = jnp.sum(wide * grad_prob, axis=-1, keepdims=True)
                grad_score = (wide * (grad_prob - inner)).astype(LOW)
                grad_value = dot_rows(prob, grad_out)
                grad_query = one_pair(dot(grad_score, projected[1, here, cols])) * scale_factor
                grad_key = (
                    dot_rows(grad_score, two_heads(projected[0, here, cols])) * scale_factor
                )
                low_query, low_value = grad_query.astype(LOW), grad_value.astype(LOW)
                slope[0, here, cols] = low_query
                slope[1, here, cols] = grad_key.astype(LOW)
                slope[2, here, cols] = low_value
                for row, low in ((Q_BIAS, low_query), (V_BIAS, low_value)):
                    vec_grads[row : row + 1, cols] = vec_grads[row : row + 1, cols] + column_sum(
                        low.astype(F32)
                    )

        row_tiles(one)

    def project_sum():
        def one(here, j):
            value = jnp.zeros((rows, TILE), F32)
            for n in range(3):
                value = value + dot_turned(
                    slope[n], held[pl.ds(at128((QKV + n) * D + j * TILE), TILE), :]
                )
            total[:, here] = value

        col_tiles(one)

    def chars_back():
        def one(here, i):
            unit, scale = normalized(chars_v[here, :].astype(F32))
            grad = total[here, :]
            note_more(A_GAIN, column_sum(grad * unit))
            note_more(A_BIAS, column_sum(grad))
            value = layer[here, :] + norm_back(unit, scale, vector(A_GAIN), grad)
            context[here, :] = value.astype(LOW)

        row_tiles(one)

    def swap(i, whole, dst, count):
        keep = whole.at[:, pl.ds(at128(s * HALF), HALF)]
        give = whole.at[:, pl.ds(at128((1 - s) * HALF), HALF)]
        there = dst.at[pl.ds(at16(s * count), count)]
        stay = pltpu.make_async_copy(keep, there, io_sem.at[3 + i])
        go = remote(give, there, swap_send.at[i], swap_recv.at[i], near["x"])
        stay.start()
        go.start()
        return [stay, go]

    c = lax.rem(g, 2)
    y = g // 2
    mine, yours = 2 * y + c, 2 * (1 - y) + c

    def core_sum(k, i):
        return remote(
            held.at[pl.ds(spot(k, 2 * i + 1 - c), SHARD)],
            core_in.at[k, i],
            g_send.at[i, k],
            g_recv.at[i, k],
            near["c"],
        )

    def y_sum(k):
        return remote(
            held.at[pl.ds(spot(k, yours), SHARD)],
            y_in.at[k],
            g_send.at[2, k],
            g_recv.at[2, k],
            near["y"],
        )

    def part(k, side):
        return held.at[pl.ds(spot(k, mine), SHARD), pl.ds(at128(side * HALF), HALF)]

    def x_sum(k):
        return remote(part(k, 1 - s), x_in.at[k], g_send.at[3, k], g_recv.at[3, k], near["x"])

    def e_sum(k):
        return remote(part(k, s), e_in.at[k], g_send.at[4, k], g_recv.at[4, k], near["e"])

    def m_sum(k):
        return remote(part(k, s), m_in.at[k], g_send.at[5, k], g_recv.at[5, k], near["m"])

    def final(k):
        return shard_block(out, k, 0, SHARD, s * HALF, HALF)

    def e_back(k):
        return remote(part(k, s), final(k), g_send.at[6, k], g_recv.at[6, k], near["e"])

    def x_back(k, src):
        return remote(src, final(k), g_send.at[7, k], g_recv.at[7, k], near["x"])

    def own_back(k):
        return pltpu.make_async_copy(part(k, s), final(k), g_own.at[k])

    def sum_step(n, k):
        if n == 0:
            for i in range(2):
                core_sum(k, i).start()
        if n == 1:
            for i in range(2):
                core_sum(k, i).wait_recv()
                add_into(held, spot(k, 2 * i + c), SHARD, 0, D, core_in.at[k, i])
            y_sum(k).start()
        if n == 2:
            y_sum(k).wait_recv()
            add_into(held, spot(k, mine), SHARD, 0, D, y_in.at[k])
            x_sum(k).start()
        if n == 3:
            x_sum(k).wait_recv()
            add_into(held, spot(k, mine), SHARD, s * HALF, HALF, x_in.at[k])

            @pl.when(border)
            def _():
                e_sum(k).start()

        if n == 4:

            @pl.when(middle)
            def _():
                e_sum(k).wait_recv()
                add_into(held, spot(k, mine), SHARD, s * HALF, HALF, e_in.at[k])
                m_sum(k).start()

        if n == 5:

            @pl.when(middle)
            def _():
                m_sum(k).wait_recv()
                m_sum(k).wait_send()
                add_into(held, spot(k, mine), SHARD, s * HALF, HALF, m_in.at[k])
                for i in range(extra):
                    copy = remote(
                        part(k, s),
                        more_in.at[k, i],
                        more_send.at[k, i],
                        more_recv.at[k, i],
                        far[i],
                    )
                    copy.start()
                    copy.wait()
                    copy = pltpu.make_async_copy(more_in.at[k, i], e_in.at[k], g_own.at[k])
                    copy.start()
                    copy.wait()
                    add_into(held, spot(k, mine), SHARD, s * HALF, HALF, e_in.at[k])
                own_back(k).start()
                e_back(k).start()
                x_back(k, part(k, s)).start()

        if n == 6:

            @pl.when(border)
            def _():
                e_back(k).wait_recv()
                x_back(k, final(k)).start()

    def sums_done():
        for k in range(COUNT):
            for i in range(2):
                core_sum(k, i).wait_send()
            y_sum(k).wait_send()
            x_sum(k).wait_send()

            @pl.when(border)
            def _():
                e_sum(k).wait_send()

            @pl.when(middle)
            def _():
                own_back(k).wait()
                e_back(k).wait_send()

            x_back(k, part(k, s)).wait()

    vec_steps = 6 + extra
    vec_moves = []

    def vec_step(n):
        if n == 0:
            top = vec_grads[...]
            high = top.astype(LOW)
            low = (top - high.astype(F32)).astype(LOW)
            for seg in range(GROUPS):
                spread = spread_matrix(seg)
                vec_segs[seg] = dot_turned(high, spread) + dot_turned(low, spread)
            for row, parts in SEGMENTS.items():
                for seg, (q, at) in enumerate(parts):
                    vecs[q, at : at + 1, :] = vec_segs[seg, row : row + 1, :]
            for i in range(2):
                copy = remote(
                    vecs.at[2 * i + 1 - c], vec_in.at[i], v_send.at[3 + i], v_recv.at[3 + i], near["c"]
                )
                copy.start()
                vec_moves.append(copy)
            return
        if n == 1:
            for i in range(2):
                vec_moves[i].wait()
                vecs[2 * i + c] = vecs[2 * i + c] + vec_in[i]
        else:
            vec_moves[-1].wait()
            vecs[mine] = vecs[mine] + vec_in[n]
        steps = [near["y"], near["x"], near["e"], near["w"]] + far
        if n <= len(steps):
            copy = remote(
                vecs.at[yours if n == 1 else mine],
                vec_in.at[1 + n],
                v_send.at[4 + n],
                v_recv.at[4 + n],
                steps[n - 1],
            )
            copy.start()
            vec_moves.append(copy)
        else:
            copy = pltpu.make_async_copy(vecs.at[mine], vec_out, io_sem.at[2])
            copy.start()
            copy.wait()

    vec_grads[...] = jnp.zeros_like(vec_grads)
    gather_step(0)
    vectors_ready()
    gather_step(1)
    norm_first()
    forward = [
        ([0], lambda: project_block(0)),
        ([1], lambda: project_block(1)),
        ([2], lambda: project_block(2)),
        ([], attend),
        ([3], attend_out),
    ]
    forward += [([FIN + n], functools.partial(inner_block, n)) for n in range(BLOCKS)]
    forward += [([8, 9, 10, 11], layer_end), ([12, 13, 14, 15], convolve)]
    for step in range(2, COUNT + x_lag):
        gather_step(step)
        while forward and all(k <= step - x_lag - 1 for k in forward[0][0]):
            need, work = forward.pop(0)
            for k in need:
                weight_ready(k)
            work()
    for need, work in forward:
        for k in need:
            weight_ready(k)
        work()
    gather_done()

    order = [12, 13, 14, 15, 8, 9, 10, 11, 4, 5, 6, 7, 3, 0, 1, 2]
    lags = [0, 1, 2, 3, 4, 5, 6]
    progress = {"at": 0}

    def advance(ready):
        while progress["at"] < ready:
            i = progress["at"]
            for n in reversed(range(len(lags))):
                j = i - lags[n]
                if 0 <= j < COUNT:
                    sum_step(n, order[j])
            progress["at"] = i + 1

    convolve_back()
    moves = swap(0, mol_v, mols_out, mols)
    advance(1)
    active_back(0)
    advance(2)
    active_back(1)
    advance(3)
    active_back(2)
    advance(4)
    active_back(3)
    advance(5)
    inner_sum()
    advance(6)
    for n in range(BLOCKS):
        weight_grad(FIN + n, normed_ffn, slope.at[n])
    advance(7)
    hidden_back()
    context_back()
    advance(8)
    attend_back()
    advance(9)
    project_sum()
    for n in range(3):
        weight_grad(QKV + n, normed, slope.at[n])
    advance(10)
    chars_back()
    moves += swap(1, context, chars_out, rows)
    for i in range(vec_steps):
        advance(11 + i)
        vec_step(i)
    advance(COUNT + lags[-1])
    sums_done()
    for copy in moves:
        copy.wait()


def run(args, chars, extra):
    rows = chars.shape[0] // 2
    mols = rows // KERNEL
    anywhere = pl.BlockSpec(memory_space=pl.ANY)
    dma = pltpu.SemaphoreType.DMA
    vmem = pltpu.VMEM
    windows = rows // WIN
    return pl.pallas_call(
        functools.partial(program_kernel, rows, extra),
        name="layer_and_sums",
        out_shape=[
            jax.ShapeDtypeStruct((2 * mols, HALF), LOW),
            jax.ShapeDtypeStruct((2 * rows, HALF), LOW),
            jax.ShapeDtypeStruct(VEC, F32),
        ]
        + [jax.ShapeDtypeStruct(shape, LOW) for shape in SHARD_SHAPES]
        + [jax.ShapeDtypeStruct((COUNT, extra, SHARD, HALF), LOW)] * (extra > 0),
        in_specs=[anywhere, pl.BlockSpec(memory_space=vmem)] + [anywhere] * 7,
        out_specs=[anywhere] * (8 + (extra > 0)),
        scratch_shapes=[
            vmem((COUNT * D, D), LOW),
            vmem((COUNT, 2, SHARD, D), LOW),
            vmem((COUNT, SHARD, D), LOW),
            vmem((COUNT, SHARD, HALF), LOW),
            vmem((COUNT, SHARD, HALF), LOW),
            vmem((COUNT, SHARD, HALF), LOW),
            vmem((GROUPS,) + VEC, F32),
            vmem((GROUPS,) + VEC, F32),
            vmem((VEC[0], D), F32),
            vmem((VEC[0], D), F32),
            vmem((7 + extra,) + VEC, F32),
            vmem((rows, D), LOW),
            vmem((mols, D), LOW),
            vmem((rows, D), LOW),
            vmem((3, rows, D), LOW),
            vmem((windows, PAIRS, 2 * WIN, WIN), LOW),
            vmem((rows, D), LOW),
            vmem((rows, D), F32),
            vmem((rows, D), LOW),
            vmem((BLOCKS, rows, D), LOW),
            vmem((BLOCKS, rows, D), LOW),
            vmem((rows, D), F32),
            vmem((KERNEL, mols, D), LOW),
            vmem((rows, D), LOW),
            vmem((rows, D), F32),
            vmem((mols, D), LOW),
            dma((5, COUNT)),
            dma((5, COUNT)),
            dma((COUNT,)),
            dma((8, COUNT)),
            dma((8, COUNT)),
            dma((COUNT,)),
            dma((COUNT, max(extra, 1))),
            dma((COUNT, max(extra, 1))),
            dma((9 + extra,)),
            dma((9 + extra,)),
            dma((5,)),
            dma((2,)),
            dma((2,)),
        ],
        compiler_params=pltpu.CompilerParams(
            collective_id=0, has_side_effects=True, vmem_limit_bytes=63 << 20
        ),
    )(*args)


VEC_COUNTS = [1, 1, 2, 1, 1, 1, 4, 1, 1, 1, 1]


def body(
    chars,
    char_codes,
    mol_cotangent,
    attn_norm_gain,
    attn_norm_bias,
    qkv_weight,
    qv_bias,
    out_weight,
    out_bias,
    ffn_norm_gain,
    ffn_norm_bias,
    ffn_in_weight,
    ffn_in_bias,
    ffn_out_weight,
    ffn_out_bias,
    conv_weight,
    conv_bias,
    down_norm_gain,
    down_norm_bias,
):
    vectors = [
        attn_norm_gain,
        attn_norm_bias,
        qv_bias,
        out_bias,
        ffn_norm_gain,
        ffn_norm_bias,
        ffn_in_bias,
        ffn_out_bias,
        conv_bias,
        down_norm_gain,
        down_norm_bias,
    ]
    packed = jnp.concatenate([v.reshape(-1, SHARD) for v in vectors], axis=0).astype(F32)
    packed = jnp.pad(packed, ((0, VEC[0] - packed.shape[0]), (0, VEC[1] - SHARD)))
    result = run(
        (
            chars,
            char_codes.reshape(-1, WIN),
            mol_cotangent,
            packed,
            qkv_weight,
            out_weight,
            ffn_in_weight,
            ffn_out_weight,
            conv_weight,
        ),
        chars,
        (lax.axis_size("replica") // RING).bit_length() - 1,
    )
    molecules, chars_grad, vec_sum = result[:3]
    t_qkv, t_out, t_in, t_ffo, t_conv = [w.astype(F32) for w in result[3:8]]
    v = []
    row = 0
    for count in VEC_COUNTS:
        v.append(vec_sum[row : row + count, :SHARD].reshape(-1))
        row += count
    return (
        molecules,
        chars_grad,
        v[0],
        v[1],
        t_qkv,
        v[2],
        t_out,
        v[3],
        v[4],
        v[5],
        t_in,
        v[6],
        t_ffo,
        v[7],
        t_conv,
        v[8],
        v[9],
        v[10],
    )


def solution(mesh):
    return jax.shard_map(
        body,
        mesh=mesh,
        in_specs=(
            P(("group", "replica"), None),
            P(("group", "replica")),
            P(("group", "replica"), None),
            P("group"),
            P("group"),
            P("group", None),
            P("group"),
            P("group", None),
            P("group"),
            P("group"),
            P("group"),
            P("group", None),
            P("group"),
            P("group", None),
            P("group"),
            P("group", None),
            P("group"),
            P("group"),
            P("group"),
        ),
        out_specs=(
            P(("group", "replica"), "section"),
            P(("group", "replica"), "section"),
            P("group"),
            P("group"),
            P("group", None),
            P("group"),
            P("group", None),
            P("group"),
            P("group"),
            P("group"),
            P("group", None),
            P("group"),
            P("group", None),
            P("group"),
            P("group", None),
            P("group"),
            P("group"),
            P("group"),
        ),
        check_vma=False,
    )
```

```python
import functools

import jax
import jax.numpy as jnp
from jax import lax
from jax.experimental import pallas as pl
from jax.experimental.pallas import tpu as pltpu
from jax.sharding import PartitionSpec as P

D = 768
HEADS = 12
HEAD_DIM = 64
FF = 3072
WIN = 128
KERNEL = 4
GROUPS = 4
RING = 4
SHARD = D // GROUPS
THIRD = SHARD // 3
EIGHTH = SHARD // 4
HALF = D // 2
TILE = 768
PAIR = 2 * HEAD_DIM
PAIRS = HEADS // 2
RUN = WIN // KERNEL
BLOCKS = FF // D
VEC = (16, 256)
norm_eps = 1e-06
mask_value = -10000.0
MESH = pl.DeviceIdType.MESH
F32 = jnp.float32
LOW = jnp.bfloat16

CHUNKS = (
    [(0, "col", j) for j in range(3)]
    + [(1, "col", 0)]
    + [(2, "col", j) for j in range(4)]
    + [(3, "row", j) for j in range(4)]
    + [(4, "row", j) for j in range(4)]
)
COUNT = len(CHUNKS)
QKV, OUT, FIN, FOUT, CONV = BASES = (0, 3, 4, 8, 12)
SHARD_SHAPES = [(SHARD, 3 * D), (SHARD, D), (SHARD, FF), (FF // GROUPS, D), (D, D)]

A_GAIN, A_BIAS, Q_BIAS, V_BIAS, O_BIAS, F_GAIN, F_BIAS = range(7)
IN_BIAS, FO_BIAS, C_BIAS, D_GAIN, D_BIAS = 7, 11, 12, 13, 14


def segments():
    table = {}
    for row, at in zip((A_GAIN, A_BIAS, O_BIAS, F_GAIN, F_BIAS), (0, 1, 4, 5, 6)):
        table[row] = [(q, at) for q in range(GROUPS)]
    table[Q_BIAS] = [(0, 2), (0, 3), (1, 2), (1, 3)]
    table[V_BIAS] = [(2, 2), (2, 3), (3, 2), (3, 3)]
    for n in range(BLOCKS):
        table[IN_BIAS + n] = [(n, 7 + i) for i in range(4)]
    for row, at in zip((FO_BIAS, C_BIAS, D_GAIN, D_BIAS), (11, 12, 13, 14)):
        table[row] = [(q, at) for q in range(GROUPS)]
    return table


SEGMENTS = segments()

UNITS = [
    (12, 0, 192, "deep"),
    (13, 0, 192, "wide"),
    (14, 0, 192, "deep_x"),
    (15, 0, 192, "wide"),
    (8, 0, 192, "wide"),
    (9, 0, 192, "wide"),
    (10, 0, 192, "wide"),
    (11, 0, 192, "wide"),
    (4, 0, 192, "wide"),
    (5, 0, 192, "wide"),
    (6, 0, 192, "deep"),
    (7, 0, 96, "line"),
    (7, 96, 96, "line"),
    (3, 0, 64, "wide"),
    (3, 64, 64, "wide"),
    (3, 128, 64, "wide"),
    (0, 0, 96, "wide"),
    (0, 96, 96, "wide"),
    (1, 0, 64, "line"),
    (1, 64, 64, "line"),
    (1, 128, 64, "line"),
    (2, 0, 48, "wide"),
    (2, 48, 48, "wide"),
    (2, 96, 48, "wide"),
    (2, 144, 48, "wide"),
]

SEM_COUNT = {"wide": 8, "line": 12, "deep": 14, "deep_x": 14}
SEM_AT = [sum(SEM_COUNT[unit[3]] for unit in UNITS[:u]) for u in range(len(UNITS))]
SEMS = sum(SEM_COUNT[unit[3]] for unit in UNITS)
LINES = sorted({unit[0] for unit in UNITS if unit[3] == "line"})
PLAN = [
    -1, 10, 30, 20, 0, -1, 11, 31, 21, -1, 1, -1, -1, 60, 40, 50, 70, 12, 22, -1, 61, 41,
    51, 71, -1, 80, 13, 32, -1, 90, 2, 81, -1, 100, 91, -1, 110, 120, 33, 101, 62, -1, 111,
    121, 14, 23, -1, 130, 140, 150, 63, 42, 24, -1, 131, 141, 151, 3, 34, -1, 43, 15, -1, 4,
    102, 52, -1, 35, -1, 64, 16, -1, 160, 170, 53, 44, 72, -1, 161, 171, 180, 190, 200, -1,
    210, 220, 230, 240, 181, 82, 191, 211, 221, 231, 241, 201, 73, 54, 103, -1, -1, 65, 36,
    83, 92, 104, 74, 45, -1, 66, 112, 84, 55, -1, 46, 122, 93, 25, 75, 113, -1, 132, 56, 85,
    142, 123, 114, -1, 76, 152, 26, 5, 94, 124, 86, -1, 162, 133, 27, 6, 172, 134, 143, 182,
    95, 115, 135, 192, 153, 7, 212, 125, 144, 116, 222, 163, 96, 183, 232, 173, 126, 193,
    242, 145, 136, 154, 184, 202, 164, 194, 105, 155, 174, 165, 146, 203, 213, 223, 106,
    233, 156, 243, 214, 175, 224, 166, 204, 185, 215, 107, 195, 234, 225, 244, 176, 186,
    196, 216, 235, 245, 226, 205, 236, 206, 246,
]


def at16(value):
    return pl.multiple_of(value, 16)


def at128(value):
    return pl.multiple_of(value, 128)


def spot(chunk, shard, first=0):
    mat, kind, j = CHUNKS[chunk]
    if kind == "col":
        return at16((BASES[mat] + j) * D + shard * SHARD + first)
    return at16((BASES[mat] + shard) * D + j * SHARD + first)


def shard_block(refs, chunk, first, rows, col=0, cols=D):
    mat, kind, j = CHUNKS[chunk]
    if kind == "col":
        return refs[mat].at[pl.ds(at16(first), rows), pl.ds(at128(j * D + col), cols)]
    return refs[mat].at[pl.ds(at16(j * SHARD + first), rows), pl.ds(at128(col), cols)]


def remote(src, dst, send, recv, target):
    return pltpu.make_async_remote_copy(
        src_ref=src,
        dst_ref=dst,
        send_sem=send,
        recv_sem=recv,
        device_id=target,
        device_id_type=MESH,
    )


def add_into(dst, row, rows, col, cols, src):
    @pl.loop(0, rows // 16)
    def _(i):
        here = pl.ds(at16(row + i * 16), 16)
        columns = pl.ds(at128(col), cols)
        dst[here, columns] = dst[here, columns] + src[pl.ds(at16(i * 16), 16), :]


def dot(left, right):
    return jnp.dot(left, right, preferred_element_type=F32)


def dot_rows(left, right):
    return lax.dot_general(left, right, (((0,), (0,)), ((), ())), preferred_element_type=F32)


def dot_turned(left, right):
    return lax.dot_general(left, right, (((1,), (1,)), ((), ())), preferred_element_type=F32)


def normalized(values):
    center = values - jnp.mean(values, axis=-1, keepdims=True)
    scale = lax.rsqrt(jnp.mean(center * center, axis=-1, keepdims=True) + norm_eps)
    return center * scale, scale


def norm_back(unit, scale, gain, grad):
    grad_unit = grad * gain
    mean_grad = jnp.mean(grad_unit, axis=-1, keepdims=True)
    mean_both = jnp.mean(grad_unit * unit, axis=-1, keepdims=True)
    return scale * (grad_unit - mean_grad - unit * mean_both)


def gelu_parts(values):
    half = 0.5 * lax.erf(values * (0.5**0.5)) + 0.5
    bell = jnp.exp(-0.5 * values * values) * 0.3989422804014327
    return values * half, half + values * bell


def column_sum(values):
    return jnp.sum(values, axis=0, keepdims=True)


def program_kernel(rows, extra, *refs):
    (chars, codes, cotangent, vec) = refs[:4]
    shards = refs[4:9]
    mols_out, chars_out, vec_out = refs[9:12]
    out = refs[12:17]
    more_in = refs[17] if extra else None
    refs = refs[:17] + refs[17 + (extra > 0) :]
    (
        held,
        core_in,
        y_in,
        x_in,
        e_in,
        m_in,
        line_in,
        vecs,
        vec_segs,
        rows_f32,
        vec_grads,
        vec_in,
        chars_v,
        cot_v,
        normed,
        projected,
        probs,
        context,
        hidden,
        normed_ffn,
        slope,
        active,
        layer,
        stacked,
        low_grad,
        total,
        mol_v,
    ) = refs[17:44]
    (
        w_send,
        w_recv,
        w_own,
        g_send,
        g_recv,
        g_own,
        more_send,
        more_recv,
        v_send,
        v_recv,
        io_sem,
        swap_send,
        swap_recv,
    ) = refs[44:]
    windows = rows // WIN
    mols = rows // KERNEL
    s, g, r = lax.axis_index("section"), lax.axis_index("group"), lax.axis_index("replica")
    near = {
        "c": (s, g ^ 1, r),
        "y": (s, g ^ 2, r),
        "x": (1 - s, g, r),
        "e": (s, g, r ^ 1),
        "m": (s, g, r ^ 3),
        "d": (s, g ^ 3, r),
        "w": (s, g, r ^ 2),
    }
    far = [(s, g, r ^ (RING << i)) for i in range(extra)]
    place = lax.rem(r, RING)
    even = lax.rem(r, 2) == 0
    middle = jnp.logical_or(place == 1, place == 2)
    border = jnp.logical_not(middle)

    loads = [
        pltpu.make_async_copy(chars.at[pl.ds(at16(s * rows), rows)], chars_v, io_sem.at[0]),
        pltpu.make_async_copy(cotangent.at[pl.ds(at16(s * mols), mols)], cot_v, io_sem.at[1]),
        pltpu.make_async_copy(vec, vecs.at[g], io_sem.at[2]),
    ]
    for copy in loads:
        copy.start()
    for k in range(COUNT):
        own_block = held.at[pl.ds(spot(k, g), SHARD)]
        pltpu.make_async_copy(shard_block(shards, k, 0, SHARD), own_block, w_own.at[k]).start()

    barrier = pltpu.get_barrier_semaphore()
    greeted = list(near.values()) + far
    for target in greeted:
        pl.semaphore_signal(barrier, inc=1, device_id=target, device_id_type=MESH)
    pl.semaphore_wait(barrier, len(greeted))

    y_third = jnp.where(even, s, 2)
    z_third = jnp.where(even, 2, s)
    x_third = 1 - s
    other = g ^ 2

    vec_copies = [
        remote(vec, vecs.at[g], v_send.at[i], v_recv.at[i], near[way])
        for i, way in enumerate("cyd")
    ]
    for copy in vec_copies:
        copy.start()

    def hop(i, k, third, way):
        here = held.at[pl.ds(spot(k, other, third * THIRD), THIRD)]
        return remote(here, here, w_send.at[i, k], w_recv.at[i, k], near[way])

    def first_hop(k):
        return remote(
            shard_block(shards, k, y_third * THIRD, THIRD),
            held.at[pl.ds(spot(k, g, y_third * THIRD), THIRD)],
            w_send.at[0, k],
            w_recv.at[0, k],
            near["y"],
        )

    def core_own(k):
        return remote(
            shard_block(shards, k, 0, SHARD),
            held.at[pl.ds(spot(k, g), SHARD)],
            w_send.at[3, k],
            w_recv.at[3, k],
            near["c"],
        )

    def core_hop(k, third):
        hop(4, k, third, "c").start()

    def core_wait(k):
        here = held.at[pl.ds(spot(k, other), SHARD)]
        return remote(here, here, w_send.at[4, k], w_recv.at[4, k], near["c"])

    for k in range(COUNT):
        first_hop(k).start()
    for k in range(COUNT):
        core_own(k).start()

    z_lag, x_lag = 2, 4

    def gather_step(k):
        if k < COUNT:
            hop(0, k, y_third, "y").wait_recv()
            hop(2, k, y_third, "e").start()

            @pl.when(even)
            def _():
                hop(1, k, s, "x").start()

            core_hop(k, y_third)
        j = k - z_lag
        if 0 <= j < COUNT:
            hop(2, j, z_third, "e").wait_recv()

            @pl.when(jnp.logical_not(even))
            def _():
                hop(1, j, s, "x").start()

            core_hop(j, z_third)
        j = k - x_lag
        if 0 <= j < COUNT:
            hop(1, j, x_third, "x").wait_recv()
            core_hop(j, x_third)

    def weight_ready(k):
        own_block = held.at[pl.ds(spot(k, g), SHARD)]
        pltpu.make_async_copy(shard_block(shards, k, 0, SHARD), own_block, w_own.at[k]).wait()
        theirs = held.at[pl.ds(spot(k, g ^ 1), SHARD)]
        remote(theirs, theirs, w_send.at[3, k], w_recv.at[3, k], near["c"]).wait_recv()
        theirs = held.at[pl.ds(spot(k, g ^ 3), SHARD)]
        remote(theirs, theirs, w_send.at[4, k], w_recv.at[4, k], near["c"]).wait_recv()

    def gather_done():
        for k in range(COUNT):
            first_hop(k).wait_send()
            hop(2, k, y_third, "e").wait_send()
            hop(1, k, s, "x").wait_send()
            core_own(k).wait_send()
            core_wait(k).wait_send()

    def spread_matrix(seg):
        i = lax.broadcasted_iota(jnp.int32, (VEC[1], D), 0)
        j = lax.broadcasted_iota(jnp.int32, (VEC[1], D), 1)
        hit = jnp.logical_and(j == i + seg * SHARD, i < SHARD)
        return jnp.where(hit, 1.0, 0.0).astype(LOW)

    def vectors_ready():
        loads[2].wait()
        for copy in vec_copies:
            copy.wait()
        vec_segs[...] = jnp.zeros_like(vec_segs)
        for row, parts in SEGMENTS.items():
            for seg, (q, at) in enumerate(parts):
                vec_segs[seg, row : row + 1, :] = vecs[q, at : at + 1, :]
        full = jnp.zeros((VEC[0], D), F32)
        for seg in range(GROUPS):
            full = full + dot(vec_segs[seg].astype(LOW), spread_matrix(seg))
        rows_f32[...] = full

    def vector(row):
        return rows_f32[row : row + 1, :]

    def vector_tile(row, j):
        return rows_f32[row : row + 1, pl.ds(at128(j * TILE), TILE)]

    def block(n, j=None):
        start = n * D
        if not isinstance(n, int):
            start = at16(start)
        if j is None:
            return held[pl.ds(start, D), :]
        return held[pl.ds(start, D), pl.ds(at128(j * TILE), TILE)]

    def row_tiles(body):
        @pl.loop(0, rows // WIN)
        def _(i):
            body(pl.ds(at128(i * WIN), WIN), i)

    def col_tiles(body):
        @pl.loop(0, D // TILE)
        def _(j):
            body(pl.ds(at128(j * TILE), TILE), j)

    def norm_first():
        loads[0].wait()

        def one(here, i):
            unit, _ = normalized(chars_v[here, :].astype(F32))
            normed[here, :] = (unit * vector(A_GAIN) + vector(A_BIAS)).astype(LOW)

        row_tiles(one)

    def project_block(n):
        def one(here, j):
            value = dot(normed[...], block(QKV + n, j))
            if n == 0:
                value = value + vector_tile(Q_BIAS, j)
            if n == 2:
                value = value + vector_tile(V_BIAS, j)
            projected[n, :, here] = value.astype(LOW)

        col_tiles(one)

    def key_bias(w):
        code = codes[pl.ds(s * windows + w, 1), :]
        return jnp.where(code != 0, 0.0, mask_value).astype(F32)

    def lanes():
        return lax.broadcasted_iota(jnp.int32, (WIN, PAIR), 1) < HEAD_DIM

    def two_heads(values):
        first = lanes()
        zero = jnp.zeros_like(values)
        return jnp.concatenate(
            [jnp.where(first, values, zero), jnp.where(first, zero, values)], axis=0
        )

    def one_pair(values):
        return jnp.where(lanes(), values[:WIN], values[WIN:])

    scale_factor = HEAD_DIM ** (-0.5)

    def attend():
        def one(here, w):
            bias = key_bias(w)
            for p in range(PAIRS):
                cols = pl.ds(p * PAIR, PAIR)
                queries = two_heads(projected[0, here, cols])
                scores = dot_turned(queries, projected[1, here, cols]) * scale_factor + bias
                top = jnp.max(scores, axis=-1, keepdims=True)
                weight = jnp.exp(scores - top)
                weight = weight / jnp.sum(weight, axis=-1, keepdims=True)
                prob = weight.astype(LOW)
                probs[w, p] = prob
                context[here, cols] = one_pair(dot(prob, projected[2, here, cols])).astype(LOW)

        row_tiles(one)

    def attend_out():
        def one(here, j):
            value = dot(context[...], block(OUT, j)) + vector_tile(O_BIAS, j)
            hidden[:, here] = chars_v[:, here].astype(F32) + value

        col_tiles(one)

        def norm(here, i):
            unit, _ = normalized(hidden[here, :])
            normed_ffn[here, :] = (unit * vector(F_GAIN) + vector(F_BIAS)).astype(LOW)

        row_tiles(norm)

    def inner_block(n):
        def one(here, j):
            value = dot(normed_ffn[...], block(FIN + n, j)) + vector_tile(IN_BIAS + n, j)
            gelu, grad = gelu_parts(value)
            active[n, :, here] = gelu.astype(LOW)
            slope[n, :, here] = grad.astype(LOW)

        col_tiles(one)

    def by_place():
        i = lax.broadcasted_iota(jnp.int32, (WIN, WIN), 0)
        j = lax.broadcasted_iota(jnp.int32, (WIN, WIN), 1)
        return jnp.where(j == KERNEL * lax.rem(i, RUN) + i // RUN, 1.0, 0.0).astype(LOW)

    def layer_end():
        def one(here, j):
            value = hidden[:, here] + vector_tile(FO_BIAS, j)
            for n in range(BLOCKS):
                value = value + dot(active[n], block(FOUT + n, j))
            low_grad[:, here] = value.astype(LOW)

        col_tiles(one)
        order = by_place()

        def sort(here, w):
            moved = dot(order, low_grad[here, :]).astype(LOW)
            for k in range(KERNEL):
                stacked[k, pl.ds(at16(w * RUN), RUN), :] = moved[k * RUN : (k + 1) * RUN]

        row_tiles(sort)

    def note(row, value):
        vec_grads[row : row + 1, :] = value

    def note_more(row, value):
        vec_grads[row : row + 1, :] = vec_grads[row : row + 1, :] + value

    def convolve():
        loads[1].wait()
        value = jnp.zeros((mols, D), F32) + vector(C_BIAS)
        for k in range(KERNEL):
            value = value + dot(stacked[k], block(CONV + k))
        gelu, grad = gelu_parts(value)
        unit, scale = normalized(gelu)
        mol_v[...] = (unit * vector(D_GAIN) + vector(D_BIAS)).astype(LOW)
        wide = cot_v[...].astype(F32)
        note(D_GAIN, column_sum(wide * unit))
        note(D_BIAS, column_sum(wide))
        grad_conv = (norm_back(unit, scale, vector(D_GAIN), wide) * grad).astype(LOW)
        cot_v[...] = grad_conv
        note(C_BIAS, column_sum(grad_conv.astype(F32)))

    def convolve_back():
        for k in range(KERNEL):
            total[k * mols : (k + 1) * mols, :] = dot_turned(cot_v[...], block(CONV + k))

        for k in range(KERNEL):

            def one(here, j):
                value = dot_rows(stacked[k, :, here], cot_v[...])
                held[pl.ds(at128((CONV + k) * D + j * TILE), TILE), :] = value.astype(LOW)

            col_tiles(one)

        order = by_place()

        def sort(here, w):
            parts = [total[pl.ds(at16(k * mols + w * RUN), RUN), :] for k in range(KERNEL)]
            value = dot_rows(order, jnp.concatenate(parts, axis=0).astype(LOW))
            layer[here, :] = value
            low_grad[here, :] = value.astype(LOW)
            note_more(FO_BIAS, column_sum(value))

        row_tiles(sort)

    def weight_grad(n, left, right):
        def one(here, j):
            value = dot_rows(left[:, here], right[...])
            held[pl.ds(at128(n * D + j * TILE), TILE), :] = value.astype(LOW)

        col_tiles(one)

    def active_back(n):
        def one(here, j):
            value = dot_turned(
                low_grad[...], held[pl.ds(at128((FOUT + n) * D + j * TILE), TILE), :]
            )
            inner = (value * slope[n, :, here].astype(F32)).astype(LOW)
            slope[n, :, here] = inner
            vec_grads[IN_BIAS + n : IN_BIAS + n + 1, here] = column_sum(inner.astype(F32))

        col_tiles(one)
        weight_grad(FOUT + n, active.at[n], low_grad)

    def inner_sum():
        def one(here, j):
            value = jnp.zeros((rows, TILE), F32)
            for n in range(BLOCKS):
                value = value + dot_turned(
                    slope[n], held[pl.ds(at128((FIN + n) * D + j * TILE), TILE), :]
                )
            total[:, here] = value

        col_tiles(one)

    def hidden_back():
        def one(here, i):
            unit, scale = normalized(hidden[here, :])
            grad = total[here, :]
            note_more(F_GAIN, column_sum(grad * unit))
            note_more(F_BIAS, column_sum(grad))
            value = layer[here, :] + norm_back(unit, scale, vector(F_GAIN), grad)
            layer[here, :] = value
            low = value.astype(LOW)
            low_grad[here, :] = low
            note_more(O_BIAS, column_sum(low.astype(F32)))

        row_tiles(one)

    def context_back():
        def one(here, j):
            value = dot_turned(low_grad[...], held[pl.ds(at128(OUT * D + j * TILE), TILE), :])
            normed_ffn[:, here] = value.astype(LOW)

        col_tiles(one)
        weight_grad(OUT, context, low_grad)

    def attend_back(w):
        here = pl.ds(w * WIN, WIN)
        for p in range(PAIRS):
            cols = pl.ds(p * PAIR, PAIR)
            grad_out = two_heads(normed_ffn[here, cols])
            prob = probs[w, p]
            wide = prob.astype(F32)
            grad_prob = dot_turned(grad_out, projected[2, here, cols])
            inner = jnp.sum(wide * grad_prob, axis=-1, keepdims=True)
            grad_score = (wide * (grad_prob - inner)).astype(LOW)
            grad_value = dot_rows(prob, grad_out)
            grad_query = one_pair(dot(grad_score, projected[1, here, cols])) * scale_factor
            grad_key = (
                dot_rows(grad_score, two_heads(projected[0, here, cols])) * scale_factor
            )
            low_query, low_value = grad_query.astype(LOW), grad_value.astype(LOW)
            slope[0, here, cols] = low_query
            slope[1, here, cols] = grad_key.astype(LOW)
            slope[2, here, cols] = low_value
            for row, low in ((Q_BIAS, low_query), (V_BIAS, low_value)):
                vec_grads[row : row + 1, cols] = vec_grads[row : row + 1, cols] + column_sum(
                    low.astype(F32)
                )

    def project_sum():
        def one(here, j):
            value = jnp.zeros((rows, TILE), F32)
            for n in range(3):
                value = value + dot_turned(
                    slope[n], held[pl.ds(at128((QKV + n) * D + j * TILE), TILE), :]
                )
            total[:, here] = value

        col_tiles(one)

    def chars_back():
        def one(here, i):
            unit, scale = normalized(chars_v[here, :].astype(F32))
            grad = total[here, :]
            note_more(A_GAIN, column_sum(grad * unit))
            note_more(A_BIAS, column_sum(grad))
            value = layer[here, :] + norm_back(unit, scale, vector(A_GAIN), grad)
            context[here, :] = value.astype(LOW)

        row_tiles(one)

    def swap(i, whole, dst, count):
        keep = whole.at[:, pl.ds(at128(s * HALF), HALF)]
        give = whole.at[:, pl.ds(at128((1 - s) * HALF), HALF)]
        there = dst.at[pl.ds(at16(s * count), count)]
        stay = pltpu.make_async_copy(keep, there, io_sem.at[3 + i])
        go = remote(give, there, swap_send.at[i], swap_recv.at[i], near["x"])
        stay.start()
        go.start()
        return [stay, go]

    c = lax.rem(g, 2)
    y = g // 2
    mine, yours = 2 * y + c, 2 * (1 - y) + c
    z_half, w_half = lax.rem(r, 2), lax.rem(r // 2, 2)
    row_one = z_half * EIGHTH * 2
    row_two = row_one + w_half * EIGHTH

    def send(u, i, src, dst, way):
        at = SEM_AT[u] + i
        return remote(src, dst, g_send.at[at], g_recv.at[at], near[way])

    def cut(k, q, row, count, col=0, cols=D):
        return held.at[pl.ds(spot(k, q, row), count), pl.ds(at128(col), cols)]

    def final(k, row, count, col=None, cols=HALF):
        return shard_block(out, k, row, count, s * HALF if col is None else col, cols)

    def add_rows(k, q, row, count, col, cols, src):
        add_into(held, spot(k, q, row), count, col, cols, src)

    def keep(u, src, dst):
        return pltpu.make_async_copy(src, dst, g_own.at[u])

    def add_far(u, row, count, col, cols):
        k = UNITS[u][0]
        for i in range(extra):
            there = more_in.at[u, i, pl.ds(0, count), pl.ds(0, cols)]
            here = core_in.at[k, 0, pl.ds(row, count), pl.ds(0, cols)]
            copy = remote(
                cut(k, mine, row, count, col, cols),
                there,
                more_send.at[u, i],
                more_recv.at[u, i],
                far[i],
            )
            copy.start()
            copy.wait()
            copy = pltpu.make_async_copy(there, here, g_own.at[u])
            copy.start()
            copy.wait()
            add_rows(k, mine, row, count, col, cols, here)

    def core_sum(u, i):
        k, row, count, _ = UNITS[u]
        there = core_in.at[k, i, pl.ds(row, count)]
        return send(u, i, cut(k, 2 * i + 1 - c, row, count), there, "c")

    def y_sum(u):
        k, row, count, _ = UNITS[u]
        return send(u, 2, cut(k, yours, row, count), y_in.at[k, pl.ds(row, count)], "y")

    def y_added(u):
        k, row, count, _ = UNITS[u]
        y_sum(u).wait_recv()
        add_rows(k, mine, row, count, 0, D, y_in.at[k, pl.ds(row, count)])

    class Wide:
        sems = 8

        def __init__(self, u):
            self.u = u
            self.k, self.row, self.count, _ = UNITS[u]
            self.here = pl.ds(self.row, self.count)

        def part(self, side):
            return cut(self.k, mine, self.row, self.count, side * HALF, HALF)

        def done_part(self):
            return final(self.k, self.row, self.count)

        def x_sum(self):
            return send(self.u, 3, self.part(1 - s), x_in.at[self.k, self.here], "x")

        def e_sum(self):
            return send(self.u, 4, self.part(s), e_in.at[self.k, self.here], "e")

        def m_sum(self):
            return send(self.u, 5, self.part(s), m_in.at[self.k, self.here], "m")

        def e_back(self):
            return send(self.u, 6, self.part(s), self.done_part(), "e")

        def x_back(self, src):
            return send(self.u, 7, src, self.done_part(), "x")

        def own(self):
            return keep(self.u, self.part(s), self.done_part())

        def add(self, buffer):
            src = buffer.at[self.k, self.here]
            add_rows(self.k, mine, self.row, self.count, s * HALF, HALF, src)

        def step(self, n):
            if n == 1:
                y_sum(self.u).start()
            if n == 2:
                y_added(self.u)
                self.x_sum().start()
            if n == 3:
                self.x_sum().wait_recv()
                self.add(x_in)

                @pl.when(border)
                def _():
                    self.e_sum().start()

            if n == 4:

                @pl.when(middle)
                def _():
                    self.e_sum().wait_recv()
                    self.add(e_in)
                    self.m_sum().start()

            if n == 5:

                @pl.when(middle)
                def _():
                    self.m_sum().wait()
                    self.add(m_in)
                    add_far(self.u, self.row, self.count, s * HALF, HALF)
                    self.own().start()
                    self.e_back().start()
                    self.x_back(self.part(s)).start()

            if n == 6:

                @pl.when(border)
                def _():
                    self.e_back().wait_recv()
                    self.x_back(self.done_part()).start()

        def finish(self):
            y_sum(self.u).wait_send()
            self.x_sum().wait_send()

            @pl.when(border)
            def _():
                self.e_sum().wait_send()

            @pl.when(middle)
            def _():
                self.own().wait()
                self.e_back().wait_send()

            self.x_back(self.part(s)).wait()

    class Line(Wide):
        sems = 12

        def half(self, which):
            return self.row + which * (self.count // 2)

        def rows_of(self, which, side=None):
            col, cols = (0, D) if side is None else (side * HALF, HALF)
            return cut(self.k, mine, self.half(which), self.count // 2, col, cols)

        def done_rows(self, which):
            return final(self.k, self.half(which), self.count // 2, 0, D)

        def e_sum(self, side):
            there = (x_in, e_in)[side].at[self.k, self.here]
            return send(self.u, 3 + side, self.part(side), there, "e")

        def m_sum(self, side):
            there = m_in.at[self.k, pl.ds(self.half(side), self.count // 2)]
            return send(self.u, 5 + side, self.rows_of(1 - w_half, side), there, "m")

        def x_sum(self):
            there = line_in.at[LINES.index(self.k), pl.ds(self.row // 2, self.count // 2)]
            return send(self.u, 7, self.rows_of(w_half), there, "x")

        def m_back(self):
            return send(self.u, 8, self.rows_of(w_half), self.done_rows(w_half), "m")

        def e_back(self, i):
            if i == 0:
                return send(self.u, 9, self.rows_of(w_half), self.done_rows(w_half), "e")
            there = self.done_rows(1 - w_half)
            return send(self.u, 10, there, there, "e")

        def own(self):
            return keep(self.u, self.rows_of(w_half), self.done_rows(w_half))

        def step(self, n):
            if n == 1:
                y_sum(self.u).start()
            if n == 2:
                y_added(self.u)

                @pl.when(border)
                def _():
                    for side in range(2):
                        self.e_sum(side).start()

            if n == 3:

                @pl.when(middle)
                def _():
                    for side in range(2):
                        self.e_sum(side).wait_recv()
                        src = (x_in, e_in)[side].at[self.k, self.here]
                        add_rows(self.k, mine, self.row, self.count, side * HALF, HALF, src)
                    for side in range(2):
                        self.m_sum(side).start()

            if n == 4:

                @pl.when(middle)
                def _():
                    for side in range(2):
                        self.m_sum(side).wait_recv()
                        src = m_in.at[self.k, pl.ds(self.half(side), self.count // 2)]
                        row = self.half(w_half)
                        add_rows(self.k, mine, row, self.count // 2, side * HALF, HALF, src)
                    self.x_sum().start()

            if n == 5:

                @pl.when(middle)
                def _():
                    self.x_sum().wait()
                    src = line_in.at[LINES.index(self.k), pl.ds(self.row // 2, self.count // 2)]
                    add_rows(self.k, mine, self.half(w_half), self.count // 2, 0, D, src)
                    add_far(self.u, self.half(w_half), self.count // 2, 0, D)
                    self.own().start()
                    self.m_back().start()
                    self.e_back(0).start()

            if n == 6:

                @pl.when(middle)
                def _():
                    self.m_back().wait_recv()
                    self.e_back(1).start()

        def finish(self):
            y_sum(self.u).wait_send()

            @pl.when(border)
            def _():
                for side in range(2):
                    self.e_sum(side).wait_send()
                for i in range(2):
                    self.e_back(i).wait_recv()

            @pl.when(middle)
            def _():
                for side in range(2):
                    self.m_sum(side).wait_send()
                self.own().wait()
                self.m_back().wait_send()
                for i in range(2):
                    self.e_back(i).wait_send()

    class Deep:
        sems = 14
        first_x = False

        def __init__(self, u):
            self.u = u
            self.k = UNITS[u][0]

        def one(self, i):
            src = cut(self.k, 2 * i + c, (1 - z_half) * EIGHTH * 2, 2 * EIGHTH)
            return send(self.u, 2 + i, src, self.one_in(i), "e")

        def one_in(self, i):
            return y_in.at[self.k, pl.ds(i * 2 * EIGHTH, 2 * EIGHTH)]

        def two(self, i, side):
            row = row_one + (1 - w_half) * EIGHTH
            src = cut(self.k, 2 * i + c, row, EIGHTH, side * HALF, HALF)
            return send(self.u, 4 + 2 * i + side, src, self.two_in(i, side), "w")

        def two_in(self, i, side):
            return x_in.at[self.k, pl.ds((2 * i + side) * EIGHTH, EIGHTH)]

        def x_sum(self, i):
            src = cut(self.k, 2 * i + c, row_two, EIGHTH, (1 - s) * HALF, HALF)
            return send(self.u, 8 + i, src, self.x_in(i), "x")

        def x_in(self, i):
            return e_in.at[self.k, pl.ds(i * EIGHTH, EIGHTH)]

        def last(self):
            src = cut(self.k, yours, row_two, EIGHTH, s * HALF, HALF)
            return send(self.u, 10, src, self.x_in(2), "y")

        def piece(self):
            return cut(self.k, mine, row_two, EIGHTH, s * HALF, HALF)

        def own(self):
            return keep(self.u, self.piece(), final(self.k, row_two, EIGHTH))

        def back(self, n):
            if n == 0:
                way = "x" if self.first_x else "w"
                return send(self.u, 11, self.piece(), final(self.k, row_two, EIGHTH), way)
            if self.first_x:
                row, count = (row_two, EIGHTH) if n == 1 else (row_one, 2 * EIGHTH)
                here = final(self.k, row, count, 0, D)
                return send(self.u, 11 + n, here, here, "we"[n - 1])
            row, count = (row_one, 2 * EIGHTH) if n == 1 else (0, SHARD)
            here = final(self.k, row, count)
            return send(self.u, 11 + n, here, here, "ex"[n - 1])

        def step(self, n):
            if n == 1:
                for i in range(2):
                    self.one(i).start()
            if n == 2:
                for i in range(2):
                    self.one(i).wait_recv()
                    add_rows(self.k, 2 * i + c, row_one, 2 * EIGHTH, 0, D, self.one_in(i))
                    for side in range(2):
                        self.two(i, side).start()
            if n == 3:
                for i in range(2):
                    for side in range(2):
                        self.two(i, side).wait_recv()
                        here = self.two_in(i, side)
                        add_rows(self.k, 2 * i + c, row_two, EIGHTH, side * HALF, HALF, here)
                    self.x_sum(i).start()
            if n == 4:
                for i in range(2):
                    self.x_sum(i).wait_recv()
                    add_rows(self.k, 2 * i + c, row_two, EIGHTH, s * HALF, HALF, self.x_in(i))
                self.last().start()
            if n == 5:
                self.last().wait_recv()
                add_rows(self.k, mine, row_two, EIGHTH, s * HALF, HALF, self.x_in(2))
                add_far(self.u, row_two, EIGHTH, s * HALF, HALF)
                self.own().start()
                self.back(0).start()
            if n == 6:
                self.own().wait()
                self.back(0).wait_recv()
                self.back(1).start()
            if n == 7:
                self.back(1).wait_recv()
                self.back(2).start()

        def finish(self):
            for i in range(2):
                self.one(i).wait_send()
                for side in range(2):
                    self.two(i, side).wait_send()
                self.x_sum(i).wait_send()
            self.last().wait_send()
            for n in range(2):
                self.back(n).wait_send()
            self.back(2).wait()

    class DeepX(Deep):
        first_x = True

    kinds = {"wide": Wide, "line": Line, "deep": Deep, "deep_x": DeepX}
    sums = [kinds[unit[3]](u) for u, unit in enumerate(UNITS)]

    def sum_step(u, n):
        if n == 0:
            for i in range(2):
                core_sum(u, i).start()
            return
        if n == 1:
            k, row, count, _ = UNITS[u]
            for i in range(2):
                core_sum(u, i).wait_recv()
                src = core_in.at[k, i, pl.ds(row, count)]
                add_rows(k, 2 * i + c, row, count, 0, D, src)
        sums[u].step(n)

    def sums_done():
        for u in range(len(UNITS)):
            for i in range(2):
                core_sum(u, i).wait_send()
            sums[u].finish()

    vec_steps = 6 + extra
    vec_moves = []

    def vec_step(n):
        if n == 0:
            top = vec_grads[...]
            high = top.astype(LOW)
            low = (top - high.astype(F32)).astype(LOW)
            for seg in range(GROUPS):
                spread = spread_matrix(seg)
                vec_segs[seg] = dot_turned(high, spread) + dot_turned(low, spread)
            for row, parts in SEGMENTS.items():
                for seg, (q, at) in enumerate(parts):
                    vecs[q, at : at + 1, :] = vec_segs[seg, row : row + 1, :]
            for i in range(2):
                copy = remote(
                    vecs.at[2 * i + 1 - c], vec_in.at[i], v_send.at[3 + i], v_recv.at[3 + i], near["c"]
                )
                copy.start()
                vec_moves.append(copy)
            return
        if n == 1:
            for i in range(2):
                vec_moves[i].wait()
                vecs[2 * i + c] = vecs[2 * i + c] + vec_in[i]
        else:
            vec_moves[-1].wait()
            vecs[mine] = vecs[mine] + vec_in[n]
        steps = [near["y"], near["x"], near["e"], near["w"]] + far
        if n <= len(steps):
            copy = remote(
                vecs.at[yours if n == 1 else mine],
                vec_in.at[1 + n],
                v_send.at[4 + n],
                v_recv.at[4 + n],
                steps[n - 1],
            )
            copy.start()
            vec_moves.append(copy)
        else:
            copy = pltpu.make_async_copy(vecs.at[mine], vec_out, io_sem.at[2])
            copy.start()
            copy.wait()

    vec_grads[...] = jnp.zeros_like(vec_grads)
    gather_step(0)
    vectors_ready()
    gather_step(1)
    norm_first()
    forward = [
        ([0], lambda: project_block(0)),
        ([1], lambda: project_block(1)),
        ([2], lambda: project_block(2)),
        ([], attend),
        ([3], attend_out),
    ]
    forward += [([FIN + n], functools.partial(inner_block, n)) for n in range(BLOCKS)]
    forward += [([8, 9, 10, 11], layer_end), ([12, 13, 14, 15], convolve)]
    for step in range(2, COUNT + x_lag):
        gather_step(step)
        while forward and all(k <= step - x_lag - 1 for k in forward[0][0]):
            need, work = forward.pop(0)
            for k in need:
                weight_ready(k)
            work()
    for need, work in forward:
        for k in need:
            weight_ready(k)
        work()
    gather_done()

    moves = []

    def end_convolution():
        convolve_back()
        moves.extend(swap(0, mol_v, mols_out, mols))

    def end_chars():
        chars_back()
        moves.extend(swap(1, context, chars_out, rows))

    backward = [end_convolution]
    backward += [functools.partial(active_back, n) for n in range(BLOCKS)]
    backward += [inner_sum]
    backward += [
        functools.partial(weight_grad, FIN + n, normed_ffn, slope.at[n]) for n in range(BLOCKS)
    ]
    backward += [hidden_back, context_back]
    backward += [functools.partial(attend_back, w) for w in range(windows)]
    backward += [project_sum]
    backward += [functools.partial(weight_grad, QKV + n, normed, slope.at[n]) for n in range(3)]
    backward += [end_chars]
    backward += [functools.partial(vec_step, n) for n in range(vec_steps)]
    for item in PLAN:
        if item < 0:
            backward.pop(0)()
        else:
            sum_step(item // 10, item % 10)
    for work in backward:
        work()
    sums_done()
    for copy in moves:
        copy.wait()


def run(args, chars, extra):
    rows = chars.shape[0] // 2
    mols = rows // KERNEL
    anywhere = pl.BlockSpec(memory_space=pl.ANY)
    dma = pltpu.SemaphoreType.DMA
    vmem = pltpu.VMEM
    windows = rows // WIN
    return pl.pallas_call(
        functools.partial(program_kernel, rows, extra),
        name="layer_and_sums",
        out_shape=[
            jax.ShapeDtypeStruct((2 * mols, HALF), LOW),
            jax.ShapeDtypeStruct((2 * rows, HALF), LOW),
            jax.ShapeDtypeStruct(VEC, F32),
        ]
        + [jax.ShapeDtypeStruct(shape, LOW) for shape in SHARD_SHAPES]
        + [jax.ShapeDtypeStruct((len(UNITS), extra, SHARD, D), LOW)] * (extra > 0),
        in_specs=[anywhere, pl.BlockSpec(memory_space=vmem)] + [anywhere] * 7,
        out_specs=[anywhere] * (8 + (extra > 0)),
        scratch_shapes=[
            vmem((COUNT * D, D), LOW),
            vmem((COUNT, 2, SHARD, D), LOW),
            vmem((COUNT, SHARD, D), LOW),
            vmem((COUNT, SHARD, HALF), LOW),
            vmem((COUNT, SHARD, HALF), LOW),
            vmem((COUNT, SHARD, HALF), LOW),
            vmem((max(len(LINES), 1), SHARD // 2, D), LOW),
            vmem((GROUPS,) + VEC, F32),
            vmem((GROUPS,) + VEC, F32),
            vmem((VEC[0], D), F32),
            vmem((VEC[0], D), F32),
            vmem((7 + extra,) + VEC, F32),
            vmem((rows, D), LOW),
            vmem((mols, D), LOW),
            vmem((rows, D), LOW),
            vmem((3, rows, D), LOW),
            vmem((windows, PAIRS, 2 * WIN, WIN), LOW),
            vmem((rows, D), LOW),
            vmem((rows, D), F32),
            vmem((rows, D), LOW),
            vmem((BLOCKS, rows, D), LOW),
            vmem((BLOCKS, rows, D), LOW),
            vmem((rows, D), F32),
            vmem((KERNEL, mols, D), LOW),
            vmem((rows, D), LOW),
            vmem((rows, D), F32),
            vmem((mols, D), LOW),
            dma((5, COUNT)),
            dma((5, COUNT)),
            dma((COUNT,)),
            dma((SEMS,)),
            dma((SEMS,)),
            dma((len(UNITS),)),
            dma((len(UNITS), max(extra, 1))),
            dma((len(UNITS), max(extra, 1))),
            dma((9 + extra,)),
            dma((9 + extra,)),
            dma((5,)),
            dma((2,)),
            dma((2,)),
        ],
        compiler_params=pltpu.CompilerParams(
            collective_id=0, has_side_effects=True, vmem_limit_bytes=63 << 20
        ),
    )(*args)


VEC_COUNTS = [1, 1, 2, 1, 1, 1, 4, 1, 1, 1, 1]


def body(
    chars,
    char_codes,
    mol_cotangent,
    attn_norm_gain,
    attn_norm_bias,
    qkv_weight,
    qv_bias,
    out_weight,
    out_bias,
    ffn_norm_gain,
    ffn_norm_bias,
    ffn_in_weight,
    ffn_in_bias,
    ffn_out_weight,
    ffn_out_bias,
    conv_weight,
    conv_bias,
    down_norm_gain,
    down_norm_bias,
):
    vectors = [
        attn_norm_gain,
        attn_norm_bias,
        qv_bias,
        out_bias,
        ffn_norm_gain,
        ffn_norm_bias,
        ffn_in_bias,
        ffn_out_bias,
        conv_bias,
        down_norm_gain,
        down_norm_bias,
    ]
    pieces = []
    for v in vectors:
        for i in range(v.shape[0] // SHARD):
            pieces += [v[i * SHARD : (i + 1) * SHARD], jnp.zeros((VEC[1] - SHARD,), LOW)]
    pieces.append(jnp.zeros((VEC[1],), LOW))
    packed = jnp.concatenate(pieces).astype(F32).reshape(VEC)
    result = run(
        (
            chars,
            char_codes.reshape(-1, WIN),
            mol_cotangent,
            packed,
            qkv_weight,
            out_weight,
            ffn_in_weight,
            ffn_out_weight,
            conv_weight,
        ),
        chars,
        (lax.axis_size("replica") // RING).bit_length() - 1,
    )
    molecules, chars_grad, vec_sum = result[:3]
    t_qkv, t_out, t_in, t_ffo, t_conv = [w.astype(F32) for w in result[3:8]]
    v = []
    row = 0
    for count in VEC_COUNTS:
        v.append(jnp.concatenate([vec_sum[row + i, :SHARD] for i in range(count)]))
        row += count
    return (
        molecules,
        chars_grad,
        v[0],
        v[1],
        t_qkv,
        v[2],
        t_out,
        v[3],
        v[4],
        v[5],
        t_in,
        v[6],
        t_ffo,
        v[7],
        t_conv,
        v[8],
        v[9],
        v[10],
    )


def solution(mesh):
    return jax.shard_map(
        body,
        mesh=mesh,
        in_specs=(
            P(("group", "replica"), None),
            P(("group", "replica")),
            P(("group", "replica"), None),
            P("group"),
            P("group"),
            P("group", None),
            P("group"),
            P("group", None),
            P("group"),
            P("group"),
            P("group"),
            P("group", None),
            P("group"),
            P("group", None),
            P("group"),
            P("group", None),
            P("group"),
            P("group"),
            P("group"),
        ),
        out_specs=(
            P(("group", "replica"), "section"),
            P(("group", "replica"), "section"),
            P("group"),
            P("group"),
            P("group", None),
            P("group"),
            P("group", None),
            P("group"),
            P("group"),
            P("group"),
            P("group", None),
            P("group"),
            P("group", None),
            P("group"),
            P("group", None),
            P("group"),
            P("group"),
            P("group"),
        ),
        check_vma=False,
    )
```

```python
import functools
import math

import jax
import jax.numpy as jnp
from jax import lax
from jax.experimental import pallas as pl
from jax.experimental.pallas import tpu as pltpu
from jax.sharding import PartitionSpec as P

D = 768
HEADS = 12
HEAD_DIM = 64
FF = 3072
WIN = 128
KERNEL = 4
GROUPS = 4
RING = 4
SHARD = D // GROUPS
THIRD = SHARD // 3
EIGHTH = SHARD // 4
HALF = D // 2
TILE = 768
PAIR = 2 * HEAD_DIM
PAIRS = HEADS // 2
RUN = WIN // KERNEL
BLOCKS = FF // D
VEC = (16, 256)
VEC_COUNTS = (1, 1, 2, 1, 1, 1, 4, 1, 1, 1, 1)
SCRATCH = 28
norm_eps = 1e-06
mask_value = -10000.0
MESH = pl.DeviceIdType.MESH
F32 = jnp.float32
LOW = jnp.bfloat16

CHUNKS = (
    [(0, "col", j) for j in range(3)]
    + [(1, "col", 0)]
    + [(2, "col", j) for j in range(4)]
    + [(3, "row", j) for j in range(4)]
    + [(4, "row", j) for j in range(4)]
)
COUNT = len(CHUNKS)
QKV, OUT, FIN, FOUT, CONV = BASES = (0, 3, 4, 8, 12)
SHARD_SHAPES = [(SHARD, 3 * D), (SHARD, D), (SHARD, FF), (FF // GROUPS, D), (D, D)]

A_GAIN, A_BIAS, Q_BIAS, V_BIAS, O_BIAS, F_GAIN, F_BIAS = range(7)
IN_BIAS, FO_BIAS, C_BIAS, D_GAIN, D_BIAS = 7, 11, 12, 13, 14


def segments():
    table = {}
    for row, at in zip((A_GAIN, A_BIAS, O_BIAS, F_GAIN, F_BIAS), (0, 1, 4, 5, 6)):
        table[row] = [(q, at) for q in range(GROUPS)]
    table[Q_BIAS] = [(0, 2), (0, 3), (1, 2), (1, 3)]
    table[V_BIAS] = [(2, 2), (2, 3), (3, 2), (3, 3)]
    for n in range(BLOCKS):
        table[IN_BIAS + n] = [(n, 7 + i) for i in range(4)]
    for row, at in zip((FO_BIAS, C_BIAS, D_GAIN, D_BIAS), (11, 12, 13, 14)):
        table[row] = [(q, at) for q in range(GROUPS)]
    return table


SEGMENTS = segments()

PIECES = [
    (0, 0, 1), (1, 0, 1), (2, 0, 1), (3, 0, 1), (4, 0, 1), (5, 0, 1), (6, 0, 1), (7, 0, 1),
    (8, 0, 1), (9, 0, 1), (10, 0, 1), (11, 0, 1), (12, 0, 1), (13, 0, 1), (14, 0, 2), (14,
    1, 2), (15, 0, 2), (15, 1, 2),
]
GATHER_PLAN = [
    -1, -1, 0, 10, 1, 20, 11, 30, 2, 21, 40, -1, 12, 31, 50, 22, 41, 60, -1, -1, 32, 51, 70,
    -1, -1, 42, 61, 80, -1, 52, 71, 90, -1, -1, 62, 81, 100, -1, 72, 91, 110, -1, 82, 101,
    120, -1, 130, 92, 111, 140, -1, 150, 102, 121, 160, 170, 112, 131, 141, -1, 122, 132,
    151, 142, 161, 171, 152, 162, 172, -1,
]

UNITS = [
    (12, 0, 192, "wide"),
    (13, 0, 192, "wide"),
    (14, 0, 192, "deep"),
    (15, 0, 192, "deep"),
    (8, 0, 192, "wide"),
    (9, 0, 192, "wide"),
    (10, 0, 192, "wide"),
    (11, 0, 192, "wide"),
    (4, 0, 192, "wide"),
    (5, 0, 192, "line"),
    (6, 0, 64, "wide"),
    (6, 64, 64, "wide"),
    (6, 128, 64, "wide"),
    (7, 0, 96, "line"),
    (7, 96, 96, "line"),
    (3, 0, 192, "deep"),
    (0, 0, 64, "line"),
    (0, 64, 64, "line"),
    (0, 128, 64, "line"),
    (1, 0, 48, "wide"),
    (1, 48, 48, "wide"),
    (1, 96, 48, "wide"),
    (1, 144, 48, "wide"),
    (2, 0, 48, "wide"),
    (2, 48, 48, "wide"),
    (2, 96, 48, "wide"),
    (2, 144, 48, "wide"),
]

SEM_COUNT = {"wide": 5, "line": 6, "deep": 8, "deep_x": 8}
SEM_AT = [sum(SEM_COUNT[unit[3]] for unit in UNITS[:u]) for u in range(len(UNITS))]
SEMS = sum(SEM_COUNT[unit[3]] for unit in UNITS)
LINES = sorted({unit[0] for unit in UNITS if unit[3] == "line"})
PLAN = [
    -1, 0, 10, 30, 20, -1, 1, 11, 31, -1, 21, -1, -1, 50, 40, 70, 2, 32, 60, -1, 51, 41, 71,
    61, -1, 80, 3, 12, -1, 90, 22, 81, -1, 100, 110, 120, 91, -1, 130, 140, 101, 52, 111,
    121, 4, 33, 131, 141, 13, -1, -1, 42, 34, 53, 14, 23, 150, -1, -1, 5, 43, 151, 54, -1,
    24, 72, 15, -1, 44, 6, -1, 55, 62, 73, -1, 160, 170, 180, 45, -1, 190, 200, 210, 220,
    161, 171, 181, 152, 191, 201, 211, 82, 16, 221, 74, -1, 230, 240, 250, 260, -1, 56, 63,
    -1, 231, 241, 251, 261, 92, 46, -1, 102, 64, 83, 153, 112, 122, 75, 132, 93, 65, 76,
    142, 84, 35, 25, 94, 66, 133, 162, 103, 85, 172, 143, 154, 113, 182, 36, 123, 192, 26,
    163, 202, 134, 104, 212, 86, 144, 95, 164, 173, 222, 105, 114, 232, 183, 193, 242, 203,
    96, 37, 252, 174, 135, 124, 106, 115, 213, 262, -1, 27, 184, 155, 145, 194, 204, 136,
    165, 214, 223, 125, 233, 116, 224, 156, 243, 146, 234, 195, 205, 253, 244, 166, 175,
    215, 126, 225, 254, 235, 263, 157, -1, 245, 176, 196, 264, 255, 206, 185, 265, 216, 226,
    186, 236, -1, 246, 256, 266, -1,
]


def at16(value):
    return pl.multiple_of(value, 16)


def at128(value):
    return pl.multiple_of(value, 128)


def spot(chunk, shard, first=0):
    mat, kind, j = CHUNKS[chunk]
    if kind == "col":
        return at16((BASES[mat] + j) * D + shard * SHARD + first)
    return at16((BASES[mat] + shard) * D + j * SHARD + first)


def shard_block(refs, chunk, first, rows, col=0, cols=D):
    mat, kind, j = CHUNKS[chunk]
    if kind == "col":
        return refs[mat].at[pl.ds(at16(first), rows), pl.ds(at128(j * D + col), cols)]
    return refs[mat].at[pl.ds(at16(j * SHARD + first), rows), pl.ds(at128(col), cols)]


def remote(src, dst, send, recv, target):
    return pltpu.make_async_remote_copy(
        src_ref=src,
        dst_ref=dst,
        send_sem=send,
        recv_sem=recv,
        device_id=target,
        device_id_type=MESH,
    )


class Tally:
    def __init__(self, sem, yard):
        self.sem, self.yard, self.size = sem, yard, 0

    def add(self, ref):
        self.size += math.prod(ref.shape)

    def wait(self):
        here = self.yard.at[pl.ds(0, self.size // D)]
        pltpu.make_async_copy(here, here, self.sem).wait()
        self.size = 0


class Move:
    def __init__(self, src, dst, sent, recv, target):
        self.src, self.dst, self.sent = src, dst, sent
        self.copy = remote(src, dst, sent.sem, recv, target)

    def start(self):
        self.sent.add(self.src)
        self.copy.start()

    def wait_recv(self):
        self.copy.wait_recv()


def add_to(dst, src):
    @pl.loop(0, dst.shape[0] // 16)
    def _(i):
        here = pl.ds(at16(i * 16), 16)
        dst[here, :] = dst[here, :] + src[here, :]


def dot(left, right):
    return jnp.dot(left, right, preferred_element_type=F32)


def dot_rows(left, right):
    return lax.dot_general(left, right, (((0,), (0,)), ((), ())), preferred_element_type=F32)


def dot_turned(left, right):
    return lax.dot_general(left, right, (((1,), (1,)), ((), ())), preferred_element_type=F32)


def normalized(values):
    center = values - jnp.mean(values, axis=-1, keepdims=True)
    scale = lax.rsqrt(jnp.mean(center * center, axis=-1, keepdims=True) + norm_eps)
    return center * scale, scale


def norm_back(unit, scale, gain, grad):
    grad_unit = grad * gain
    mean_grad = jnp.mean(grad_unit, axis=-1, keepdims=True)
    mean_both = jnp.mean(grad_unit * unit, axis=-1, keepdims=True)
    return scale * (grad_unit - mean_grad - unit * mean_both)


def gelu_parts(values):
    half = 0.5 * lax.erf(values * (0.5**0.5)) + 0.5
    bell = jnp.exp(-0.5 * values * values) * 0.3989422804014327
    return values * half, half + values * bell


def column_sum(values):
    return jnp.sum(values, axis=0, keepdims=True)


def program_kernel(rows, extra, *refs):
    count = len(VEC_COUNTS)
    (chars, codes, cotangent) = refs[:3]
    shards = refs[3:8]
    vectors = refs[8 : 8 + count]
    mols_out, chars_out, vec_out = refs[8 + count : 11 + count]
    out = refs[11 + count : 16 + count]
    more_in = refs[16 + count] if extra else None
    refs = refs[16 + count + (extra > 0) :]
    flat, refs = refs[:count], refs[count:]
    (
        held,
        core_in,
        y_in,
        x_in,
        e_in,
        m_in,
        line_in,
        vec,
        vecs,
        vec_segs,
        rows_f32,
        vec_grads,
        vec_in,
        chars_v,
        cot_v,
        normed,
        projected,
        probs,
        context,
        hidden,
        normed_ffn,
        slope,
        active,
        layer,
        stacked,
        low_grad,
        total,
        mol_v,
    ) = refs[:SCRATCH]
    (
        w_send,
        w_recv,
        c_recv,
        g_send,
        g_recv,
        more_send,
        more_recv,
        v_send,
        v_recv,
        io_sem,
        swap_send,
        swap_recv,
    ) = refs[SCRATCH:]
    windows = rows // WIN
    mols = rows // KERNEL
    s, g, r = lax.axis_index("section"), lax.axis_index("group"), lax.axis_index("replica")
    near = {
        "c": (s, g ^ 1, r),
        "y": (s, g ^ 2, r),
        "x": (1 - s, g, r),
        "e": (s, g, r ^ 1),
        "m": (s, g, r ^ 3),
        "d": (s, g ^ 3, r),
        "w": (s, g, r ^ 2),
    }
    far = [(s, g, r ^ (RING << i)) for i in range(extra)]
    place = lax.rem(r, RING)
    even = lax.rem(r, 2) == 0
    middle = jnp.logical_or(place == 1, place == 2)
    border = jnp.logical_not(middle)

    loads = [
        pltpu.make_async_copy(chars.at[pl.ds(at16(s * rows), rows)], chars_v, io_sem.at[0]),
        pltpu.make_async_copy(cotangent.at[pl.ds(at16(s * mols), mols)], cot_v, io_sem.at[1]),
    ]
    for copy in loads:
        copy.start()
    flat_copies = [
        pltpu.make_async_copy(src, dst, io_sem.at[5 + i])
        for i, (src, dst) in enumerate(zip(vectors, flat))
    ]
    for copy in flat_copies:
        copy.start()
    for k in range(COUNT):
        own_block = held.at[pl.ds(spot(k, g), SHARD)]
        pltpu.make_async_copy(shard_block(shards, k, 0, SHARD), own_block, c_recv.at[k]).start()
    vec[...] = jnp.zeros_like(vec)
    at = 0
    for copy, values, rows_held in zip(flat_copies, flat, VEC_COUNTS):
        copy.wait()
        wide = values[...].astype(F32)
        for i in range(rows_held):
            line = wide[i * SHARD : (i + 1) * SHARD].reshape(1, SHARD)
            vec[at : at + 1, pl.ds(0, SHARD)] = line
            at += 1
    own_vec = pltpu.make_async_copy(vec, vecs.at[g], io_sem.at[2])
    own_vec.start()

    barrier = pltpu.get_barrier_semaphore()
    greeted = list(near.values()) + far
    for target in greeted:
        pl.semaphore_signal(barrier, inc=1, device_id=target, device_id_type=MESH)
    pl.semaphore_wait(barrier, len(greeted))

    y_third = jnp.where(even, s, 2)
    z_third = jnp.where(even, 2, s)
    x_third = 1 - s
    other = g ^ 2

    vec_copies = [
        remote(vec, vecs.at[g], v_send.at[i], v_recv.at[i], near[way])
        for i, way in enumerate("cyd")
    ]
    for copy in vec_copies:
        copy.start()

    def piece_of(u, third):
        k, part, parts = PIECES[u]
        return k, third * THIRD + part * (THIRD // parts), THIRD // parts

    sent = Tally(w_send.at[0], held)

    def hop(i, u, third, way):
        k, first, count = piece_of(u, third)
        here = held.at[pl.ds(spot(k, other, first), count)]
        return Move(here, here, sent, w_recv.at[i, u], near[way])

    def first_hop(u):
        k, first, count = piece_of(u, y_third)
        src = shard_block(shards, k, first, count)
        there = held.at[pl.ds(spot(k, g, first), count)]
        return Move(src, there, sent, w_recv.at[0, u], near["y"])

    def core_own(k):
        src = shard_block(shards, k, 0, SHARD)
        there = held.at[pl.ds(spot(k, g), SHARD)]
        return Move(src, there, sent, c_recv.at[k], near["c"])

    def core_hop(u, third):
        k, first, count = piece_of(u, third)
        here = held.at[pl.ds(spot(k, other, first), count)]
        Move(here, here, sent, c_recv.at[k], near["c"]).start()

    for u in range(len(PIECES)):
        first_hop(u).start()
    for k in range(COUNT):
        core_own(k).start()

    def gather_step(u, n):
        if n == 0:
            hop(0, u, y_third, "y").wait_recv()
            hop(2, u, y_third, "e").start()

            @pl.when(even)
            def _():
                hop(1, u, s, "x").start()

            core_hop(u, y_third)
        if n == 1:
            hop(2, u, z_third, "e").wait_recv()

            @pl.when(jnp.logical_not(even))
            def _():
                hop(1, u, s, "x").copy.start()

            core_hop(u, z_third)
        if n == 2:
            hop(1, u, x_third, "x").wait_recv()
            core_hop(u, x_third)

    def weight_ready(k):
        here = held.at[pl.ds(0, 3 * SHARD)]
        pltpu.make_async_copy(here, here, c_recv.at[k]).wait()

    def gather_done():
        sent.wait()

    def spread_matrix(seg):
        i = lax.broadcasted_iota(jnp.int32, (VEC[1], D), 0)
        j = lax.broadcasted_iota(jnp.int32, (VEC[1], D), 1)
        hit = jnp.logical_and(j == i + seg * SHARD, i < SHARD)
        return jnp.where(hit, 1.0, 0.0).astype(LOW)

    def vectors_ready():
        own_vec.wait()
        for copy in vec_copies:
            copy.wait()
        vec_segs[...] = jnp.zeros_like(vec_segs)
        for row, parts in SEGMENTS.items():
            for seg, (q, at) in enumerate(parts):
                vec_segs[seg, row : row + 1, :] = vecs[q, at : at + 1, :]
        full = jnp.zeros((VEC[0], D), F32)
        for seg in range(GROUPS):
            full = full + dot(vec_segs[seg].astype(LOW), spread_matrix(seg))
        rows_f32[...] = full

    def vector(row):
        return rows_f32[row : row + 1, :]

    def vector_tile(row, j):
        return rows_f32[row : row + 1, pl.ds(at128(j * TILE), TILE)]

    def block(n, j=None):
        start = n * D
        if not isinstance(n, int):
            start = at16(start)
        if j is None:
            return held[pl.ds(start, D), :]
        return held[pl.ds(start, D), pl.ds(at128(j * TILE), TILE)]

    def row_tiles(body):
        @pl.loop(0, rows // WIN)
        def _(i):
            body(pl.ds(at128(i * WIN), WIN), i)

    def col_tiles(body):
        @pl.loop(0, D // TILE)
        def _(j):
            body(pl.ds(at128(j * TILE), TILE), j)

    def norm_first():
        loads[0].wait()

        def one(here, i):
            unit, _ = normalized(chars_v[here, :].astype(F32))
            normed[here, :] = (unit * vector(A_GAIN) + vector(A_BIAS)).astype(LOW)

        row_tiles(one)

    def project_block(n):
        def one(here, j):
            value = dot(normed[...], block(QKV + n, j))
            if n == 0:
                value = value + vector_tile(Q_BIAS, j)
            if n == 2:
                value = value + vector_tile(V_BIAS, j)
            projected[n, :, here] = value.astype(LOW)

        col_tiles(one)

    def key_bias(w):
        code = codes[pl.ds(s * windows + w, 1), :]
        return jnp.where(code != 0, 0.0, mask_value).astype(F32)

    def lanes():
        return lax.broadcasted_iota(jnp.int32, (WIN, PAIR), 1) < HEAD_DIM

    def two_heads(values):
        first = lanes()
        zero = jnp.zeros_like(values)
        return jnp.concatenate(
            [jnp.where(first, values, zero), jnp.where(first, zero, values)], axis=0
        )

    def one_pair(values):
        return jnp.where(lanes(), values[:WIN], values[WIN:])

    scale_factor = HEAD_DIM ** (-0.5)

    def attend(w):
        here = pl.ds(w * WIN, WIN)
        bias = key_bias(w)
        for p in range(PAIRS):
            cols = pl.ds(p * PAIR, PAIR)
            queries = two_heads(projected[0, here, cols])
            scores = dot_turned(queries, projected[1, here, cols]) * scale_factor + bias
            top = jnp.max(scores, axis=-1, keepdims=True)
            weight = jnp.exp(scores - top)
            weight = weight / jnp.sum(weight, axis=-1, keepdims=True)
            prob = weight.astype(LOW)
            probs[w, p] = prob
            context[here, cols] = one_pair(dot(prob, projected[2, here, cols])).astype(LOW)

    def attend_out():
        def one(here, j):
            value = dot(context[...], block(OUT, j)) + vector_tile(O_BIAS, j)
            hidden[:, here] = chars_v[:, here].astype(F32) + value

        col_tiles(one)

        def norm(here, i):
            unit, _ = normalized(hidden[here, :])
            normed_ffn[here, :] = (unit * vector(F_GAIN) + vector(F_BIAS)).astype(LOW)

        row_tiles(norm)

    def inner_block(n):
        def one(here, j):
            value = dot(normed_ffn[...], block(FIN + n, j)) + vector_tile(IN_BIAS + n, j)
            gelu, grad = gelu_parts(value)
            active[n, :, here] = gelu.astype(LOW)
            slope[n, :, here] = grad.astype(LOW)

        col_tiles(one)

    def by_place():
        i = lax.broadcasted_iota(jnp.int32, (WIN, WIN), 0)
        j = lax.broadcasted_iota(jnp.int32, (WIN, WIN), 1)
        return jnp.where(j == KERNEL * lax.rem(i, RUN) + i // RUN, 1.0, 0.0).astype(LOW)

    def layer_end():
        def one(here, j):
            value = hidden[:, here] + vector_tile(FO_BIAS, j)
            for n in range(BLOCKS):
                value = value + dot(active[n], block(FOUT + n, j))
            low_grad[:, here] = value.astype(LOW)

        col_tiles(one)
        order = by_place()

        def sort(here, w):
            moved = dot(order, low_grad[here, :]).astype(LOW)
            for k in range(KERNEL):
                stacked[k, pl.ds(at16(w * RUN), RUN), :] = moved[k * RUN : (k + 1) * RUN]

        row_tiles(sort)

    def note(row, value):
        vec_grads[row : row + 1, :] = value

    def note_more(row, value):
        vec_grads[row : row + 1, :] = vec_grads[row : row + 1, :] + value

    def convolve():
        loads[1].wait()
        value = jnp.zeros((mols, D), F32) + vector(C_BIAS)
        for k in range(KERNEL):
            value = value + dot(stacked[k], block(CONV + k))
        gelu, grad = gelu_parts(value)
        unit, scale = normalized(gelu)
        mol_v[...] = (unit * vector(D_GAIN) + vector(D_BIAS)).astype(LOW)
        wide = cot_v[...].astype(F32)
        note(D_GAIN, column_sum(wide * unit))
        note(D_BIAS, column_sum(wide))
        grad_conv = (norm_back(unit, scale, vector(D_GAIN), wide) * grad).astype(LOW)
        cot_v[...] = grad_conv
        note(C_BIAS, column_sum(grad_conv.astype(F32)))

    def convolve_back():
        for k in range(KERNEL):
            total[k * mols : (k + 1) * mols, :] = dot_turned(cot_v[...], block(CONV + k))

        for k in range(KERNEL):

            def one(here, j):
                value = dot_rows(stacked[k, :, here], cot_v[...])
                held[pl.ds(at128((CONV + k) * D + j * TILE), TILE), :] = value.astype(LOW)

            col_tiles(one)

        order = by_place()

        def sort(here, w):
            parts = [total[pl.ds(at16(k * mols + w * RUN), RUN), :] for k in range(KERNEL)]
            value = dot_rows(order, jnp.concatenate(parts, axis=0).astype(LOW))
            layer[here, :] = value
            low_grad[here, :] = value.astype(LOW)
            note_more(FO_BIAS, column_sum(value))

        row_tiles(sort)

    def weight_grad(n, left, right):
        def one(here, j):
            value = dot_rows(left[:, here], right[...])
            held[pl.ds(at128(n * D + j * TILE), TILE), :] = value.astype(LOW)

        col_tiles(one)

    def active_back(n):
        def one(here, j):
            value = dot_turned(
                low_grad[...], held[pl.ds(at128((FOUT + n) * D + j * TILE), TILE), :]
            )
            inner = (value * slope[n, :, here].astype(F32)).astype(LOW)
            slope[n, :, here] = inner
            vec_grads[IN_BIAS + n : IN_BIAS + n + 1, here] = column_sum(inner.astype(F32))

        col_tiles(one)
        weight_grad(FOUT + n, active.at[n], low_grad)

    def inner_sum():
        def one(here, j):
            value = jnp.zeros((rows, TILE), F32)
            for n in range(BLOCKS):
                value = value + dot_turned(
                    slope[n], held[pl.ds(at128((FIN + n) * D + j * TILE), TILE), :]
                )
            total[:, here] = value

        col_tiles(one)

    def hidden_back():
        def one(here, i):
            unit, scale = normalized(hidden[here, :])
            grad = total[here, :]
            note_more(F_GAIN, column_sum(grad * unit))
            note_more(F_BIAS, column_sum(grad))
            value = layer[here, :] + norm_back(unit, scale, vector(F_GAIN), grad)
            layer[here, :] = value
            low = value.astype(LOW)
            low_grad[here, :] = low
            note_more(O_BIAS, column_sum(low.astype(F32)))

        row_tiles(one)

    def context_back():
        def one(here, j):
            value = dot_turned(low_grad[...], held[pl.ds(at128(OUT * D + j * TILE), TILE), :])
            normed_ffn[:, here] = value.astype(LOW)

        col_tiles(one)
        weight_grad(OUT, context, low_grad)

    def attend_back(w):
        here = pl.ds(w * WIN, WIN)
        for p in range(PAIRS):
            cols = pl.ds(p * PAIR, PAIR)
            grad_out = two_heads(normed_ffn[here, cols])
            prob = probs[w, p]
            wide = prob.astype(F32)
            grad_prob = dot_turned(grad_out, projected[2, here, cols])
            inner = jnp.sum(wide * grad_prob, axis=-1, keepdims=True)
            grad_score = (wide * (grad_prob - inner)).astype(LOW)
            grad_value = dot_rows(prob, grad_out)
            grad_query = one_pair(dot(grad_score, projected[1, here, cols])) * scale_factor
            grad_key = (
                dot_rows(grad_score, two_heads(projected[0, here, cols])) * scale_factor
            )
            low_query, low_value = grad_query.astype(LOW), grad_value.astype(LOW)
            slope[0, here, cols] = low_query
            slope[1, here, cols] = grad_key.astype(LOW)
            slope[2, here, cols] = low_value
            for row, low in ((Q_BIAS, low_query), (V_BIAS, low_value)):
                vec_grads[row : row + 1, cols] = vec_grads[row : row + 1, cols] + column_sum(
                    low.astype(F32)
                )

    def project_sum():
        def one(here, j):
            value = jnp.zeros((rows, TILE), F32)
            for n in range(3):
                value = value + dot_turned(
                    slope[n], held[pl.ds(at128((QKV + n) * D + j * TILE), TILE), :]
                )
            total[:, here] = value

        col_tiles(one)

    def chars_back():
        def one(here, i):
            unit, scale = normalized(chars_v[here, :].astype(F32))
            grad = total[here, :]
            note_more(A_GAIN, column_sum(grad * unit))
            note_more(A_BIAS, column_sum(grad))
            value = layer[here, :] + norm_back(unit, scale, vector(A_GAIN), grad)
            context[here, :] = value.astype(LOW)

        row_tiles(one)

    def swap(i, whole, dst, count):
        keep = whole.at[:, pl.ds(at128(s * HALF), HALF)]
        give = whole.at[:, pl.ds(at128((1 - s) * HALF), HALF)]
        there = dst.at[pl.ds(at16(s * count), count)]
        stay = pltpu.make_async_copy(keep, there, io_sem.at[3 + i])
        go = remote(give, there, swap_send.at[i], swap_recv.at[i], near["x"])
        stay.start()
        go.start()
        return [stay, go]

    c = lax.rem(g, 2)
    y = g // 2
    mine, yours = 2 * y + c, 2 * (1 - y) + c
    z_half, w_half = lax.rem(r, 2), lax.rem(r // 2, 2)
    row_one = z_half * EIGHTH * 2
    row_two = row_one + w_half * EIGHTH

    to_core, to_all = Tally(g_send.at[0], held), Tally(g_send.at[1], held)
    from_border, from_middle = Tally(g_send.at[2], held), Tally(g_send.at[3], held)
    kept = Tally(g_send.at[4], held)
    done, done_border = Tally(g_send.at[5], held), Tally(g_send.at[6], held)

    def send(u, i, src, dst, way, sender=to_all):
        return Move(src, dst, sender, g_recv.at[SEM_AT[u] + i], near[way])

    def send_last(src, dst, way, sender=to_all, ends=done):
        move = Move(src, dst, sender, ends.sem, near[way])
        move.start()

    def cut(k, q, row, count, col=0, cols=D):
        return held.at[pl.ds(spot(k, q, row), count), pl.ds(at128(col), cols)]

    def final(k, row, count, col=None, cols=HALF):
        return shard_block(out, k, row, count, s * HALF if col is None else col, cols)

    def add_far(u, row, here):
        k = UNITS[u][0]
        count, cols = here.shape
        for i in range(extra):
            there = more_in.at[u, i, pl.ds(0, count), pl.ds(0, cols)]
            near_by = core_in.at[k, 0, pl.ds(row, count), pl.ds(0, cols)]
            copy = remote(here, there, more_send.at[u, i], more_recv.at[u, i], far[i])
            copy.start()
            copy.wait()
            copy = pltpu.make_async_copy(there, near_by, more_send.at[u, i])
            copy.start()
            copy.wait()
            add_to(here, near_by)

    def core_sum(u, i):
        k, row, count, _ = UNITS[u]
        there = core_in.at[k, i, pl.ds(row, count)]
        return send(u, 0, cut(k, 2 * i + 1 - c, row, count), there, "c", to_core)

    def wait_rows(u, i, count):
        here = held.at[pl.ds(0, count)]
        pltpu.make_async_copy(here, here, g_recv.at[SEM_AT[u] + i]).wait()

    def y_sum(u):
        k, row, count, _ = UNITS[u]
        return send(u, 1, cut(k, yours, row, count), y_in.at[k, pl.ds(row, count)], "y")

    def y_added(u):
        k, row, count, _ = UNITS[u]
        y_sum(u).wait_recv()
        add_to(cut(k, mine, row, count), y_in.at[k, pl.ds(row, count)])

    class Wide:
        def __init__(self, u):
            self.u = u
            self.k, self.row, self.count, _ = UNITS[u]
            self.here = pl.ds(self.row, self.count)
            self.total = m_in.at[self.k, self.here]

        def part(self, side):
            return cut(self.k, mine, self.row, self.count, side * HALF, HALF)

        def done_part(self):
            return final(self.k, self.row, self.count)

        def x_sum(self):
            return send(self.u, 2, self.part(1 - s), x_in.at[self.k, self.here], "x")

        def e_sum(self):
            return send(self.u, 3, self.part(s), e_in.at[self.k, self.here], "e", from_border)

        def m_sum(self):
            return send(self.u, 4, self.part(s), self.total, "m", from_middle)

        def e_back(self):
            return send(self.u, 3, self.total, self.done_part(), "e", from_middle)

        def step(self, n):
            if n == 1:
                y_sum(self.u).start()
            if n == 2:
                y_added(self.u)
                self.x_sum().start()
            if n == 3:
                self.x_sum().wait_recv()
                add_to(self.part(s), x_in.at[self.k, self.here])

                @pl.when(border)
                def _():
                    self.e_sum().start()

            if n == 4:

                @pl.when(middle)
                def _():
                    self.e_sum().wait_recv()
                    add_to(self.part(s), e_in.at[self.k, self.here])
                    self.m_sum().start()

            if n == 5:

                @pl.when(middle)
                def _():
                    self.m_sum().wait_recv()
                    add_to(self.total, self.part(s))
                    add_far(self.u, self.row, self.total)
                    kept.add(self.total)
                    pltpu.make_async_copy(self.total, self.done_part(), kept.sem).start()
                    self.e_back().start()
                    send_last(self.total, self.done_part(), "x", from_middle)

            if n == 6:

                @pl.when(border)
                def _():
                    self.e_back().wait_recv()
                    send_last(self.done_part(), self.done_part(), "x", from_border)

                done.add(self.total)

    class Line(Wide):
        def half(self, which):
            return self.row + which * (self.count // 2)

        def rows_of(self, which, side=None):
            col, cols = (0, D) if side is None else (side * HALF, HALF)
            return cut(self.k, mine, self.half(which), self.count // 2, col, cols)

        def done_rows(self, which):
            return final(self.k, self.half(which), self.count // 2, 0, D)

        def e_in(self, side):
            return (x_in, e_in)[side].at[self.k, self.here]

        def m_in(self, side):
            return m_in.at[self.k, pl.ds(self.row + side * (self.count // 2), self.count // 2)]

        def sum_line(self):
            return line_in.at[LINES.index(self.k), pl.ds(self.row // 2, self.count // 2)]

        def x_sum(self):
            return send(self.u, 4, self.rows_of(w_half), self.sum_line(), "x", from_middle)

        def m_back(self):
            return send(self.u, 5, self.sum_line(), self.done_rows(w_half), "m", from_middle)

        def step(self, n):
            if n == 1:
                y_sum(self.u).start()
            if n == 2:
                y_added(self.u)

                @pl.when(border)
                def _():
                    for side in range(2):
                        send(
                            self.u, 2, self.part(side), self.e_in(side), "e", from_border
                        ).start()

            if n == 3:

                @pl.when(middle)
                def _():
                    wait_rows(self.u, 2, self.count)
                    for side in range(2):
                        add_to(self.part(side), self.e_in(side))
                    for side in range(2):
                        src = self.rows_of(1 - w_half, side)
                        send(self.u, 3, src, self.m_in(side), "m", from_middle).start()

            if n == 4:

                @pl.when(middle)
                def _():
                    wait_rows(self.u, 3, self.count // 2)
                    for side in range(2):
                        add_to(self.rows_of(w_half, side), self.m_in(side))
                    self.x_sum().start()

            if n == 5:

                @pl.when(middle)
                def _():
                    self.x_sum().wait_recv()
                    add_to(self.sum_line(), self.rows_of(w_half))
                    add_far(self.u, self.row, self.sum_line())
                    kept.add(self.sum_line())
                    pltpu.make_async_copy(
                        self.sum_line(), self.done_rows(w_half), kept.sem
                    ).start()
                    self.m_back().start()
                    there = self.done_rows(w_half)
                    send_last(self.sum_line(), there, "e", from_middle, done_border)

            if n == 6:

                @pl.when(middle)
                def _():
                    self.m_back().wait_recv()
                    there = self.done_rows(1 - w_half)
                    send_last(there, there, "e", from_middle, done_border)

                for _ in range(2):
                    done_border.add(self.sum_line())

    class Deep:
        first_x = False

        def __init__(self, u):
            self.u = u
            self.k = UNITS[u][0]

        def one(self, i):
            src = cut(self.k, 2 * i + c, (1 - z_half) * EIGHTH * 2, 2 * EIGHTH)
            return send(self.u, 1, src, self.one_in(i), "e")

        def one_in(self, i):
            return y_in.at[self.k, pl.ds(i * 2 * EIGHTH, 2 * EIGHTH)]

        def two(self, i, side):
            row = row_one + (1 - w_half) * EIGHTH
            src = cut(self.k, 2 * i + c, row, EIGHTH, side * HALF, HALF)
            return send(self.u, 2, src, self.two_in(i, side), "w")

        def two_in(self, i, side):
            return x_in.at[self.k, pl.ds((2 * i + side) * EIGHTH, EIGHTH)]

        def x_sum(self, i):
            src = cut(self.k, 2 * i + c, row_two, EIGHTH, (1 - s) * HALF, HALF)
            return send(self.u, 3, src, self.x_in(i), "x")

        def x_in(self, i):
            return e_in.at[self.k, pl.ds(i * EIGHTH, EIGHTH)]

        def last(self):
            src = cut(self.k, yours, row_two, EIGHTH, s * HALF, HALF)
            return send(self.u, 4, src, self.x_in(2), "y")

        def piece(self):
            return cut(self.k, mine, row_two, EIGHTH, s * HALF, HALF)

        def own(self):
            there = final(self.k, row_two, EIGHTH)
            return pltpu.make_async_copy(self.piece(), there, g_recv.at[SEM_AT[self.u] + 7])

        def back(self, n):
            if n == 0:
                way = "x" if self.first_x else "w"
                return send(self.u, 5, self.piece(), final(self.k, row_two, EIGHTH), way)
            if self.first_x:
                here = final(self.k, row_two, EIGHTH, 0, D)
            else:
                here = final(self.k, row_one, 2 * EIGHTH)
            return send(self.u, 6, here, here, "w" if self.first_x else "e")

        def back_last(self):
            if self.first_x:
                here = final(self.k, row_one, 2 * EIGHTH, 0, D)
            else:
                here = final(self.k, 0, SHARD)
            send_last(here, here, "e" if self.first_x else "x")
            done.add(here)

        def step(self, n):
            if n == 1:
                for i in range(2):
                    self.one(i).start()
            if n == 2:
                wait_rows(self.u, 1, 4 * EIGHTH)
                for i in range(2):
                    add_to(cut(self.k, 2 * i + c, row_one, 2 * EIGHTH), self.one_in(i))
                    for side in range(2):
                        self.two(i, side).start()
            if n == 3:
                wait_rows(self.u, 2, 2 * EIGHTH)
                for i in range(2):
                    for side in range(2):
                        here = cut(self.k, 2 * i + c, row_two, EIGHTH, side * HALF, HALF)
                        add_to(here, self.two_in(i, side))
                    self.x_sum(i).start()
            if n == 4:
                wait_rows(self.u, 3, EIGHTH)
                for i in range(2):
                    here = cut(self.k, 2 * i + c, row_two, EIGHTH, s * HALF, HALF)
                    add_to(here, self.x_in(i))
                self.last().start()
            if n == 5:
                self.last().wait_recv()
                add_to(self.piece(), self.x_in(2))
                add_far(self.u, 0, self.piece())
                self.own().start()
                self.back(0).start()
            if n == 6:
                self.own().wait()
                self.back(0).wait_recv()
                self.back(1).start()
            if n == 7:
                self.back(1).wait_recv()
                self.back_last()

    class DeepX(Deep):
        first_x = True

    kinds = {"wide": Wide, "line": Line, "deep": Deep, "deep_x": DeepX}
    sums = [kinds[unit[3]](u) for u, unit in enumerate(UNITS)]

    def sum_step(u, n):
        if n == 0:
            for i in range(2):
                core_sum(u, i).start()
            return
        if n == 1:
            k, row, count, _ = UNITS[u]
            wait_rows(u, 0, 2 * count)
            for i in range(2):
                add_to(cut(k, 2 * i + c, row, count), core_in.at[k, i, pl.ds(row, count)])
        sums[u].step(n)

    def sums_done():
        to_core.wait()
        to_all.wait()
        done.wait()

        @pl.when(border)
        def _():
            from_border.wait()
            if LINES:
                done_border.wait()

        @pl.when(middle)
        def _():
            from_middle.wait()
            kept.wait()

    vec_steps = 6 + extra
    vec_moves = []

    def vec_step(n):
        if n == 0:
            top = vec_grads[...]
            high = top.astype(LOW)
            low = (top - high.astype(F32)).astype(LOW)
            for seg in range(GROUPS):
                spread = spread_matrix(seg)
                vec_segs[seg] = dot_turned(high, spread) + dot_turned(low, spread)
            for row, parts in SEGMENTS.items():
                for seg, (q, at) in enumerate(parts):
                    vecs[q, at : at + 1, :] = vec_segs[seg, row : row + 1, :]
            for i in range(2):
                copy = remote(
                    vecs.at[2 * i + 1 - c], vec_in.at[i], v_send.at[3 + i], v_recv.at[3 + i], near["c"]
                )
                copy.start()
                vec_moves.append(copy)
            return
        if n == 1:
            for i in range(2):
                vec_moves[i].wait()
                vecs[2 * i + c] = vecs[2 * i + c] + vec_in[i]
        else:
            vec_moves[-1].wait()
            vecs[mine] = vecs[mine] + vec_in[n]
        steps = [near["y"], near["x"], near["e"], near["w"]] + far
        if n <= len(steps):
            copy = remote(
                vecs.at[yours if n == 1 else mine],
                vec_in.at[1 + n],
                v_send.at[4 + n],
                v_recv.at[4 + n],
                steps[n - 1],
            )
            copy.start()
            vec_moves.append(copy)
        else:
            copy = pltpu.make_async_copy(vecs.at[mine], vec_out, io_sem.at[2])
            copy.start()
            copy.wait()

    vec_grads[...] = jnp.zeros_like(vec_grads)
    forward = [([], vectors_ready), ([], norm_first)]
    forward += [([QKV + n], functools.partial(project_block, n)) for n in range(3)]
    forward += [([], functools.partial(attend, w)) for w in range(windows)]
    forward += [([OUT], attend_out)]
    forward += [([FIN + n], functools.partial(inner_block, n)) for n in range(BLOCKS)]
    forward += [([8, 9, 10, 11], layer_end), ([12, 13, 14, 15], convolve)]
    for item in GATHER_PLAN:
        if item < 0:
            need, work = forward.pop(0)
            for k in need:
                weight_ready(k)
            work()
        else:
            gather_step(item // 10, item % 10)
    gather_done()

    moves = []

    def end_convolution():
        convolve_back()
        moves.extend(swap(0, mol_v, mols_out, mols))

    def end_chars():
        chars_back()
        moves.extend(swap(1, context, chars_out, rows))

    backward = [end_convolution]
    backward += [functools.partial(active_back, n) for n in range(BLOCKS)]
    backward += [inner_sum]
    backward += [
        functools.partial(weight_grad, FIN + n, normed_ffn, slope.at[n]) for n in range(BLOCKS)
    ]
    backward += [hidden_back, context_back]
    backward += [functools.partial(attend_back, w) for w in range(windows)]
    backward += [project_sum]
    backward += [functools.partial(weight_grad, QKV + n, normed, slope.at[n]) for n in range(3)]
    backward += [end_chars]
    backward += [functools.partial(vec_step, n) for n in range(vec_steps)]
    for item in PLAN:
        if item < 0:
            backward.pop(0)()
        else:
            sum_step(item // 10, item % 10)
    for work in backward:
        work()
    sums_done()
    for copy in moves:
        copy.wait()


def run(args, chars, extra):
    rows = chars.shape[0] // 2
    mols = rows // KERNEL
    anywhere = pl.BlockSpec(memory_space=pl.ANY)
    dma = pltpu.SemaphoreType.DMA
    vmem = pltpu.VMEM
    windows = rows // WIN
    return pl.pallas_call(
        functools.partial(program_kernel, rows, extra),
        name="layer_and_sums",
        out_shape=[
            jax.ShapeDtypeStruct((2 * mols, HALF), LOW),
            jax.ShapeDtypeStruct((2 * rows, HALF), LOW),
            jax.ShapeDtypeStruct(VEC, F32),
        ]
        + [jax.ShapeDtypeStruct(shape, LOW) for shape in SHARD_SHAPES]
        + [jax.ShapeDtypeStruct((len(UNITS), extra, SHARD, D), LOW)] * (extra > 0),
        in_specs=[anywhere, pl.BlockSpec(memory_space=vmem)] + [anywhere] * (len(args) - 2),
        out_specs=[anywhere] * (8 + (extra > 0)),
        scratch_shapes=[vmem((n * SHARD,), LOW) for n in VEC_COUNTS]
        + [
            vmem((COUNT * D, D), LOW),
            vmem((COUNT, 2, SHARD, D), LOW),
            vmem((COUNT, SHARD, D), LOW),
            vmem((COUNT, SHARD, HALF), LOW),
            vmem((COUNT, SHARD, HALF), LOW),
            vmem((COUNT, SHARD, HALF), LOW),
            vmem((max(len(LINES), 1), SHARD // 2, D), LOW),
            vmem(VEC, F32),
            vmem((GROUPS,) + VEC, F32),
            vmem((GROUPS,) + VEC, F32),
            vmem((VEC[0], D), F32),
            vmem((VEC[0], D), F32),
            vmem((7 + extra,) + VEC, F32),
            vmem((rows, D), LOW),
            vmem((mols, D), LOW),
            vmem((rows, D), LOW),
            vmem((3, rows, D), LOW),
            vmem((windows, PAIRS, 2 * WIN, WIN), LOW),
            vmem((rows, D), LOW),
            vmem((rows, D), F32),
            vmem((rows, D), LOW),
            vmem((BLOCKS, rows, D), LOW),
            vmem((BLOCKS, rows, D), LOW),
            vmem((rows, D), F32),
            vmem((KERNEL, mols, D), LOW),
            vmem((rows, D), LOW),
            vmem((rows, D), F32),
            vmem((mols, D), LOW),
            dma((1,)),
            dma((3, len(PIECES))),
            dma((COUNT,)),
            dma((7,)),
            dma((SEMS,)),
            dma((len(UNITS), extra) if extra else (1, 1)),
            dma((len(UNITS), extra) if extra else (1, 1)),
            dma((9 + extra,)),
            dma((9 + extra,)),
            dma((5 + len(VEC_COUNTS),)),
            dma((2,)),
            dma((2,)),
        ],
        compiler_params=pltpu.CompilerParams(
            collective_id=0, has_side_effects=True, vmem_limit_bytes=63 << 20
        ),
    )(*args)


def finish_kernel(mols, layer, vec, *refs):
    sums, (mols_out, layer_out) = refs[:5], refs[5:7]
    outs, vec_outs = refs[7:12], refs[12 : 12 + len(VEC_COUNTS)]
    low, wide, load, store, whole, mols_held, layer_held = refs[12 + len(VEC_COUNTS) :]
    through = [
        pltpu.make_async_copy(mols, mols_held, whole.at[0]),
        pltpu.make_async_copy(layer, layer_held, whole.at[1]),
    ]
    loads = [
        pltpu.make_async_copy(shard_block(sums, k, 0, SHARD), low.at[k], load.at[k])
        for k in range(COUNT)
    ]
    for copy in loads + through:
        copy.start()
    copies = [
        pltpu.make_async_copy(mols_held, mols_out, whole.at[0]),
        pltpu.make_async_copy(layer_held, layer_out, whole.at[1]),
    ]
    at = 0
    for ref, count in zip(vec_outs, VEC_COUNTS):
        for i in range(count):
            line = vec[at : at + 1, :][:, :SHARD].reshape(SHARD)
            ref[i * SHARD : (i + 1) * SHARD] = line
            at += 1
    for before, after in zip(through, copies):
        before.wait()
        after.start()
    for k in range(COUNT):
        loads[k].wait()
        wide[k] = low[k].astype(F32)
        copy = pltpu.make_async_copy(wide.at[k], shard_block(outs, k, 0, SHARD), store.at[k])
        copy.start()
        copies.append(copy)
    for copy in copies:
        copy.wait()


def finish(mols, layer, vec, sums):
    anywhere = pl.BlockSpec(memory_space=pltpu.HBM)
    inside = pl.BlockSpec(memory_space=pltpu.VMEM)
    shape = jax.ShapeDtypeStruct
    out = pl.pallas_call(
        finish_kernel,
        name="widen_sums",
        out_shape=[shape(mols.shape, LOW), shape(layer.shape, LOW)]
        + [shape(w.shape, F32) for w in sums]
        + [shape((n * SHARD,), F32) for n in VEC_COUNTS],
        in_specs=[anywhere, anywhere, inside] + [anywhere] * 5,
        out_specs=[anywhere] * 7 + [inside] * len(VEC_COUNTS),
        scratch_shapes=[
            pltpu.VMEM((COUNT, SHARD, D), LOW),
            pltpu.VMEM((COUNT, SHARD, D), F32),
            pltpu.SemaphoreType.DMA((COUNT,)),
            pltpu.SemaphoreType.DMA((COUNT,)),
            pltpu.SemaphoreType.DMA((2,)),
            pltpu.VMEM(mols.shape, LOW),
            pltpu.VMEM(layer.shape, LOW),
        ],
        compiler_params=pltpu.CompilerParams(vmem_limit_bytes=60 << 20),
    )(mols, layer, vec, *sums)
    return out[0], out[1], out[2:7], out[7:]


def body(
    chars,
    char_codes,
    mol_cotangent,
    attn_norm_gain,
    attn_norm_bias,
    qkv_weight,
    qv_bias,
    out_weight,
    out_bias,
    ffn_norm_gain,
    ffn_norm_bias,
    ffn_in_weight,
    ffn_in_bias,
    ffn_out_weight,
    ffn_out_bias,
    conv_weight,
    conv_bias,
    down_norm_gain,
    down_norm_bias,
):
    vectors = [
        attn_norm_gain,
        attn_norm_bias,
        qv_bias,
        out_bias,
        ffn_norm_gain,
        ffn_norm_bias,
        ffn_in_bias,
        ffn_out_bias,
        conv_bias,
        down_norm_gain,
        down_norm_bias,
    ]
    result = run(
        (
            chars,
            char_codes.reshape(-1, WIN),
            mol_cotangent,
            qkv_weight,
            out_weight,
            ffn_in_weight,
            ffn_out_weight,
            conv_weight,
            *vectors,
        ),
        chars,
        (lax.axis_size("replica") // RING).bit_length() - 1,
    )
    molecules, chars_grad, big, v = finish(*result[:3], result[3:8])
    t_qkv, t_out, t_in, t_ffo, t_conv = big
    return (
        molecules,
        chars_grad,
        v[0],
        v[1],
        t_qkv,
        v[2],
        t_out,
        v[3],
        v[4],
        v[5],
        t_in,
        v[6],
        t_ffo,
        v[7],
        t_conv,
        v[8],
        v[9],
        v[10],
    )


def solution(mesh):
    return jax.shard_map(
        body,
        mesh=mesh,
        in_specs=(
            P(("group", "replica"), None),
            P(("group", "replica")),
            P(("group", "replica"), None),
            P("group"),
            P("group"),
            P("group", None),
            P("group"),
            P("group", None),
            P("group"),
            P("group"),
            P("group"),
            P("group", None),
            P("group"),
            P("group", None),
            P("group"),
            P("group", None),
            P("group"),
            P("group"),
            P("group"),
        ),
        out_specs=(
            P(("group", "replica"), "section"),
            P(("group", "replica"), "section"),
            P("group"),
            P("group"),
            P("group", None),
            P("group"),
            P("group", None),
            P("group"),
            P("group"),
            P("group"),
            P("group", None),
            P("group"),
            P("group", None),
            P("group"),
            P("group", None),
            P("group"),
            P("group"),
            P("group"),
        ),
        check_vma=False,
    )
```

```python
import functools
import math

import jax
import jax.numpy as jnp
from jax import lax
from jax.experimental import pallas as pl
from jax.experimental.pallas import tpu as pltpu
from jax.sharding import PartitionSpec as P

D = 768
HEADS = 12
HEAD_DIM = 64
FF = 3072
WIN = 128
KERNEL = 4
GROUPS = 4
RING = 4
SHARD = D // GROUPS
THIRD = SHARD // 3
EIGHTH = SHARD // 4
HALF = D // 2
TILE = 768
PAIR = 2 * HEAD_DIM
PAIRS = HEADS // 2
RUN = WIN // KERNEL
BLOCKS = FF // D
VEC = (16, 256)
VEC_COUNTS = (1, 1, 2, 1, 1, 1, 4, 1, 1, 1, 1)
SCRATCH = 28
norm_eps = 1e-06
mask_value = -10000.0
MESH = pl.DeviceIdType.MESH
F32 = jnp.float32
LOW = jnp.bfloat16

CHUNKS = (
    [(0, "col", j) for j in range(3)]
    + [(1, "col", 0)]
    + [(2, "col", j) for j in range(4)]
    + [(3, "row", j) for j in range(4)]
    + [(4, "row", j) for j in range(4)]
)
COUNT = len(CHUNKS)
QKV, OUT, FIN, FOUT, CONV = BASES = (0, 3, 4, 8, 12)
SHARD_SHAPES = [(SHARD, 3 * D), (SHARD, D), (SHARD, FF), (FF // GROUPS, D), (D, D)]

A_GAIN, A_BIAS, Q_BIAS, V_BIAS, O_BIAS, F_GAIN, F_BIAS = range(7)
IN_BIAS, FO_BIAS, C_BIAS, D_GAIN, D_BIAS = 7, 11, 12, 13, 14


def segments():
    table = {}
    for row, at in zip((A_GAIN, A_BIAS, O_BIAS, F_GAIN, F_BIAS), (0, 1, 4, 5, 6)):
        table[row] = [(q, at) for q in range(GROUPS)]
    table[Q_BIAS] = [(0, 2), (0, 3), (1, 2), (1, 3)]
    table[V_BIAS] = [(2, 2), (2, 3), (3, 2), (3, 3)]
    for n in range(BLOCKS):
        table[IN_BIAS + n] = [(n, 7 + i) for i in range(4)]
    for row, at in zip((FO_BIAS, C_BIAS, D_GAIN, D_BIAS), (11, 12, 13, 14)):
        table[row] = [(q, at) for q in range(GROUPS)]
    return table


SEGMENTS = segments()

PIECES = [
    (0, 0, 1), (1, 0, 1), (2, 0, 1), (3, 0, 1), (4, 0, 1), (5, 0, 1), (6, 0, 1), (7, 0, 1),
    (8, 0, 1), (9, 0, 1), (10, 0, 1), (11, 0, 1), (12, 0, 1), (13, 0, 1), (14, 0, 2), (14,
    1, 2), (15, 0, 2), (15, 1, 2),
]
GATHER_PLAN = [
    -1, -1, 0, 10, 1, 20, 11, 30, 2, 21, 40, -1, 12, 31, 50, 22, 41, 60, -1, -1, 32, 51, 70,
    -1, -1, 42, 61, 80, -1, 52, 71, 90, -1, -1, 62, 81, 100, -1, 72, 91, 110, -1, 82, 101,
    120, -1, 130, 92, 111, 140, -1, 150, 102, 121, 160, 170, 112, 131, 141, -1, 122, 132,
    151, 142, 161, 171, 152, 162, 172, -1,
]

UNITS = [
    (12, 0, 192, "wide"),
    (13, 0, 192, "deep_x"),
    (14, 0, 192, "cross"),
    (15, 0, 96, "wide"),
    (15, 96, 96, "wide"),
    (8, 0, 48, "wide"),
    (8, 48, 48, "wide"),
    (8, 96, 48, "wide"),
    (8, 144, 48, "wide"),
    (9, 0, 96, "wide"),
    (9, 96, 96, "wide"),
    (10, 0, 192, "deep_x"),
    (11, 0, 192, "cross"),
    (4, 0, 192, "line"),
    (5, 0, 192, "cross"),
    (6, 0, 96, "wide"),
    (6, 96, 96, "wide"),
    (7, 0, 64, "line"),
    (7, 64, 64, "line"),
    (7, 128, 64, "line"),
    (3, 0, 96, "wide"),
    (3, 96, 96, "wide"),
    (0, 0, 64, "line"),
    (0, 64, 64, "line"),
    (0, 128, 64, "line"),
    (1, 0, 64, "wide"),
    (1, 64, 64, "wide"),
    (1, 128, 64, "wide"),
    (2, 0, 48, "wide"),
    (2, 48, 48, "wide"),
    (2, 96, 48, "wide"),
    (2, 144, 48, "wide"),
]

SEM_COUNT = {"wide": 5, "cross": 5, "line": 6, "deep": 8, "deep_x": 8}
SEM_AT = [sum(SEM_COUNT[unit[3]] for unit in UNITS[:u]) for u in range(len(UNITS))]
SEMS = sum(SEM_COUNT[unit[3]] for unit in UNITS)
LINES = sorted({unit[0] for unit in UNITS if unit[3] == "line"})
PLAN = [
    -1, 0, 10, -1, 1, 20, 11, 30, 40, -1, 21, 31, 41, -1, -1, -1, 2, 12, -1, 22, 120, 32,
    90, 100, 50, 42, 60, 70, 80, 110, 121, 91, 3, 101, 51, 61, 71, 81, 33, 111, 23, 13, 43,
    -1, 92, 4, -1, 130, 34, -1, 140, 102, -1, 122, 52, 131, 5, 141, 150, 160, 62, 14, 35,
    93, -1, 72, 170, 180, 190, 151, 82, 161, 103, 171, 181, 191, 53, 6, 24, 112, 36, -1,
    123, 94, 44, -1, 25, 104, 54, 200, 210, -1, 132, 63, 201, 211, 142, 15, -1, 152, 73, 83,
    124, 113, -1, 26, 162, 95, 45, 16, -1, 172, 153, 133, 105, 55, 64, 96, 182, 114, 74, -1,
    192, 125, 84, 163, 46, -1, 173, 202, 17, 220, 230, 106, 240, 154, -1, 134, 56, 250, 212,
    183, 65, 75, 260, 270, 251, 126, 85, 221, 193, 261, 174, 271, 203, 143, 231, 115, 164,
    155, 241, -1, 280, 290, 300, 310, 184, 194, 135, 281, 291, 301, 311, 252, 66, 76, 86,
    213, 156, 165, 204, 262, 222, -1, 175, 272, 136, 116, 144, 214, -1, 166, 205, 232, 185,
    176, 223, 195, -1, 242, 253, 282, 233, 263, 292, 117, 243, 302, 206, 254, 312, 145, -1,
    264, 215, 186, 224, 196, 273, 234, 244, 146, 255, 283, 274, 293, 265, 216, 303, 313,
    284, 275, 294, 304, 256, 314, 285, 266, -1, 295, 276, 305, 315, 286, -1, 225, 296, 235,
    306, 316, 245, -1, 226, 236, 246,
]


def at16(value):
    return pl.multiple_of(value, 16)


def at128(value):
    return pl.multiple_of(value, 128)


def spot(chunk, shard, first=0):
    mat, kind, j = CHUNKS[chunk]
    if kind == "col":
        return at16((BASES[mat] + j) * D + shard * SHARD + first)
    return at16((BASES[mat] + shard) * D + j * SHARD + first)


def shard_block(refs, chunk, first, rows, col=0, cols=D):
    mat, kind, j = CHUNKS[chunk]
    if kind == "col":
        return refs[mat].at[pl.ds(at16(first), rows), pl.ds(at128(j * D + col), cols)]
    return refs[mat].at[pl.ds(at16(j * SHARD + first), rows), pl.ds(at128(col), cols)]


def remote(src, dst, send, recv, target):
    return pltpu.make_async_remote_copy(
        src_ref=src,
        dst_ref=dst,
        send_sem=send,
        recv_sem=recv,
        device_id=target,
        device_id_type=MESH,
    )


class Tally:
    def __init__(self, sem, yard):
        self.sem, self.yard, self.size = sem, yard, 0

    def add(self, ref):
        self.size += math.prod(ref.shape)

    def wait(self):
        here = self.yard.at[pl.ds(0, self.size // D)]
        pltpu.make_async_copy(here, here, self.sem).wait()
        self.size = 0


class Move:
    def __init__(self, src, dst, sent, recv, target):
        self.src, self.dst, self.sent = src, dst, sent
        self.copy = remote(src, dst, sent.sem, recv, target)

    def start(self):
        self.sent.add(self.src)
        self.copy.start()

    def wait_recv(self):
        self.copy.wait_recv()


def add_to(dst, src):
    @pl.loop(0, dst.shape[0] // 16)
    def _(i):
        here = pl.ds(at16(i * 16), 16)
        dst[here, :] = dst[here, :] + src[here, :]


def dot(left, right):
    return jnp.dot(left, right, preferred_element_type=F32)


def dot_rows(left, right):
    return lax.dot_general(left, right, (((0,), (0,)), ((), ())), preferred_element_type=F32)


def dot_turned(left, right):
    return lax.dot_general(left, right, (((1,), (1,)), ((), ())), preferred_element_type=F32)


def normalized(values):
    center = values - jnp.mean(values, axis=-1, keepdims=True)
    scale = lax.rsqrt(jnp.mean(center * center, axis=-1, keepdims=True) + norm_eps)
    return center * scale, scale


def norm_back(unit, scale, gain, grad):
    grad_unit = grad * gain
    mean_grad = jnp.mean(grad_unit, axis=-1, keepdims=True)
    mean_both = jnp.mean(grad_unit * unit, axis=-1, keepdims=True)
    return scale * (grad_unit - mean_grad - unit * mean_both)


def gelu_parts(values):
    half = 0.5 * lax.erf(values * (0.5**0.5)) + 0.5
    bell = jnp.exp(-0.5 * values * values) * 0.3989422804014327
    return values * half, half + values * bell


def column_sum(values):
    return jnp.sum(values, axis=0, keepdims=True)


def program_kernel(rows, extra, *refs):
    count = len(VEC_COUNTS)
    (chars, codes, cotangent) = refs[:3]
    shards = refs[3:8]
    vectors = refs[8 : 8 + count]
    mols_out, chars_out, vec_out = refs[8 + count : 11 + count]
    out = refs[11 + count : 16 + count]
    more_in = refs[16 + count] if extra else None
    refs = refs[16 + count + (extra > 0) :]
    flat, refs = refs[:count], refs[count:]
    (
        held,
        core_in,
        y_in,
        x_in,
        e_in,
        m_in,
        line_in,
        vec,
        vecs,
        vec_segs,
        rows_f32,
        vec_grads,
        vec_in,
        chars_v,
        cot_v,
        normed,
        projected,
        probs,
        context,
        hidden,
        normed_ffn,
        slope,
        active,
        layer,
        stacked,
        low_grad,
        total,
        mol_v,
    ) = refs[:SCRATCH]
    (
        w_send,
        w_recv,
        c_recv,
        g_send,
        g_recv,
        more_send,
        more_recv,
        v_send,
        v_recv,
        io_sem,
        swap_send,
        swap_recv,
    ) = refs[SCRATCH:]
    windows = rows // WIN
    mols = rows // KERNEL
    s, g, r = lax.axis_index("section"), lax.axis_index("group"), lax.axis_index("replica")
    near = {
        "c": (s, g ^ 1, r),
        "y": (s, g ^ 2, r),
        "x": (1 - s, g, r),
        "e": (s, g, r ^ 1),
        "m": (s, g, r ^ 3),
        "d": (s, g ^ 3, r),
        "w": (s, g, r ^ 2),
    }
    far = [(s, g, r ^ (RING << i)) for i in range(extra)]
    place = lax.rem(r, RING)
    even = lax.rem(r, 2) == 0
    middle = jnp.logical_or(place == 1, place == 2)
    border = jnp.logical_not(middle)

    barrier = pltpu.get_barrier_semaphore()
    greeted = list(near.values()) + far
    for target in greeted:
        pl.semaphore_signal(barrier, inc=1, device_id=target, device_id_type=MESH)

    flat_copies = [
        pltpu.make_async_copy(src, dst, io_sem.at[5 + i])
        for i, (src, dst) in enumerate(zip(vectors, flat))
    ]
    for copy in flat_copies:
        copy.start()
    vec[...] = jnp.zeros_like(vec)
    vec_grads[...] = jnp.zeros_like(vec_grads)
    vec_segs[...] = jnp.zeros_like(vec_segs)
    at = 0
    for copy, values, rows_held in zip(flat_copies, flat, VEC_COUNTS):
        copy.wait()
        wide = values[...].astype(F32)
        for i in range(rows_held):
            line = wide[i * SHARD : (i + 1) * SHARD].reshape(1, SHARD)
            vec[at : at + 1, pl.ds(0, SHARD)] = line
            at += 1
    pl.semaphore_wait(barrier, len(greeted))

    y_third = jnp.where(even, s, 2)
    z_third = jnp.where(even, 2, s)
    x_third = 1 - s
    other = g ^ 2

    own_vec = pltpu.make_async_copy(vec, vecs.at[g], io_sem.at[2])
    vec_copies = [
        remote(vec, vecs.at[g], v_send.at[i], v_recv.at[i], near[way])
        for i, way in enumerate("cyd")
    ]
    for copy in vec_copies + [own_vec]:
        copy.start()

    def piece_of(u, third):
        k, part, parts = PIECES[u]
        return k, third * THIRD + part * (THIRD // parts), THIRD // parts

    sent = Tally(w_send.at[0], held)

    def hop(i, u, third, way):
        k, first, count = piece_of(u, third)
        here = held.at[pl.ds(spot(k, other, first), count)]
        return Move(here, here, sent, w_recv.at[i, u], near[way])

    def first_hop(u):
        k, first, count = piece_of(u, y_third)
        src = shard_block(shards, k, first, count)
        there = held.at[pl.ds(spot(k, g, first), count)]
        return Move(src, there, sent, w_recv.at[0, u], near["y"])

    def core_own(k):
        src = shard_block(shards, k, 0, SHARD)
        there = held.at[pl.ds(spot(k, g), SHARD)]
        return Move(src, there, sent, c_recv.at[k], near["c"])

    def core_hop(u, third):
        k, first, count = piece_of(u, third)
        here = held.at[pl.ds(spot(k, other, first), count)]
        Move(here, here, sent, c_recv.at[k], near["c"]).start()

    for u in range(len(PIECES)):
        first_hop(u).start()
    loads = [
        pltpu.make_async_copy(chars.at[pl.ds(at16(s * rows), rows)], chars_v, io_sem.at[0]),
        pltpu.make_async_copy(cotangent.at[pl.ds(at16(s * mols), mols)], cot_v, io_sem.at[1]),
    ]
    for copy in loads:
        copy.start()
    for k in range(COUNT):
        own_block = held.at[pl.ds(spot(k, g), SHARD)]
        pltpu.make_async_copy(shard_block(shards, k, 0, SHARD), own_block, c_recv.at[k]).start()
        core_own(k).start()

    def gather_step(u, n):
        if n == 0:
            hop(0, u, y_third, "y").wait_recv()
            hop(2, u, y_third, "e").start()

            @pl.when(even)
            def _():
                hop(1, u, s, "x").start()

            core_hop(u, y_third)
        if n == 1:
            hop(2, u, z_third, "e").wait_recv()

            @pl.when(jnp.logical_not(even))
            def _():
                hop(1, u, s, "x").copy.start()

            core_hop(u, z_third)
        if n == 2:
            hop(1, u, x_third, "x").wait_recv()
            core_hop(u, x_third)

    def weight_ready(k):
        here = held.at[pl.ds(0, 3 * SHARD)]
        pltpu.make_async_copy(here, here, c_recv.at[k]).wait()

    def gather_done():
        sent.wait()

    def spread_matrix(seg):
        i = lax.broadcasted_iota(jnp.int32, (VEC[1], D), 0)
        j = lax.broadcasted_iota(jnp.int32, (VEC[1], D), 1)
        hit = jnp.logical_and(j == i + seg * SHARD, i < SHARD)
        return jnp.where(hit, 1.0, 0.0).astype(LOW)

    def vectors_ready():
        own_vec.wait()
        for copy in vec_copies:
            copy.wait()
        for row, parts in SEGMENTS.items():
            for seg, (q, at) in enumerate(parts):
                vec_segs[seg, row : row + 1, :] = vecs[q, at : at + 1, :]
        full = jnp.zeros((VEC[0], D), F32)
        for seg in range(GROUPS):
            full = full + dot(vec_segs[seg].astype(LOW), spread_matrix(seg))
        rows_f32[...] = full

    def vector(row):
        return rows_f32[row : row + 1, :]

    def vector_tile(row, j):
        return rows_f32[row : row + 1, pl.ds(at128(j * TILE), TILE)]

    def block(n, j=None):
        start = n * D
        if not isinstance(n, int):
            start = at16(start)
        if j is None:
            return held[pl.ds(start, D), :]
        return held[pl.ds(start, D), pl.ds(at128(j * TILE), TILE)]

    def row_tiles(body):
        @pl.loop(0, rows // WIN)
        def _(i):
            body(pl.ds(at128(i * WIN), WIN), i)

    def col_tiles(body):
        @pl.loop(0, D // TILE)
        def _(j):
            body(pl.ds(at128(j * TILE), TILE), j)

    def norm_first():
        loads[0].wait()

        def one(here, i):
            unit, _ = normalized(chars_v[here, :].astype(F32))
            normed[here, :] = (unit * vector(A_GAIN) + vector(A_BIAS)).astype(LOW)

        row_tiles(one)

    def project_block(n):
        def one(here, j):
            value = dot(normed[...], block(QKV + n, j))
            if n == 0:
                value = value + vector_tile(Q_BIAS, j)
            if n == 2:
                value = value + vector_tile(V_BIAS, j)
            projected[n, :, here] = value.astype(LOW)

        col_tiles(one)

    def key_bias(w):
        code = codes[pl.ds(s * windows + w, 1), :]
        return jnp.where(code != 0, 0.0, mask_value).astype(F32)

    def lanes():
        return lax.broadcasted_iota(jnp.int32, (WIN, PAIR), 1) < HEAD_DIM

    def two_heads(values):
        first = lanes()
        zero = jnp.zeros_like(values)
        return jnp.concatenate(
            [jnp.where(first, values, zero), jnp.where(first, zero, values)], axis=0
        )

    def one_pair(values):
        return jnp.where(lanes(), values[:WIN], values[WIN:])

    scale_factor = HEAD_DIM ** (-0.5)

    def attend(w):
        here = pl.ds(w * WIN, WIN)
        bias = key_bias(w)
        for p in range(PAIRS):
            cols = pl.ds(p * PAIR, PAIR)
            queries = two_heads(projected[0, here, cols])
            scores = dot_turned(queries, projected[1, here, cols]) * scale_factor + bias
            top = jnp.max(scores, axis=-1, keepdims=True)
            weight = jnp.exp(scores - top)
            weight = weight / jnp.sum(weight, axis=-1, keepdims=True)
            prob = weight.astype(LOW)
            probs[w, p] = prob
            context[here, cols] = one_pair(dot(prob, projected[2, here, cols])).astype(LOW)

    def attend_out():
        def one(here, j):
            value = dot(context[...], block(OUT, j)) + vector_tile(O_BIAS, j)
            hidden[:, here] = chars_v[:, here].astype(F32) + value

        col_tiles(one)

        def norm(here, i):
            unit, _ = normalized(hidden[here, :])
            normed_ffn[here, :] = (unit * vector(F_GAIN) + vector(F_BIAS)).astype(LOW)

        row_tiles(norm)

    def inner_block(n):
        def one(here, j):
            value = dot(normed_ffn[...], block(FIN + n, j)) + vector_tile(IN_BIAS + n, j)
            gelu, grad = gelu_parts(value)
            active[n, :, here] = gelu.astype(LOW)
            slope[n, :, here] = grad.astype(LOW)

        col_tiles(one)

    def by_place():
        i = lax.broadcasted_iota(jnp.int32, (WIN, WIN), 0)
        j = lax.broadcasted_iota(jnp.int32, (WIN, WIN), 1)
        return jnp.where(j == KERNEL * lax.rem(i, RUN) + i // RUN, 1.0, 0.0).astype(LOW)

    def layer_end():
        def one(here, j):
            value = hidden[:, here] + vector_tile(FO_BIAS, j)
            for n in range(BLOCKS):
                value = value + dot(active[n], block(FOUT + n, j))
            low_grad[:, here] = value.astype(LOW)

        col_tiles(one)
        order = by_place()

        def sort(here, w):
            moved = dot(order, low_grad[here, :]).astype(LOW)
            for k in range(KERNEL):
                stacked[k, pl.ds(at16(w * RUN), RUN), :] = moved[k * RUN : (k + 1) * RUN]

        row_tiles(sort)

    def note(row, value):
        vec_grads[row : row + 1, :] = value

    def note_more(row, value):
        vec_grads[row : row + 1, :] = vec_grads[row : row + 1, :] + value

    def convolve():
        loads[1].wait()
        value = jnp.zeros((mols, D), F32) + vector(C_BIAS)
        for k in range(KERNEL):
            value = value + dot(stacked[k], block(CONV + k))
        gelu, grad = gelu_parts(value)
        unit, scale = normalized(gelu)
        mol_v[...] = (unit * vector(D_GAIN) + vector(D_BIAS)).astype(LOW)
        wide = cot_v[...].astype(F32)
        note(D_GAIN, column_sum(wide * unit))
        note(D_BIAS, column_sum(wide))
        grad_conv = (norm_back(unit, scale, vector(D_GAIN), wide) * grad).astype(LOW)
        cot_v[...] = grad_conv
        note(C_BIAS, column_sum(grad_conv.astype(F32)))

    def convolve_back(side):
        cols = pl.ds(side * HALF, HALF)
        for k in range(KERNEL):
            here = pl.ds((CONV + k) * D + side * HALF, HALF)
            total[k * mols : (k + 1) * mols, cols] = dot_turned(cot_v[...], held[here, :])
        for k in range(KERNEL):
            here = pl.ds((CONV + k) * D + side * HALF, HALF)
            held[here, :] = dot_rows(stacked[k, :, cols], cot_v[...]).astype(LOW)

    def layer_back():
        order = by_place()

        def sort(here, w):
            parts = [total[pl.ds(at16(k * mols + w * RUN), RUN), :] for k in range(KERNEL)]
            value = dot_rows(order, jnp.concatenate(parts, axis=0).astype(LOW))
            layer[here, :] = value
            low_grad[here, :] = value.astype(LOW)
            note_more(FO_BIAS, column_sum(value))

        row_tiles(sort)
        moves.extend(swap(0, mol_v, mols_out, mols))

    def weight_grad(n, left, right):
        def one(here, j):
            value = dot_rows(left[:, here], right[...])
            held[pl.ds(at128(n * D + j * TILE), TILE), :] = value.astype(LOW)

        col_tiles(one)

    def active_back(n):
        def one(here, j):
            value = dot_turned(
                low_grad[...], held[pl.ds(at128((FOUT + n) * D + j * TILE), TILE), :]
            )
            inner = (value * slope[n, :, here].astype(F32)).astype(LOW)
            slope[n, :, here] = inner
            vec_grads[IN_BIAS + n : IN_BIAS + n + 1, here] = column_sum(inner.astype(F32))

        col_tiles(one)
        weight_grad(FOUT + n, active.at[n], low_grad)

    def inner_sum():
        def one(here, j):
            value = jnp.zeros((rows, TILE), F32)
            for n in range(BLOCKS):
                value = value + dot_turned(
                    slope[n], held[pl.ds(at128((FIN + n) * D + j * TILE), TILE), :]
                )
            total[:, here] = value

        col_tiles(one)

    def hidden_back():
        def one(here, i):
            unit, scale = normalized(hidden[here, :])
            grad = total[here, :]
            note_more(F_GAIN, column_sum(grad * unit))
            note_more(F_BIAS, column_sum(grad))
            value = layer[here, :] + norm_back(unit, scale, vector(F_GAIN), grad)
            layer[here, :] = value
            low = value.astype(LOW)
            low_grad[here, :] = low
            note_more(O_BIAS, column_sum(low.astype(F32)))

        row_tiles(one)

    def context_back():
        def one(here, j):
            value = dot_turned(low_grad[...], held[pl.ds(at128(OUT * D + j * TILE), TILE), :])
            normed_ffn[:, here] = value.astype(LOW)

        col_tiles(one)
        weight_grad(OUT, context, low_grad)

    def attend_back(w):
        here = pl.ds(w * WIN, WIN)
        for p in range(PAIRS):
            cols = pl.ds(p * PAIR, PAIR)
            grad_out = two_heads(normed_ffn[here, cols])
            prob = probs[w, p]
            wide = prob.astype(F32)
            grad_prob = dot_turned(grad_out, projected[2, here, cols])
            inner = jnp.sum(wide * grad_prob, axis=-1, keepdims=True)
            grad_score = (wide * (grad_prob - inner)).astype(LOW)
            grad_value = dot_rows(prob, grad_out)
            grad_query = one_pair(dot(grad_score, projected[1, here, cols])) * scale_factor
            grad_key = (
                dot_rows(grad_score, two_heads(projected[0, here, cols])) * scale_factor
            )
            low_query, low_value = grad_query.astype(LOW), grad_value.astype(LOW)
            slope[0, here, cols] = low_query
            slope[1, here, cols] = grad_key.astype(LOW)
            slope[2, here, cols] = low_value
            for row, low in ((Q_BIAS, low_query), (V_BIAS, low_value)):
                vec_grads[row : row + 1, cols] = vec_grads[row : row + 1, cols] + column_sum(
                    low.astype(F32)
                )

    def project_sum():
        def one(here, j):
            value = jnp.zeros((rows, TILE), F32)
            for n in range(3):
                value = value + dot_turned(
                    slope[n], held[pl.ds(at128((QKV + n) * D + j * TILE), TILE), :]
                )
            total[:, here] = value

        col_tiles(one)

    def chars_back():
        def one(here, i):
            unit, scale = normalized(chars_v[here, :].astype(F32))
            grad = total[here, :]
            note_more(A_GAIN, column_sum(grad * unit))
            note_more(A_BIAS, column_sum(grad))
            value = layer[here, :] + norm_back(unit, scale, vector(A_GAIN), grad)
            context[here, :] = value.astype(LOW)

        row_tiles(one)

    def swap(i, whole, dst, count):
        keep = whole.at[:, pl.ds(at128(s * HALF), HALF)]
        give = whole.at[:, pl.ds(at128((1 - s) * HALF), HALF)]
        there = dst.at[pl.ds(at16(s * count), count)]
        stay = pltpu.make_async_copy(keep, there, io_sem.at[3 + i])
        go = remote(give, there, swap_send.at[i], swap_recv.at[i], near["x"])
        stay.start()
        go.start()
        return [stay, go]

    c = lax.rem(g, 2)
    y = g // 2
    mine, yours = 2 * y + c, 2 * (1 - y) + c
    z_half, w_half = lax.rem(r, 2), lax.rem(r // 2, 2)
    row_one = z_half * EIGHTH * 2
    row_two = row_one + w_half * EIGHTH

    to_core, to_all = Tally(g_send.at[0], held), Tally(g_send.at[1], held)
    from_border, from_middle = Tally(g_send.at[2], held), Tally(g_send.at[3], held)
    kept = Tally(g_send.at[4], held)
    done, done_border = Tally(g_send.at[5], held), Tally(g_send.at[6], held)

    def send(u, i, src, dst, way, sender=to_all):
        return Move(src, dst, sender, g_recv.at[SEM_AT[u] + i], near[way])

    def send_last(src, dst, way, sender=to_all, ends=done):
        move = Move(src, dst, sender, ends.sem, near[way])
        move.start()

    def cut(k, q, row, count, col=0, cols=D):
        return held.at[pl.ds(spot(k, q, row), count), pl.ds(at128(col), cols)]

    def final(k, row, count, col=None, cols=HALF):
        return shard_block(out, k, row, count, s * HALF if col is None else col, cols)

    def add_far(u, row, here):
        k = UNITS[u][0]
        count, cols = here.shape
        for i in range(extra):
            there = more_in.at[u, i, pl.ds(0, count), pl.ds(0, cols)]
            near_by = core_in.at[k, 0, pl.ds(row, count), pl.ds(0, cols)]
            copy = remote(here, there, more_send.at[u, i], more_recv.at[u, i], far[i])
            copy.start()
            copy.wait()
            copy = pltpu.make_async_copy(there, near_by, more_send.at[u, i])
            copy.start()
            copy.wait()
            add_to(here, near_by)

    def core_sum(u, i):
        k, row, count, _ = UNITS[u]
        there = core_in.at[k, i, pl.ds(row, count)]
        return send(u, 0, cut(k, 2 * i + 1 - c, row, count), there, "c", to_core)

    def wait_rows(u, i, count):
        here = held.at[pl.ds(0, count)]
        pltpu.make_async_copy(here, here, g_recv.at[SEM_AT[u] + i]).wait()

    def y_sum(u):
        k, row, count, _ = UNITS[u]
        return send(u, 1, cut(k, yours, row, count), y_in.at[k, pl.ds(row, count)], "y")

    def y_added(u):
        k, row, count, _ = UNITS[u]
        y_sum(u).wait_recv()
        add_to(cut(k, mine, row, count), y_in.at[k, pl.ds(row, count)])

    class Wide:
        def __init__(self, u):
            self.u = u
            self.k, self.row, self.count, _ = UNITS[u]
            self.here = pl.ds(self.row, self.count)
            self.total = m_in.at[self.k, self.here]

        def part(self, side):
            return cut(self.k, mine, self.row, self.count, side * HALF, HALF)

        def done_part(self):
            return final(self.k, self.row, self.count)

        def x_sum(self):
            return send(self.u, 2, self.part(1 - s), x_in.at[self.k, self.here], "x")

        def e_sum(self):
            return send(self.u, 3, self.part(s), e_in.at[self.k, self.here], "e", from_border)

        def m_sum(self):
            return send(self.u, 4, self.part(s), self.total, "m", from_middle)

        def e_back(self):
            return send(self.u, 3, self.total, self.done_part(), "e", from_middle)

        def step(self, n):
            if n == 1:
                y_sum(self.u).start()
            if n == 2:
                y_added(self.u)
                self.x_sum().start()
            if n == 3:
                self.x_sum().wait_recv()
                add_to(self.part(s), x_in.at[self.k, self.here])

                @pl.when(border)
                def _():
                    self.e_sum().start()

            if n == 4:

                @pl.when(middle)
                def _():
                    self.e_sum().wait_recv()
                    add_to(self.part(s), e_in.at[self.k, self.here])
                    self.m_sum().start()

            if n == 5:

                @pl.when(middle)
                def _():
                    self.m_sum().wait_recv()
                    add_to(self.total, self.part(s))
                    add_far(self.u, self.row, self.total)
                    kept.add(self.total)
                    pltpu.make_async_copy(self.total, self.done_part(), kept.sem).start()
                    self.e_back().start()
                    send_last(self.total, self.done_part(), "x", from_middle)

            if n == 6:

                @pl.when(border)
                def _():
                    self.e_back().wait_recv()
                    send_last(self.done_part(), self.done_part(), "x", from_border)

                done.add(self.total)

    class Cross(Wide):
        def both_in(self, i):
            return y_in.at[self.k, self.here, pl.ds(i * HALF, HALF)]

        def both_part(self, i, side):
            return cut(self.k, 2 * i + c, self.row, self.count, side * HALF, HALF)

        def y_sum(self):
            src = cut(self.k, yours, self.row, self.count, s * HALF, HALF)
            return send(self.u, 2, src, x_in.at[self.k, self.here], "y")

        def step(self, n):
            if n == 1:
                for i in range(2):
                    send(self.u, 1, self.both_part(i, 1 - s), self.both_in(i), "x").start()
            elif n == 2:
                wait_rows(self.u, 1, self.count)
                for i in range(2):
                    add_to(self.both_part(i, s), self.both_in(i))
                self.y_sum().start()
            elif n == 3:
                self.y_sum().wait_recv()
                add_to(self.part(s), x_in.at[self.k, self.here])

                @pl.when(border)
                def _():
                    self.e_sum().start()

            else:
                super().step(n)

    class Line(Wide):
        def half(self, which):
            return self.row + which * (self.count // 2)

        def rows_of(self, which, side=None):
            col, cols = (0, D) if side is None else (side * HALF, HALF)
            return cut(self.k, mine, self.half(which), self.count // 2, col, cols)

        def done_rows(self, which):
            return final(self.k, self.half(which), self.count // 2, 0, D)

        def e_in(self, side):
            return (x_in, e_in)[side].at[self.k, self.here]

        def m_in(self, side):
            return m_in.at[self.k, pl.ds(self.row + side * (self.count // 2), self.count // 2)]

        def sum_line(self):
            return line_in.at[LINES.index(self.k), pl.ds(self.row // 2, self.count // 2)]

        def x_sum(self):
            return send(self.u, 4, self.rows_of(w_half), self.sum_line(), "x", from_middle)

        def m_back(self):
            return send(self.u, 5, self.sum_line(), self.done_rows(w_half), "m", from_middle)

        def step(self, n):
            if n == 1:
                y_sum(self.u).start()
            if n == 2:
                y_added(self.u)

                @pl.when(border)
                def _():
                    for side in range(2):
                        send(
                            self.u, 2, self.part(side), self.e_in(side), "e", from_border
                        ).start()

            if n == 3:

                @pl.when(middle)
                def _():
                    wait_rows(self.u, 2, self.count)
                    for side in range(2):
                        add_to(self.part(side), self.e_in(side))
                    for side in range(2):
                        src = self.rows_of(1 - w_half, side)
                        send(self.u, 3, src, self.m_in(side), "m", from_middle).start()

            if n == 4:

                @pl.when(middle)
                def _():
                    wait_rows(self.u, 3, self.count // 2)
                    for side in range(2):
                        add_to(self.rows_of(w_half, side), self.m_in(side))
                    self.x_sum().start()

            if n == 5:

                @pl.when(middle)
                def _():
                    self.x_sum().wait_recv()
                    add_to(self.sum_line(), self.rows_of(w_half))
                    add_far(self.u, self.row, self.sum_line())
                    kept.add(self.sum_line())
                    pltpu.make_async_copy(
                        self.sum_line(), self.done_rows(w_half), kept.sem
                    ).start()
                    self.m_back().start()
                    there = self.done_rows(w_half)
                    send_last(self.sum_line(), there, "e", from_middle, done_border)

            if n == 6:

                @pl.when(middle)
                def _():
                    self.m_back().wait_recv()
                    there = self.done_rows(1 - w_half)
                    send_last(there, there, "e", from_middle, done_border)

                for _ in range(2):
                    done_border.add(self.sum_line())

    class Deep:
        first_x = False

        def __init__(self, u):
            self.u = u
            self.k = UNITS[u][0]

        def one(self, i):
            src = cut(self.k, 2 * i + c, (1 - z_half) * EIGHTH * 2, 2 * EIGHTH)
            return send(self.u, 1, src, self.one_in(i), "e")

        def one_in(self, i):
            return y_in.at[self.k, pl.ds(i * 2 * EIGHTH, 2 * EIGHTH)]

        def two(self, i, side):
            row = row_one + (1 - w_half) * EIGHTH
            src = cut(self.k, 2 * i + c, row, EIGHTH, side * HALF, HALF)
            return send(self.u, 2, src, self.two_in(i, side), "w")

        def two_in(self, i, side):
            return x_in.at[self.k, pl.ds((2 * i + side) * EIGHTH, EIGHTH)]

        def x_sum(self, i):
            src = cut(self.k, 2 * i + c, row_two, EIGHTH, (1 - s) * HALF, HALF)
            return send(self.u, 3, src, self.x_in(i), "x")

        def x_in(self, i):
            return e_in.at[self.k, pl.ds(i * EIGHTH, EIGHTH)]

        def last(self):
            src = cut(self.k, yours, row_two, EIGHTH, s * HALF, HALF)
            return send(self.u, 4, src, self.x_in(2), "y")

        def piece(self):
            return cut(self.k, mine, row_two, EIGHTH, s * HALF, HALF)

        def own(self):
            there = final(self.k, row_two, EIGHTH)
            return pltpu.make_async_copy(self.piece(), there, g_recv.at[SEM_AT[self.u] + 7])

        def back(self, n):
            if n == 0:
                way = "x" if self.first_x else "w"
                return send(self.u, 5, self.piece(), final(self.k, row_two, EIGHTH), way)
            if self.first_x:
                here = final(self.k, row_two, EIGHTH, 0, D)
            else:
                here = final(self.k, row_one, 2 * EIGHTH)
            return send(self.u, 6, here, here, "w" if self.first_x else "e")

        def back_last(self):
            if self.first_x:
                here = final(self.k, row_one, 2 * EIGHTH, 0, D)
            else:
                here = final(self.k, 0, SHARD)
            send_last(here, here, "e" if self.first_x else "x")
            done.add(here)

        def step(self, n):
            if n == 1:
                for i in range(2):
                    self.one(i).start()
            if n == 2:
                wait_rows(self.u, 1, 4 * EIGHTH)
                for i in range(2):
                    add_to(cut(self.k, 2 * i + c, row_one, 2 * EIGHTH), self.one_in(i))
                    for side in range(2):
                        self.two(i, side).start()
            if n == 3:
                wait_rows(self.u, 2, 2 * EIGHTH)
                for i in range(2):
                    for side in range(2):
                        here = cut(self.k, 2 * i + c, row_two, EIGHTH, side * HALF, HALF)
                        add_to(here, self.two_in(i, side))
                    self.x_sum(i).start()
            if n == 4:
                wait_rows(self.u, 3, EIGHTH)
                for i in range(2):
                    here = cut(self.k, 2 * i + c, row_two, EIGHTH, s * HALF, HALF)
                    add_to(here, self.x_in(i))
                self.last().start()
            if n == 5:
                self.last().wait_recv()
                add_to(self.piece(), self.x_in(2))
                add_far(self.u, 0, self.piece())
                self.own().start()
                self.back(0).start()
            if n == 6:
                self.own().wait()
                self.back(0).wait_recv()
                self.back(1).start()
            if n == 7:
                self.back(1).wait_recv()
                self.back_last()

    class DeepX(Deep):
        first_x = True

    kinds = {"wide": Wide, "cross": Cross, "line": Line, "deep": Deep, "deep_x": DeepX}
    sums = [kinds[unit[3]](u) for u, unit in enumerate(UNITS)]

    def sum_step(u, n):
        if n == 0:
            for i in range(2):
                core_sum(u, i).start()
            return
        if n == 1:
            k, row, count, _ = UNITS[u]
            wait_rows(u, 0, 2 * count)
            for i in range(2):
                add_to(cut(k, 2 * i + c, row, count), core_in.at[k, i, pl.ds(row, count)])
        sums[u].step(n)

    def sums_done():
        to_core.wait()
        to_all.wait()
        done.wait()

        @pl.when(border)
        def _():
            from_border.wait()
            if LINES:
                done_border.wait()

        @pl.when(middle)
        def _():
            from_middle.wait()
            kept.wait()

    vec_steps = 6 + extra
    vec_moves = []

    def vec_step(n):
        if n == 0:
            top = vec_grads[...]
            high = top.astype(LOW)
            low = (top - high.astype(F32)).astype(LOW)
            for seg in range(GROUPS):
                spread = spread_matrix(seg)
                vec_segs[seg] = dot_turned(high, spread) + dot_turned(low, spread)
            for row, parts in SEGMENTS.items():
                for seg, (q, at) in enumerate(parts):
                    vecs[q, at : at + 1, :] = vec_segs[seg, row : row + 1, :]
            for i in range(2):
                copy = remote(
                    vecs.at[2 * i + 1 - c], vec_in.at[i], v_send.at[3 + i], v_recv.at[3 + i], near["c"]
                )
                copy.start()
                vec_moves.append(copy)
            return
        if n == 1:
            for i in range(2):
                vec_moves[i].wait()
                vecs[2 * i + c] = vecs[2 * i + c] + vec_in[i]
        else:
            vec_moves[-1].wait()
            vecs[mine] = vecs[mine] + vec_in[n]
        steps = [near["y"], near["x"], near["e"], near["w"]] + far
        if n <= len(steps):
            copy = remote(
                vecs.at[yours if n == 1 else mine],
                vec_in.at[1 + n],
                v_send.at[4 + n],
                v_recv.at[4 + n],
                steps[n - 1],
            )
            copy.start()
            vec_moves.append(copy)
        else:
            copy = pltpu.make_async_copy(vecs.at[mine], vec_out, io_sem.at[2])
            copy.start()
            copy.wait()

    forward = [([], vectors_ready), ([], norm_first)]
    forward += [([QKV + n], functools.partial(project_block, n)) for n in range(3)]
    forward += [([], functools.partial(attend, w)) for w in range(windows)]
    forward += [([OUT], attend_out)]
    forward += [([FIN + n], functools.partial(inner_block, n)) for n in range(BLOCKS)]
    forward += [([8, 9, 10, 11], layer_end), ([12, 13, 14, 15], convolve)]
    for item in GATHER_PLAN:
        if item < 0:
            need, work = forward.pop(0)
            for k in need:
                weight_ready(k)
            work()
        else:
            gather_step(item // 10, item % 10)
    gather_done()

    moves = []

    def end_chars():
        chars_back()
        moves.extend(swap(1, context, chars_out, rows))

    backward = [functools.partial(convolve_back, side) for side in range(2)] + [layer_back]
    backward += [functools.partial(active_back, n) for n in range(BLOCKS)]
    backward += [inner_sum]
    backward += [
        functools.partial(weight_grad, FIN + n, normed_ffn, slope.at[n]) for n in range(BLOCKS)
    ]
    backward += [hidden_back, context_back]
    backward += [functools.partial(attend_back, w) for w in range(windows)]
    backward += [project_sum]
    backward += [functools.partial(weight_grad, QKV + n, normed, slope.at[n]) for n in range(3)]
    backward += [end_chars]
    backward += [functools.partial(vec_step, n) for n in range(vec_steps)]
    for item in PLAN:
        if item < 0:
            backward.pop(0)()
        else:
            sum_step(item // 10, item % 10)
    for work in backward:
        work()
    sums_done()
    for copy in moves:
        copy.wait()


def run(args, chars, extra):
    rows = chars.shape[0] // 2
    mols = rows // KERNEL
    anywhere = pl.BlockSpec(memory_space=pl.ANY)
    dma = pltpu.SemaphoreType.DMA
    vmem = pltpu.VMEM
    windows = rows // WIN
    return pl.pallas_call(
        functools.partial(program_kernel, rows, extra),
        name="layer_and_sums",
        out_shape=[
            jax.ShapeDtypeStruct((2 * mols, HALF), LOW),
            jax.ShapeDtypeStruct((2 * rows, HALF), LOW),
            jax.ShapeDtypeStruct(VEC, F32),
        ]
        + [jax.ShapeDtypeStruct(shape, LOW) for shape in SHARD_SHAPES]
        + [jax.ShapeDtypeStruct((len(UNITS), extra, SHARD, D), LOW)] * (extra > 0),
        in_specs=[anywhere, pl.BlockSpec(memory_space=vmem)] + [anywhere] * (len(args) - 2),
        out_specs=[anywhere] * (8 + (extra > 0)),
        scratch_shapes=[vmem((n * SHARD,), LOW) for n in VEC_COUNTS]
        + [
            vmem((COUNT * D, D), LOW),
            vmem((COUNT, 2, SHARD, D), LOW),
            vmem((COUNT, SHARD, D), LOW),
            vmem((COUNT, SHARD, HALF), LOW),
            vmem((COUNT, SHARD, HALF), LOW),
            vmem((COUNT, SHARD, HALF), LOW),
            vmem((max(len(LINES), 1), SHARD // 2, D), LOW),
            vmem(VEC, F32),
            vmem((GROUPS,) + VEC, F32),
            vmem((GROUPS,) + VEC, F32),
            vmem((VEC[0], D), F32),
            vmem((VEC[0], D), F32),
            vmem((7 + extra,) + VEC, F32),
            vmem((rows, D), LOW),
            vmem((mols, D), LOW),
            vmem((rows, D), LOW),
            vmem((3, rows, D), LOW),
            vmem((windows, PAIRS, 2 * WIN, WIN), LOW),
            vmem((rows, D), LOW),
            vmem((rows, D), F32),
            vmem((rows, D), LOW),
            vmem((BLOCKS, rows, D), LOW),
            vmem((BLOCKS, rows, D), LOW),
            vmem((rows, D), F32),
            vmem((KERNEL, mols, D), LOW),
            vmem((rows, D), LOW),
            vmem((rows, D), F32),
            vmem((mols, D), LOW),
            dma((1,)),
            dma((3, len(PIECES))),
            dma((COUNT,)),
            dma((7,)),
            dma((SEMS,)),
            dma((len(UNITS), extra) if extra else (1, 1)),
            dma((len(UNITS), extra) if extra else (1, 1)),
            dma((9 + extra,)),
            dma((9 + extra,)),
            dma((5 + len(VEC_COUNTS),)),
            dma((2,)),
            dma((2,)),
        ],
        compiler_params=pltpu.CompilerParams(
            collective_id=0, has_side_effects=True, vmem_limit_bytes=63 << 20
        ),
    )(*args)


def finish_kernel(mols, layer, vec, *refs):
    sums, (mols_out, layer_out) = refs[:5], refs[5:7]
    outs, vec_outs = refs[7:12], refs[12 : 12 + len(VEC_COUNTS)]
    low, wide, load, store, whole, mols_held, layer_held = refs[12 + len(VEC_COUNTS) :]
    through = [
        pltpu.make_async_copy(mols, mols_held, whole.at[0]),
        pltpu.make_async_copy(layer, layer_held, whole.at[1]),
    ]
    loads = [
        pltpu.make_async_copy(shard_block(sums, k, 0, SHARD), low.at[k], load.at[k])
        for k in range(COUNT)
    ]
    for copy in loads + through:
        copy.start()
    copies = [
        pltpu.make_async_copy(mols_held, mols_out, whole.at[0]),
        pltpu.make_async_copy(layer_held, layer_out, whole.at[1]),
    ]
    at = 0
    for ref, count in zip(vec_outs, VEC_COUNTS):
        for i in range(count):
            line = vec[at : at + 1, :][:, :SHARD].reshape(SHARD)
            ref[i * SHARD : (i + 1) * SHARD] = line
            at += 1
    for before, after in zip(through, copies):
        before.wait()
        after.start()
    for k in range(COUNT):
        loads[k].wait()
        wide[k] = low[k].astype(F32)
        copy = pltpu.make_async_copy(wide.at[k], shard_block(outs, k, 0, SHARD), store.at[k])
        copy.start()
        copies.append(copy)
    for copy in copies:
        copy.wait()


def finish(mols, layer, vec, sums):
    anywhere = pl.BlockSpec(memory_space=pltpu.HBM)
    inside = pl.BlockSpec(memory_space=pltpu.VMEM)
    shape = jax.ShapeDtypeStruct
    out = pl.pallas_call(
        finish_kernel,
        name="widen_sums",
        out_shape=[shape(mols.shape, LOW), shape(layer.shape, LOW)]
        + [shape(w.shape, F32) for w in sums]
        + [shape((n * SHARD,), F32) for n in VEC_COUNTS],
        in_specs=[anywhere, anywhere, inside] + [anywhere] * 5,
        out_specs=[anywhere] * 7 + [inside] * len(VEC_COUNTS),
        scratch_shapes=[
            pltpu.VMEM((COUNT, SHARD, D), LOW),
            pltpu.VMEM((COUNT, SHARD, D), F32),
            pltpu.SemaphoreType.DMA((COUNT,)),
            pltpu.SemaphoreType.DMA((COUNT,)),
            pltpu.SemaphoreType.DMA((2,)),
            pltpu.VMEM(mols.shape, LOW),
            pltpu.VMEM(layer.shape, LOW),
        ],
        compiler_params=pltpu.CompilerParams(vmem_limit_bytes=60 << 20),
    )(mols, layer, vec, *sums)
    return out[0], out[1], out[2:7], out[7:]


def body(
    chars,
    char_codes,
    mol_cotangent,
    attn_norm_gain,
    attn_norm_bias,
    qkv_weight,
    qv_bias,
    out_weight,
    out_bias,
    ffn_norm_gain,
    ffn_norm_bias,
    ffn_in_weight,
    ffn_in_bias,
    ffn_out_weight,
    ffn_out_bias,
    conv_weight,
    conv_bias,
    down_norm_gain,
    down_norm_bias,
):
    vectors = [
        attn_norm_gain,
        attn_norm_bias,
        qv_bias,
        out_bias,
        ffn_norm_gain,
        ffn_norm_bias,
        ffn_in_bias,
        ffn_out_bias,
        conv_bias,
        down_norm_gain,
        down_norm_bias,
    ]
    result = run(
        (
            chars,
            char_codes.reshape(-1, WIN),
            mol_cotangent,
            qkv_weight,
            out_weight,
            ffn_in_weight,
            ffn_out_weight,
            conv_weight,
            *vectors,
        ),
        chars,
        (lax.axis_size("replica") // RING).bit_length() - 1,
    )
    molecules, chars_grad, big, v = finish(*result[:3], result[3:8])
    t_qkv, t_out, t_in, t_ffo, t_conv = big
    return (
        molecules,
        chars_grad,
        v[0],
        v[1],
        t_qkv,
        v[2],
        t_out,
        v[3],
        v[4],
        v[5],
        t_in,
        v[6],
        t_ffo,
        v[7],
        t_conv,
        v[8],
        v[9],
        v[10],
    )


def solution(mesh):
    return jax.shard_map(
        body,
        mesh=mesh,
        in_specs=(
            P(("group", "replica"), None),
            P(("group", "replica")),
            P(("group", "replica"), None),
            P("group"),
            P("group"),
            P("group", None),
            P("group"),
            P("group", None),
            P("group"),
            P("group"),
            P("group"),
            P("group", None),
            P("group"),
            P("group", None),
            P("group"),
            P("group", None),
            P("group"),
            P("group"),
            P("group"),
        ),
        out_specs=(
            P(("group", "replica"), "section"),
            P(("group", "replica"), "section"),
            P("group"),
            P("group"),
            P("group", None),
            P("group"),
            P("group", None),
            P("group"),
            P("group"),
            P("group"),
            P("group", None),
            P("group"),
            P("group", None),
            P("group"),
            P("group", None),
            P("group"),
            P("group"),
            P("group"),
        ),
        check_vma=False,
    )
```

```python
import functools
import math

import jax
import jax.numpy as jnp
from jax import lax
from jax.experimental import pallas as pl
from jax.experimental.pallas import tpu as pltpu
from jax.sharding import PartitionSpec as P

D = 768
HEADS = 12
HEAD_DIM = 64
FF = 3072
WIN = 128
KERNEL = 4
GROUPS = 4
RING = 4
SHARD = D // GROUPS
THIRD = SHARD // 3
EIGHTH = SHARD // 4
HALF = D // 2
TILE = 768
PAIR = 2 * HEAD_DIM
PAIRS = HEADS // 2
RUN = WIN // KERNEL
BLOCKS = FF // D
VEC = (16, 256)
VEC_COUNTS = (1, 1, 2, 1, 1, 1, 4, 1, 1, 1, 1)
SCRATCH = 28
norm_eps = 1e-06
mask_value = -10000.0
MESH = pl.DeviceIdType.MESH
F32 = jnp.float32
LOW = jnp.bfloat16

CHUNKS = (
    [(0, "col", j) for j in range(3)]
    + [(1, "col", 0)]
    + [(2, "col", j) for j in range(4)]
    + [(3, "row", j) for j in range(4)]
    + [(4, "row", j) for j in range(4)]
)
COUNT = len(CHUNKS)
QKV, OUT, FIN, FOUT, CONV = BASES = (0, 3, 4, 8, 12)
SHARD_SHAPES = [(SHARD, 3 * D), (SHARD, D), (SHARD, FF), (FF // GROUPS, D), (D, D)]

A_GAIN, A_BIAS, Q_BIAS, V_BIAS, O_BIAS, F_GAIN, F_BIAS = range(7)
IN_BIAS, FO_BIAS, C_BIAS, D_GAIN, D_BIAS = 7, 11, 12, 13, 14


def segments():
    table = {}
    for row, at in zip((A_GAIN, A_BIAS, O_BIAS, F_GAIN, F_BIAS), (0, 1, 4, 5, 6)):
        table[row] = [(q, at) for q in range(GROUPS)]
    table[Q_BIAS] = [(0, 2), (0, 3), (1, 2), (1, 3)]
    table[V_BIAS] = [(2, 2), (2, 3), (3, 2), (3, 3)]
    for n in range(BLOCKS):
        table[IN_BIAS + n] = [(n, 7 + i) for i in range(4)]
    for row, at in zip((FO_BIAS, C_BIAS, D_GAIN, D_BIAS), (11, 12, 13, 14)):
        table[row] = [(q, at) for q in range(GROUPS)]
    return table


SEGMENTS = segments()

PIECES = [
    (0, 0, 1, 3), (1, 0, 1, 3), (2, 0, 1, 3), (3, 0, 1, 3), (4, 0, 1, 3), (5, 0, 1, 3), (6,
    0, 1, 3), (7, 0, 1, 3), (8, 0, 1, 3), (9, 0, 1, 3), (10, 0, 1, 3), (11, 0, 1, 3), (12,
    0, 1, 3), (13, 0, 1, 3), (14, 0, 2, 3), (14, 1, 2, 3), (15, 0, 2, 3), (15, 1, 2, 3),
]
GATHER_PLAN = [
    -1, -1, 0, 10, 1, 20, 11, 30, 2, 21, 40, -1, 12, 31, 50, 22, 41, 60, -1, -1, 32, 51, 70,
    -1, -1, 42, 61, 80, -1, 52, 71, 90, -1, -1, 62, 81, 100, -1, 72, 91, 110, -1, 82, 101,
    120, -1, 130, 92, 111, 140, -1, 150, 102, 121, 160, 170, 112, 131, 141, -1, 122, 151,
    161, -1, 132, 142, 171, -1, 152, -1, 162, 172, -1,
]

UNITS = [
    (12, 0, 192, "deep_x"),
    (13, 0, 192, "bounce"),
    (14, 0, 192, "cross"),
    (15, 0, 192, "bounce"),
    (8, 0, 192, "cross"),
    (9, 0, 96, "line"),
    (9, 96, 96, "line"),
    (10, 0, 96, "cross"),
    (10, 96, 96, "cross"),
    (11, 0, 64, "line"),
    (11, 64, 64, "line"),
    (11, 128, 64, "line"),
    (4, 0, 192, "cross"),
    (5, 0, 192, "line"),
    (6, 0, 192, "bounce"),
    (7, 0, 192, "bounce"),
    (3, 0, 64, "bounce"),
    (3, 64, 64, "bounce"),
    (3, 128, 64, "bounce"),
    (0, 0, 96, "cross"),
    (0, 96, 96, "cross"),
    (1, 0, 96, "wide"),
    (1, 96, 96, "wide"),
    (2, 0, 64, "line"),
    (2, 64, 64, "line"),
    (2, 128, 64, "line"),
]

SEM_COUNT = {"wide": 5, "cross": 5, "bounce": 5, "line": 6, "deep": 8, "deep_x": 8}
SEM_AT = [sum(SEM_COUNT[unit[3]] for unit in UNITS[:u]) for u in range(len(UNITS))]
SEMS = sum(SEM_COUNT[unit[3]] for unit in UNITS)
LINES = sorted({unit[0] for unit in UNITS if unit[3] == "line"})
SWAP_PARTS = 2
PLAN = [
    -1, 10, 0, -1, 20, 11, 30, 1, -1, -2, 31, 21, -1, -1, 12, -1, 2, -1, 22, 70, 80, 50, 60,
    32, 90, 100, 110, 71, 40, 81, 13, 51, 61, 91, 101, 111, -1, 33, 3, 23, 41, -1, 14, 120,
    52, 72, -1, 130, -1, 34, 140, 82, 121, 131, 62, 15, 4, 92, 141, 24, -1, 102, 150, -1,
    35, 16, 53, 73, 112, 151, 25, 42, 83, 63, -1, 160, 170, 36, 180, 54, 93, 64, 161, 171,
    103, 181, -1, 122, 74, 26, 132, 5, 94, 113, 104, -1, 84, 75, 17, 55, -1, 37, 65, 114,
    142, 85, 76, 95, -1, 56, 133, 105, 66, 6, -1, 86, 115, 96, 152, -1, 190, 200, 143, 134,
    -1, 210, 220, 191, 201, 43, 106, -1, 230, 240, 250, 7, 162, 211, 221, 231, 241, 251,
    144, 172, 116, 153, 135, 182, -1, -2, -2, -1, 44, 192, 123, -1, 145, 202, 212, 163, 136,
    154, 173, 183, 222, 146, 45, 124, 164, 232, 174, 155, 184, 242, 233, 252, 46, 125, 193,
    165, -1, 243, 175, 213, 203, 156, 185, 253, 223, 147, 234, 194, 244, 126, 254, 214, 166,
    176, 195, 204, 186, 224, 215, -1, 157, 196, 235, 205, 245, 216, 225, -1, 255, 236, 167,
    246, 177, 206, 187, 226, -1, 256,
]


def at16(value):
    return pl.multiple_of(value, 16)


def at128(value):
    return pl.multiple_of(value, 128)


def spot(chunk, shard, first=0):
    mat, kind, j = CHUNKS[chunk]
    if kind == "col":
        return at16((BASES[mat] + j) * D + shard * SHARD + first)
    return at16((BASES[mat] + shard) * D + j * SHARD + first)


def shard_block(refs, chunk, first, rows, col=0, cols=D):
    mat, kind, j = CHUNKS[chunk]
    if kind == "col":
        return refs[mat].at[pl.ds(at16(first), rows), pl.ds(at128(j * D + col), cols)]
    return refs[mat].at[pl.ds(at16(j * SHARD + first), rows), pl.ds(at128(col), cols)]


def remote(src, dst, send, recv, target):
    return pltpu.make_async_remote_copy(
        src_ref=src,
        dst_ref=dst,
        send_sem=send,
        recv_sem=recv,
        device_id=target,
        device_id_type=MESH,
    )


class Tally:
    def __init__(self, sem, yard):
        self.sem, self.yard, self.size = sem, yard, 0

    def add(self, ref):
        self.size += math.prod(ref.shape)

    def wait(self):
        here = self.yard.at[pl.ds(0, self.size // D)]
        pltpu.make_async_copy(here, here, self.sem).wait()
        self.size = 0


class Move:
    def __init__(self, src, dst, sent, recv, target):
        self.src, self.dst, self.sent = src, dst, sent
        self.copy = remote(src, dst, sent.sem, recv, target)

    def start(self):
        self.sent.add(self.src)
        self.copy.start()

    def wait_recv(self):
        self.copy.wait_recv()


def add_to(dst, src):
    @pl.loop(0, dst.shape[0] // 16)
    def _(i):
        here = pl.ds(at16(i * 16), 16)
        dst[here, :] = dst[here, :] + src[here, :]


def dot(left, right):
    return jnp.dot(left, right, preferred_element_type=F32)


def dot_rows(left, right):
    return lax.dot_general(left, right, (((0,), (0,)), ((), ())), preferred_element_type=F32)


def dot_turned(left, right):
    return lax.dot_general(left, right, (((1,), (1,)), ((), ())), preferred_element_type=F32)


def normalized(values):
    center = values - jnp.mean(values, axis=-1, keepdims=True)
    scale = lax.rsqrt(jnp.mean(center * center, axis=-1, keepdims=True) + norm_eps)
    return center * scale, scale


def norm_back(unit, scale, gain, grad):
    grad_unit = grad * gain
    mean_grad = jnp.mean(grad_unit, axis=-1, keepdims=True)
    mean_both = jnp.mean(grad_unit * unit, axis=-1, keepdims=True)
    return scale * (grad_unit - mean_grad - unit * mean_both)


def gelu_parts(values):
    half = 0.5 * lax.erf(values * (0.5**0.5)) + 0.5
    bell = jnp.exp(-0.5 * values * values) * 0.3989422804014327
    return values * half, half + values * bell


def column_sum(values):
    return jnp.sum(values, axis=0, keepdims=True)


def program_kernel(rows, extra, *refs):
    count = len(VEC_COUNTS)
    (chars, codes, cotangent) = refs[:3]
    shards = refs[3:8]
    vectors = refs[8 : 8 + count]
    mols_out, chars_out, vec_out = refs[8 + count : 11 + count]
    out = refs[11 + count : 16 + count]
    more_in = refs[16 + count] if extra else None
    refs = refs[16 + count + (extra > 0) :]
    flat, refs = refs[:count], refs[count:]
    (
        held,
        core_in,
        y_in,
        x_in,
        e_in,
        m_in,
        line_in,
        vec,
        vecs,
        vec_segs,
        rows_f32,
        vec_grads,
        vec_in,
        chars_v,
        cot_v,
        normed,
        projected,
        probs,
        context,
        hidden,
        normed_ffn,
        slope,
        active,
        layer,
        stacked,
        low_grad,
        total,
        mol_v,
    ) = refs[:SCRATCH]
    (
        w_send,
        w_recv,
        c_recv,
        g_send,
        g_recv,
        more_send,
        more_recv,
        v_send,
        v_recv,
        io_sem,
        swap_sem,
    ) = refs[SCRATCH:]
    windows = rows // WIN
    mols = rows // KERNEL
    s, g, r = lax.axis_index("section"), lax.axis_index("group"), lax.axis_index("replica")
    near = {
        "c": (s, g ^ 1, r),
        "y": (s, g ^ 2, r),
        "x": (1 - s, g, r),
        "e": (s, g, r ^ 1),
        "m": (s, g, r ^ 3),
        "d": (s, g ^ 3, r),
        "w": (s, g, r ^ 2),
    }
    far = [(s, g, r ^ (RING << i)) for i in range(extra)]
    place = lax.rem(r, RING)
    even = lax.rem(r, 2) == 0
    middle = jnp.logical_or(place == 1, place == 2)
    border = jnp.logical_not(middle)

    barrier = pltpu.get_barrier_semaphore()
    greeted = list(near.values()) + far
    for target in greeted:
        pl.semaphore_signal(barrier, inc=1, device_id=target, device_id_type=MESH)

    flat_copies = [
        pltpu.make_async_copy(src, dst, io_sem.at[5 + i])
        for i, (src, dst) in enumerate(zip(vectors, flat))
    ]
    for copy in flat_copies:
        copy.start()
    vec[...] = jnp.zeros_like(vec)
    vec_grads[...] = jnp.zeros_like(vec_grads)
    vec_segs[...] = jnp.zeros_like(vec_segs)
    at = 0
    for copy, values, rows_held in zip(flat_copies, flat, VEC_COUNTS):
        copy.wait()
        wide = values[...].astype(F32)
        for i in range(rows_held):
            line = wide[i * SHARD : (i + 1) * SHARD].reshape(1, SHARD)
            vec[at : at + 1, pl.ds(0, SHARD)] = line
            at += 1
    pl.semaphore_wait(barrier, len(greeted))

    y_third = jnp.where(even, s, 2)
    z_third = jnp.where(even, 2, s)
    x_third = 1 - s
    other = g ^ 2

    own_vec = pltpu.make_async_copy(vec, vecs.at[g], io_sem.at[2])
    vec_copies = [
        remote(vec, vecs.at[g], v_send.at[i], v_recv.at[i], near[way])
        for i, way in enumerate("cyd")
    ]
    for copy in vec_copies + [own_vec]:
        copy.start()

    sent = Tally(w_send.at[0], held)

    def rows_by(u, way):
        k, part, parts, ways = PIECES[u]
        if ways == 2:
            count = SHARD // parts
            which = s if way == "y" else 1 - s
            return k, part * count + which * (count // 2), count // 2
        third = {"y": y_third, "z": z_third, "x": x_third}[way]
        return k, third * THIRD + part * (THIRD // parts), THIRD // parts

    def arrived(u, way):
        k, first, count = rows_by(u, way)
        return held.at[pl.ds(spot(k, other, first), count)]

    def hop(u, way, src_way):
        here = arrived(u, src_way)
        i = "yxz".index(way)
        return Move(here, here, sent, w_recv.at[i, u], near["yxe"[i]])

    def first_hop(u):
        k, first, count = rows_by(u, "y")
        src = shard_block(shards, k, first, count)
        there = held.at[pl.ds(spot(k, g, first), count)]
        return Move(src, there, sent, w_recv.at[0, u], near["y"])

    def core_own(k):
        src = shard_block(shards, k, 0, SHARD)
        there = held.at[pl.ds(spot(k, g), SHARD)]
        return Move(src, there, sent, c_recv.at[k], near["c"])

    def core_hop(u, way):
        here = arrived(u, way)
        Move(here, here, sent, c_recv.at[PIECES[u][0]], near["c"]).start()

    for u in range(len(PIECES)):
        first_hop(u).start()
    loads = [
        pltpu.make_async_copy(chars.at[pl.ds(at16(s * rows), rows)], chars_v, io_sem.at[0]),
        pltpu.make_async_copy(cotangent.at[pl.ds(at16(s * mols), mols)], cot_v, io_sem.at[1]),
    ]
    for copy in loads:
        copy.start()
    for k in range(COUNT):
        own_block = held.at[pl.ds(spot(k, g), SHARD)]
        pltpu.make_async_copy(shard_block(shards, k, 0, SHARD), own_block, c_recv.at[k]).start()
        core_own(k).start()

    def gather_step(u, n):
        two = PIECES[u][3] == 2
        if n == 0:
            hop(u, "y", "y").wait_recv()
            if two:
                hop(u, "x", "y").start()
            else:
                hop(u, "z", "y").start()

                @pl.when(even)
                def _():
                    hop(u, "x", "y").start()

            core_hop(u, "y")
        if n == 1:
            hop(u, "z", "z").wait_recv()

            @pl.when(jnp.logical_not(even))
            def _():
                hop(u, "x", "z").copy.start()

            core_hop(u, "z")
        if n == 2:
            hop(u, "x", "x").wait_recv()
            core_hop(u, "x")

    def weight_ready(k):
        here = held.at[pl.ds(0, 3 * SHARD)]
        pltpu.make_async_copy(here, here, c_recv.at[k]).wait()

    def gather_done():
        sent.wait()

    def spread_matrix(seg):
        i = lax.broadcasted_iota(jnp.int32, (VEC[1], D), 0)
        j = lax.broadcasted_iota(jnp.int32, (VEC[1], D), 1)
        hit = jnp.logical_and(j == i + seg * SHARD, i < SHARD)
        return jnp.where(hit, 1.0, 0.0).astype(LOW)

    def vectors_ready():
        own_vec.wait()
        for copy in vec_copies:
            copy.wait()
        for row, parts in SEGMENTS.items():
            for seg, (q, at) in enumerate(parts):
                vec_segs[seg, row : row + 1, :] = vecs[q, at : at + 1, :]
        full = jnp.zeros((VEC[0], D), F32)
        for seg in range(GROUPS):
            full = full + dot(vec_segs[seg].astype(LOW), spread_matrix(seg))
        rows_f32[...] = full

    def vector(row):
        return rows_f32[row : row + 1, :]

    def vector_tile(row, j):
        return rows_f32[row : row + 1, pl.ds(at128(j * TILE), TILE)]

    def block(n, j=None):
        start = n * D
        if not isinstance(n, int):
            start = at16(start)
        if j is None:
            return held[pl.ds(start, D), :]
        return held[pl.ds(start, D), pl.ds(at128(j * TILE), TILE)]

    def row_tiles(body):
        @pl.loop(0, rows // WIN)
        def _(i):
            body(pl.ds(at128(i * WIN), WIN), i)

    def col_tiles(body):
        @pl.loop(0, D // TILE)
        def _(j):
            body(pl.ds(at128(j * TILE), TILE), j)

    def norm_first():
        loads[0].wait()

        def one(here, i):
            unit, _ = normalized(chars_v[here, :].astype(F32))
            normed[here, :] = (unit * vector(A_GAIN) + vector(A_BIAS)).astype(LOW)

        row_tiles(one)

    def project_block(n):
        def one(here, j):
            value = dot(normed[...], block(QKV + n, j))
            if n == 0:
                value = value + vector_tile(Q_BIAS, j)
            if n == 2:
                value = value + vector_tile(V_BIAS, j)
            projected[n, :, here] = value.astype(LOW)

        col_tiles(one)

    def key_bias(w):
        code = codes[pl.ds(s * windows + w, 1), :]
        return jnp.where(code != 0, 0.0, mask_value).astype(F32)

    def lanes():
        return lax.broadcasted_iota(jnp.int32, (WIN, PAIR), 1) < HEAD_DIM

    def two_heads(values):
        first = lanes()
        zero = jnp.zeros_like(values)
        return jnp.concatenate(
            [jnp.where(first, values, zero), jnp.where(first, zero, values)], axis=0
        )

    def one_pair(values):
        return jnp.where(lanes(), values[:WIN], values[WIN:])

    scale_factor = HEAD_DIM ** (-0.5)

    def attend(w):
        here = pl.ds(w * WIN, WIN)
        bias = key_bias(w)
        for p in range(PAIRS):
            cols = pl.ds(p * PAIR, PAIR)
            queries = two_heads(projected[0, here, cols])
            scores = dot_turned(queries, projected[1, here, cols]) * scale_factor + bias
            top = jnp.max(scores, axis=-1, keepdims=True)
            weight = jnp.exp(scores - top)
            weight = weight / jnp.sum(weight, axis=-1, keepdims=True)
            prob = weight.astype(LOW)
            probs[w, p] = prob
            context[here, cols] = one_pair(dot(prob, projected[2, here, cols])).astype(LOW)

    def attend_out():
        def one(here, j):
            value = dot(context[...], block(OUT, j)) + vector_tile(O_BIAS, j)
            hidden[:, here] = chars_v[:, here].astype(F32) + value

        col_tiles(one)

        def norm(here, i):
            unit, _ = normalized(hidden[here, :])
            normed_ffn[here, :] = (unit * vector(F_GAIN) + vector(F_BIAS)).astype(LOW)

        row_tiles(norm)

    def inner_block(n):
        def one(here, j):
            value = dot(normed_ffn[...], block(FIN + n, j)) + vector_tile(IN_BIAS + n, j)
            gelu, grad = gelu_parts(value)
            active[n, :, here] = gelu.astype(LOW)
            slope[n, :, here] = grad.astype(LOW)

        col_tiles(one)

    def by_place():
        i = lax.broadcasted_iota(jnp.int32, (WIN, WIN), 0)
        j = lax.broadcasted_iota(jnp.int32, (WIN, WIN), 1)
        return jnp.where(j == KERNEL * lax.rem(i, RUN) + i // RUN, 1.0, 0.0).astype(LOW)

    def layer_part(side):
        cols = pl.ds(side * HALF, HALF)
        value = hidden[:, cols] + rows_f32[FO_BIAS : FO_BIAS + 1, cols]
        for n in range(BLOCKS):
            value = value + dot(active[n], held[pl.ds((FOUT + n) * D, D), cols])
        low_grad[:, cols] = value.astype(LOW)

    def layer_sort():
        order = by_place()

        def sort(here, w):
            moved = dot(order, low_grad[here, :]).astype(LOW)
            for k in range(KERNEL):
                stacked[k, pl.ds(at16(w * RUN), RUN), :] = moved[k * RUN : (k + 1) * RUN]

        row_tiles(sort)

    def note(row, value):
        vec_grads[row : row + 1, :] = value

    def note_more(row, value):
        vec_grads[row : row + 1, :] = vec_grads[row : row + 1, :] + value

    def convolve_part(side):
        cols = pl.ds(side * HALF, HALF)
        value = 0.0
        for k in range(KERNEL):
            here = pl.ds((CONV + k) * D + side * HALF, HALF)
            value = value + dot(stacked[k, :, cols], held[here, :])
        return value

    first_mols = pl.ds(0, mols)

    def convolve_start():
        total[first_mols, :] = convolve_part(0) + vector(C_BIAS)

    def convolve():
        loads[1].wait()
        gelu, grad = gelu_parts(total[first_mols, :] + convolve_part(1))
        unit, scale = normalized(gelu)
        low = cot_v[...]
        grad_unit = norm_back(unit, scale, vector(D_GAIN), low.astype(F32))
        cot_v[...] = (grad_unit * grad).astype(LOW)
        layer[first_mols, :] = unit
        mol_v[...] = low

    def convolve_end():
        unit = layer[first_mols, :]
        wide = mol_v[...].astype(F32)
        note(D_GAIN, column_sum(wide * unit))
        note(D_BIAS, column_sum(wide))
        note(C_BIAS, column_sum(cot_v[...].astype(F32)))
        mol_v[...] = (unit * vector(D_GAIN) + vector(D_BIAS)).astype(LOW)

    def convolve_back(side):
        cols = pl.ds(side * HALF, HALF)
        for k in range(KERNEL):
            here = pl.ds((CONV + k) * D + side * HALF, HALF)
            total[k * mols : (k + 1) * mols, cols] = dot_turned(cot_v[...], held[here, :])
        for k in range(KERNEL):
            here = pl.ds((CONV + k) * D + side * HALF, HALF)
            held[here, :] = dot_rows(stacked[k, :, cols], cot_v[...]).astype(LOW)

    def layer_back():
        convolve_end()
        order = by_place()

        def sort(here, w):
            parts = [total[pl.ds(at16(k * mols + w * RUN), RUN), :] for k in range(KERNEL)]
            value = dot_rows(order, jnp.concatenate(parts, axis=0).astype(LOW))
            layer[here, :] = value
            low_grad[here, :] = value.astype(LOW)
            note_more(FO_BIAS, column_sum(value))

        row_tiles(sort)

    def weight_grad(n, left, right):
        def one(here, j):
            value = dot_rows(left[:, here], right[...])
            held[pl.ds(at128(n * D + j * TILE), TILE), :] = value.astype(LOW)

        col_tiles(one)

    def active_back(n):
        def one(here, j):
            value = dot_turned(
                low_grad[...], held[pl.ds(at128((FOUT + n) * D + j * TILE), TILE), :]
            )
            inner = (value * slope[n, :, here].astype(F32)).astype(LOW)
            slope[n, :, here] = inner
            vec_grads[IN_BIAS + n : IN_BIAS + n + 1, here] = column_sum(inner.astype(F32))

        col_tiles(one)
        weight_grad(FOUT + n, active.at[n], low_grad)

    def inner_sum():
        def one(here, j):
            value = jnp.zeros((rows, TILE), F32)
            for n in range(BLOCKS):
                value = value + dot_turned(
                    slope[n], held[pl.ds(at128((FIN + n) * D + j * TILE), TILE), :]
                )
            total[:, here] = value

        col_tiles(one)

    def hidden_back():
        def one(here, i):
            unit, scale = normalized(hidden[here, :])
            grad = total[here, :]
            note_more(F_GAIN, column_sum(grad * unit))
            note_more(F_BIAS, column_sum(grad))
            value = layer[here, :] + norm_back(unit, scale, vector(F_GAIN), grad)
            layer[here, :] = value
            low = value.astype(LOW)
            low_grad[here, :] = low
            note_more(O_BIAS, column_sum(low.astype(F32)))

        row_tiles(one)

    def context_back():
        def one(here, j):
            value = dot_turned(low_grad[...], held[pl.ds(at128(OUT * D + j * TILE), TILE), :])
            normed_ffn[:, here] = value.astype(LOW)

        col_tiles(one)
        weight_grad(OUT, context, low_grad)

    def attend_back(w):
        here = pl.ds(w * WIN, WIN)
        for p in range(PAIRS):
            cols = pl.ds(p * PAIR, PAIR)
            grad_out = two_heads(normed_ffn[here, cols])
            prob = probs[w, p]
            wide = prob.astype(F32)
            grad_prob = dot_turned(grad_out, projected[2, here, cols])
            inner = jnp.sum(wide * grad_prob, axis=-1, keepdims=True)
            grad_score = (wide * (grad_prob - inner)).astype(LOW)
            grad_value = dot_rows(prob, grad_out)
            grad_query = one_pair(dot(grad_score, projected[1, here, cols])) * scale_factor
            grad_key = (
                dot_rows(grad_score, two_heads(projected[0, here, cols])) * scale_factor
            )
            low_query, low_value = grad_query.astype(LOW), grad_value.astype(LOW)
            slope[0, here, cols] = low_query
            slope[1, here, cols] = grad_key.astype(LOW)
            slope[2, here, cols] = low_value
            for row, low in ((Q_BIAS, low_query), (V_BIAS, low_value)):
                vec_grads[row : row + 1, cols] = vec_grads[row : row + 1, cols] + column_sum(
                    low.astype(F32)
                )

    def project_sum():
        def one(here, j):
            value = jnp.zeros((rows, TILE), F32)
            for n in range(3):
                value = value + dot_turned(
                    slope[n], held[pl.ds(at128((QKV + n) * D + j * TILE), TILE), :]
                )
            total[:, here] = value

        col_tiles(one)

    def chars_back():
        def one(here, i):
            unit, scale = normalized(chars_v[here, :].astype(F32))
            grad = total[here, :]
            note_more(A_GAIN, column_sum(grad * unit))
            note_more(A_BIAS, column_sum(grad))
            value = layer[here, :] + norm_back(unit, scale, vector(A_GAIN), grad)
            context[here, :] = value.astype(LOW)

        row_tiles(one)

    def swap(i, whole, dst, count, part=0, parts=1):
        here = pl.ds(part * (count // parts), count // parts)
        keep = whole.at[here, pl.ds(at128(s * HALF), HALF)]
        give = whole.at[here, pl.ds(at128((1 - s) * HALF), HALF)]
        there = dst.at[pl.ds(at16(s * count + part * (count // parts)), count // parts)]
        stay = pltpu.make_async_copy(keep, there, swap_sem.at[2 * i])
        go = remote(give, there, swap_sem.at[2 * i], swap_sem.at[2 * i + 1], near["x"])
        stay.start()
        go.start()

    def swaps_done():
        for i, whole in enumerate((mol_v, context)):
            pltpu.make_async_copy(whole, whole, swap_sem.at[2 * i]).wait()
            here = whole.at[:, pl.ds(0, HALF)]
            pltpu.make_async_copy(here, here, swap_sem.at[2 * i + 1]).wait()

    c = lax.rem(g, 2)
    y = g // 2
    mine, yours = 2 * y + c, 2 * (1 - y) + c
    z_half, w_half = lax.rem(r, 2), lax.rem(r // 2, 2)
    row_one = z_half * EIGHTH * 2
    row_two = row_one + w_half * EIGHTH

    to_core, to_all = Tally(g_send.at[0], held), Tally(g_send.at[1], held)
    from_border, from_middle = Tally(g_send.at[2], held), Tally(g_send.at[3], held)
    kept = Tally(g_send.at[4], held)
    done, done_border = Tally(g_send.at[5], held), Tally(g_send.at[6], held)
    done_middle = Tally(g_send.at[7], held)

    def send(u, i, src, dst, way, sender=to_all):
        return Move(src, dst, sender, g_recv.at[SEM_AT[u] + i], near[way])

    def send_last(src, dst, way, sender=to_all, ends=done):
        move = Move(src, dst, sender, ends.sem, near[way])
        move.start()

    def cut(k, q, row, count, col=0, cols=D):
        return held.at[pl.ds(spot(k, q, row), count), pl.ds(at128(col), cols)]

    def final(k, row, count, col=None, cols=HALF):
        return shard_block(out, k, row, count, s * HALF if col is None else col, cols)

    def add_far(u, row, here):
        k = UNITS[u][0]
        count, cols = here.shape
        for i in range(extra):
            there = more_in.at[u, i, pl.ds(0, count), pl.ds(0, cols)]
            near_by = core_in.at[k, 0, pl.ds(row, count), pl.ds(0, cols)]
            copy = remote(here, there, more_send.at[u, i], more_recv.at[u, i], far[i])
            copy.start()
            copy.wait()
            copy = pltpu.make_async_copy(there, near_by, more_send.at[u, i])
            copy.start()
            copy.wait()
            add_to(here, near_by)

    def core_sum(u, i):
        k, row, count, _ = UNITS[u]
        there = core_in.at[k, i, pl.ds(row, count)]
        return send(u, 0, cut(k, 2 * i + 1 - c, row, count), there, "c", to_core)

    def wait_rows(u, i, count):
        here = held.at[pl.ds(0, count)]
        pltpu.make_async_copy(here, here, g_recv.at[SEM_AT[u] + i]).wait()

    def y_sum(u):
        k, row, count, _ = UNITS[u]
        return send(u, 1, cut(k, yours, row, count), y_in.at[k, pl.ds(row, count)], "y")

    def y_added(u):
        k, row, count, _ = UNITS[u]
        y_sum(u).wait_recv()
        add_to(cut(k, mine, row, count), y_in.at[k, pl.ds(row, count)])

    class Wide:
        def __init__(self, u):
            self.u = u
            self.k, self.row, self.count, _ = UNITS[u]
            self.here = pl.ds(self.row, self.count)
            self.total = m_in.at[self.k, self.here]

        def part(self, side):
            return cut(self.k, mine, self.row, self.count, side * HALF, HALF)

        def done_part(self):
            return final(self.k, self.row, self.count)

        def x_sum(self):
            return send(self.u, 2, self.part(1 - s), x_in.at[self.k, self.here], "x")

        def e_sum(self):
            return send(self.u, 3, self.part(s), e_in.at[self.k, self.here], "e", from_border)

        def m_sum(self):
            return send(self.u, 4, self.part(s), self.total, "m", from_middle)

        def e_back(self):
            return send(self.u, 3, self.total, self.done_part(), "e", from_middle)

        def step(self, n):
            if n == 1:
                y_sum(self.u).start()
            if n == 2:
                y_added(self.u)
                self.x_sum().start()
            if n == 3:
                self.x_sum().wait_recv()
                add_to(self.part(s), x_in.at[self.k, self.here])

                @pl.when(border)
                def _():
                    self.e_sum().start()

            if n == 4:

                @pl.when(middle)
                def _():
                    self.e_sum().wait_recv()
                    add_to(self.part(s), e_in.at[self.k, self.here])
                    self.m_sum().start()

            if n == 5:

                @pl.when(middle)
                def _():
                    self.m_sum().wait_recv()
                    add_to(self.total, self.part(s))
                    add_far(self.u, self.row, self.total)
                    kept.add(self.total)
                    pltpu.make_async_copy(self.total, self.done_part(), kept.sem).start()
                    self.e_back().start()
                    send_last(self.total, self.done_part(), "x", from_middle)

            if n == 6:

                @pl.when(border)
                def _():
                    self.e_back().wait_recv()
                    send_last(self.done_part(), self.done_part(), "x", from_border)

                done.add(self.total)

    class Cross(Wide):
        def both_in(self, i):
            return y_in.at[self.k, self.here, pl.ds(i * HALF, HALF)]

        def both_part(self, i, side):
            return cut(self.k, 2 * i + c, self.row, self.count, side * HALF, HALF)

        def y_sum(self):
            src = cut(self.k, yours, self.row, self.count, s * HALF, HALF)
            return send(self.u, 2, src, x_in.at[self.k, self.here], "y")

        def step(self, n):
            if n == 1:
                for i in range(2):
                    send(self.u, 1, self.both_part(i, 1 - s), self.both_in(i), "x").start()
            elif n == 2:
                wait_rows(self.u, 1, self.count)
                for i in range(2):
                    add_to(self.both_part(i, s), self.both_in(i))
                self.y_sum().start()
            elif n == 3:
                self.y_sum().wait_recv()
                add_to(self.part(s), x_in.at[self.k, self.here])

                @pl.when(border)
                def _():
                    self.e_sum().start()

            else:
                super().step(n)

    class Bounce(Wide):
        def step(self, n):
            if n == 5:

                @pl.when(middle)
                def _():
                    self.m_sum().wait_recv()
                    add_to(self.total, self.part(s))
                    add_far(self.u, self.row, self.total)
                    kept.add(self.total)
                    pltpu.make_async_copy(self.total, self.done_part(), kept.sem).start()
                    self.e_back().start()

            elif n == 6:

                @pl.when(border)
                def _():
                    self.e_back().wait_recv()
                    here = self.done_part()
                    send(self.u, 4, here, here, "x", from_border).start()

            elif n == 7:

                @pl.when(border)
                def _():
                    there = final(self.k, self.row, self.count, (1 - s) * HALF)
                    send(self.u, 4, there, there, "x").wait_recv()
                    send_last(there, there, "e", from_border, done_middle)

                done_middle.add(self.total)
            else:
                super().step(n)

    class Line(Wide):
        def half(self, which):
            return self.row + which * (self.count // 2)

        def rows_of(self, which, side=None):
            col, cols = (0, D) if side is None else (side * HALF, HALF)
            return cut(self.k, mine, self.half(which), self.count // 2, col, cols)

        def done_rows(self, which):
            return final(self.k, self.half(which), self.count // 2, 0, D)

        def e_in(self, side):
            return (x_in, e_in)[side].at[self.k, self.here]

        def m_in(self, side):
            return m_in.at[self.k, pl.ds(self.row + side * (self.count // 2), self.count // 2)]

        def sum_line(self):
            return line_in.at[LINES.index(self.k), pl.ds(self.row // 2, self.count // 2)]

        def x_sum(self):
            return send(self.u, 4, self.rows_of(w_half), self.sum_line(), "x", from_middle)

        def m_back(self):
            return send(self.u, 5, self.sum_line(), self.done_rows(w_half), "m", from_middle)

        def step(self, n):
            if n == 1:
                y_sum(self.u).start()
            if n == 2:
                y_added(self.u)

                @pl.when(border)
                def _():
                    for side in range(2):
                        send(
                            self.u, 2, self.part(side), self.e_in(side), "e", from_border
                        ).start()

            if n == 3:

                @pl.when(middle)
                def _():
                    wait_rows(self.u, 2, self.count)
                    for side in range(2):
                        add_to(self.part(side), self.e_in(side))
                    for side in range(2):
                        src = self.rows_of(1 - w_half, side)
                        send(self.u, 3, src, self.m_in(side), "m", from_middle).start()

            if n == 4:

                @pl.when(middle)
                def _():
                    wait_rows(self.u, 3, self.count // 2)
                    for side in range(2):
                        add_to(self.rows_of(w_half, side), self.m_in(side))
                    self.x_sum().start()

            if n == 5:

                @pl.when(middle)
                def _():
                    self.x_sum().wait_recv()
                    add_to(self.sum_line(), self.rows_of(w_half))
                    add_far(self.u, self.row, self.sum_line())
                    kept.add(self.sum_line())
                    pltpu.make_async_copy(
                        self.sum_line(), self.done_rows(w_half), kept.sem
                    ).start()
                    self.m_back().start()
                    there = self.done_rows(w_half)
                    send_last(self.sum_line(), there, "e", from_middle, done_border)

            if n == 6:

                @pl.when(middle)
                def _():
                    self.m_back().wait_recv()
                    there = self.done_rows(1 - w_half)
                    send_last(there, there, "e", from_middle, done_border)

                for _ in range(2):
                    done_border.add(self.sum_line())

    class Deep:
        first_x = False

        def __init__(self, u):
            self.u = u
            self.k = UNITS[u][0]

        def one(self, i):
            src = cut(self.k, 2 * i + c, (1 - z_half) * EIGHTH * 2, 2 * EIGHTH)
            return send(self.u, 1, src, self.one_in(i), "e")

        def one_in(self, i):
            return y_in.at[self.k, pl.ds(i * 2 * EIGHTH, 2 * EIGHTH)]

        def two(self, i, side):
            row = row_one + (1 - w_half) * EIGHTH
            src = cut(self.k, 2 * i + c, row, EIGHTH, side * HALF, HALF)
            return send(self.u, 2, src, self.two_in(i, side), "w")

        def two_in(self, i, side):
            return x_in.at[self.k, pl.ds((2 * i + side) * EIGHTH, EIGHTH)]

        def x_sum(self, i):
            src = cut(self.k, 2 * i + c, row_two, EIGHTH, (1 - s) * HALF, HALF)
            return send(self.u, 3, src, self.x_in(i), "x")

        def x_in(self, i):
            return e_in.at[self.k, pl.ds(i * EIGHTH, EIGHTH)]

        def last(self):
            src = cut(self.k, yours, row_two, EIGHTH, s * HALF, HALF)
            return send(self.u, 4, src, self.x_in(2), "y")

        def piece(self):
            return cut(self.k, mine, row_two, EIGHTH, s * HALF, HALF)

        def own(self):
            there = final(self.k, row_two, EIGHTH)
            return pltpu.make_async_copy(self.piece(), there, g_recv.at[SEM_AT[self.u] + 7])

        def back(self, n):
            if n == 0:
                way = "x" if self.first_x else "w"
                return send(self.u, 5, self.piece(), final(self.k, row_two, EIGHTH), way)
            if self.first_x:
                here = final(self.k, row_two, EIGHTH, 0, D)
            else:
                here = final(self.k, row_one, 2 * EIGHTH)
            return send(self.u, 6, here, here, "w" if self.first_x else "e")

        def back_last(self):
            if self.first_x:
                here = final(self.k, row_one, 2 * EIGHTH, 0, D)
            else:
                here = final(self.k, 0, SHARD)
            send_last(here, here, "e" if self.first_x else "x")
            done.add(here)

        def step(self, n):
            if n == 1:
                for i in range(2):
                    self.one(i).start()
            if n == 2:
                wait_rows(self.u, 1, 4 * EIGHTH)
                for i in range(2):
                    add_to(cut(self.k, 2 * i + c, row_one, 2 * EIGHTH), self.one_in(i))
                    for side in range(2):
                        self.two(i, side).start()
            if n == 3:
                wait_rows(self.u, 2, 2 * EIGHTH)
                for i in range(2):
                    for side in range(2):
                        here = cut(self.k, 2 * i + c, row_two, EIGHTH, side * HALF, HALF)
                        add_to(here, self.two_in(i, side))
                    self.x_sum(i).start()
            if n == 4:
                wait_rows(self.u, 3, EIGHTH)
                for i in range(2):
                    here = cut(self.k, 2 * i + c, row_two, EIGHTH, s * HALF, HALF)
                    add_to(here, self.x_in(i))
                self.last().start()
            if n == 5:
                self.last().wait_recv()
                add_to(self.piece(), self.x_in(2))
                add_far(self.u, 0, self.piece())
                self.own().start()
                self.back(0).start()
            if n == 6:
                self.own().wait()
                self.back(0).wait_recv()
                self.back(1).start()
            if n == 7:
                self.back(1).wait_recv()
                self.back_last()

    class DeepX(Deep):
        first_x = True

    kinds = {"wide": Wide, "cross": Cross, "bounce": Bounce, "line": Line, "deep": Deep, "deep_x": DeepX}
    sums = [kinds[unit[3]](u) for u, unit in enumerate(UNITS)]

    def sum_step(u, n):
        if n == 0:
            for i in range(2):
                core_sum(u, i).start()
            return
        if n == 1:
            k, row, count, _ = UNITS[u]
            wait_rows(u, 0, 2 * count)
            for i in range(2):
                add_to(cut(k, 2 * i + c, row, count), core_in.at[k, i, pl.ds(row, count)])
        sums[u].step(n)

    def sums_done():
        to_core.wait()
        to_all.wait()
        if done.size:
            done.wait()

        @pl.when(border)
        def _():
            from_border.wait()
            if done_border.size:
                done_border.wait()

        @pl.when(middle)
        def _():
            from_middle.wait()
            kept.wait()
            if done_middle.size:
                done_middle.wait()

    vec_steps = 6 + extra
    vec_moves = []

    def vec_step(n):
        if n == 0:
            top = vec_grads[...]
            high = top.astype(LOW)
            low = (top - high.astype(F32)).astype(LOW)
            for seg in range(GROUPS):
                spread = spread_matrix(seg)
                vec_segs[seg] = dot_turned(high, spread) + dot_turned(low, spread)
            for row, parts in SEGMENTS.items():
                for seg, (q, at) in enumerate(parts):
                    vecs[q, at : at + 1, :] = vec_segs[seg, row : row + 1, :]
            for i in range(2):
                copy = remote(
                    vecs.at[2 * i + 1 - c], vec_in.at[i], v_send.at[3 + i], v_recv.at[3 + i], near["c"]
                )
                copy.start()
                vec_moves.append(copy)
            return
        if n == 1:
            for i in range(2):
                vec_moves[i].wait()
                vecs[2 * i + c] = vecs[2 * i + c] + vec_in[i]
        else:
            vec_moves[-1].wait()
            vecs[mine] = vecs[mine] + vec_in[n]
        steps = [near["y"], near["x"], near["e"], near["w"]] + far
        if n <= len(steps):
            copy = remote(
                vecs.at[yours if n == 1 else mine],
                vec_in.at[1 + n],
                v_send.at[4 + n],
                v_recv.at[4 + n],
                steps[n - 1],
            )
            copy.start()
            vec_moves.append(copy)
        else:
            copy = pltpu.make_async_copy(vecs.at[mine], vec_out, io_sem.at[2])
            copy.start()
            copy.wait()

    forward = [([], vectors_ready), ([], norm_first)]
    forward += [([QKV + n], functools.partial(project_block, n)) for n in range(3)]
    forward += [([], functools.partial(attend, w)) for w in range(windows)]
    forward += [([OUT], attend_out)]
    forward += [([FIN + n], functools.partial(inner_block, n)) for n in range(BLOCKS)]
    forward += [([8, 9, 10, 11], functools.partial(layer_part, 0))]
    forward += [([], functools.partial(layer_part, 1)), ([], layer_sort)]
    forward += [([12, 13], convolve_start), ([14, 15], convolve)]
    for item in GATHER_PLAN:
        if item < 0:
            need, work = forward.pop(0)
            for k in need:
                weight_ready(k)
            work()
        else:
            gather_step(item // 10, item % 10)
    gather_done()

    backward = [functools.partial(convolve_back, side) for side in range(2)] + [layer_back]
    backward += [functools.partial(active_back, n) for n in range(BLOCKS)]
    backward += [inner_sum]
    backward += [
        functools.partial(weight_grad, FIN + n, normed_ffn, slope.at[n]) for n in range(BLOCKS)
    ]
    backward += [hidden_back, context_back]
    backward += [functools.partial(attend_back, w) for w in range(windows)]
    backward += [project_sum]
    backward += [functools.partial(weight_grad, QKV + n, normed, slope.at[n]) for n in range(3)]
    backward += [chars_back]
    backward += [functools.partial(vec_step, n) for n in range(vec_steps)]
    swaps = [functools.partial(swap, 0, mol_v, mols_out, mols)]
    for part in range(SWAP_PARTS):
        swaps.append(functools.partial(swap, 1, context, chars_out, rows, part, SWAP_PARTS))
    for item in PLAN:
        if item == -1:
            backward.pop(0)()
        elif item == -2:
            swaps.pop(0)()
        else:
            sum_step(item // 10, item % 10)
    for work in backward:
        work()
    sums_done()
    swaps_done()


def run(args, chars, extra):
    rows = chars.shape[0] // 2
    mols = rows // KERNEL
    anywhere = pl.BlockSpec(memory_space=pl.ANY)
    dma = pltpu.SemaphoreType.DMA
    vmem = pltpu.VMEM
    windows = rows // WIN
    return pl.pallas_call(
        functools.partial(program_kernel, rows, extra),
        name="layer_and_sums",
        out_shape=[
            jax.ShapeDtypeStruct((2 * mols, HALF), LOW),
            jax.ShapeDtypeStruct((2 * rows, HALF), LOW),
            jax.ShapeDtypeStruct(VEC, F32),
        ]
        + [jax.ShapeDtypeStruct(shape, LOW) for shape in SHARD_SHAPES]
        + [jax.ShapeDtypeStruct((len(UNITS), extra, SHARD, D), LOW)] * (extra > 0),
        in_specs=[anywhere, pl.BlockSpec(memory_space=vmem)] + [anywhere] * (len(args) - 2),
        out_specs=[anywhere] * (8 + (extra > 0)),
        scratch_shapes=[vmem((n * SHARD,), LOW) for n in VEC_COUNTS]
        + [
            vmem((COUNT * D, D), LOW),
            vmem((COUNT, 2, SHARD, D), LOW),
            vmem((COUNT, SHARD, D), LOW),
            vmem((COUNT, SHARD, HALF), LOW),
            vmem((COUNT, SHARD, HALF), LOW),
            vmem((COUNT, SHARD, HALF), LOW),
            vmem((max(len(LINES), 1), SHARD // 2, D), LOW),
            vmem(VEC, F32),
            vmem((GROUPS,) + VEC, F32),
            vmem((GROUPS,) + VEC, F32),
            vmem((VEC[0], D), F32),
            vmem((VEC[0], D), F32),
            vmem((7 + extra,) + VEC, F32),
            vmem((rows, D), LOW),
            vmem((mols, D), LOW),
            vmem((rows, D), LOW),
            vmem((3, rows, D), LOW),
            vmem((windows, PAIRS, 2 * WIN, WIN), LOW),
            vmem((rows, D), LOW),
            vmem((rows, D), F32),
            vmem((rows, D), LOW),
            vmem((BLOCKS, rows, D), LOW),
            vmem((BLOCKS, rows, D), LOW),
            vmem((rows, D), F32),
            vmem((KERNEL, mols, D), LOW),
            vmem((rows, D), LOW),
            vmem((rows, D), F32),
            vmem((mols, D), LOW),
            dma((1,)),
            dma((3, len(PIECES))),
            dma((COUNT,)),
            dma((8,)),
            dma((SEMS,)),
            dma((len(UNITS), extra) if extra else (1, 1)),
            dma((len(UNITS), extra) if extra else (1, 1)),
            dma((9 + extra,)),
            dma((9 + extra,)),
            dma((5 + len(VEC_COUNTS),)),
            dma((4,)),
        ],
        compiler_params=pltpu.CompilerParams(
            collective_id=0, has_side_effects=True, vmem_limit_bytes=63 << 20
        ),
    )(*args)


def finish_kernel(mols, layer, vec, *refs):
    count = len(VEC_COUNTS)
    sums, (mols_out, layer_out), refs = refs[:5], refs[5:7], refs[7:]
    outs, vec_outs, flat, refs = refs[:5], refs[5 : 5 + count], refs[5 + count : 5 + 2 * count], refs[5 + 2 * count :]
    low, wide, load, store, whole, vec_sem, vec_held, mols_held, layer_held = refs
    loads = [
        pltpu.make_async_copy(shard_block(sums, k, 0, SHARD), low.at[k], load.at[k])
        for k in range(COUNT)
    ]
    through = [
        pltpu.make_async_copy(vec, vec_held, whole.at[2]),
        pltpu.make_async_copy(mols, mols_held, whole.at[0]),
        pltpu.make_async_copy(layer, layer_held, whole.at[1]),
    ]
    for copy in through + loads:
        copy.start()
    through[0].wait()
    at = 0
    copies = []
    for i, (ref, there, rows_held) in enumerate(zip(flat, vec_outs, VEC_COUNTS)):
        for j in range(rows_held):
            line = vec_held[at : at + 1, :][:, :SHARD].reshape(SHARD)
            ref[j * SHARD : (j + 1) * SHARD] = line
            at += 1
        copies.append(pltpu.make_async_copy(ref, there, vec_sem.at[i]))
        copies[-1].start()
    backs = [
        pltpu.make_async_copy(mols_held, mols_out, whole.at[0]),
        pltpu.make_async_copy(layer_held, layer_out, whole.at[1]),
    ]
    for before, after in zip(through[1:], backs):
        before.wait()
        after.start()
    for k in range(COUNT):
        loads[k].wait()
        wide[k] = low[k].astype(F32)
        copy = pltpu.make_async_copy(wide.at[k], shard_block(outs, k, 0, SHARD), store.at[k])
        copy.start()
        copies.append(copy)
    for copy in copies + backs:
        copy.wait()


def finish(mols, layer, vec, sums):
    anywhere = pl.BlockSpec(memory_space=pltpu.HBM)
    shape = jax.ShapeDtypeStruct
    vmem, dma = pltpu.VMEM, pltpu.SemaphoreType.DMA
    out = pl.pallas_call(
        finish_kernel,
        name="widen_sums",
        out_shape=[shape(mols.shape, LOW), shape(layer.shape, LOW)]
        + [shape(w.shape, F32) for w in sums]
        + [shape((n * SHARD,), F32) for n in VEC_COUNTS],
        in_specs=[anywhere] * 8,
        out_specs=[anywhere] * (7 + len(VEC_COUNTS)),
        scratch_shapes=[vmem((n * SHARD,), F32) for n in VEC_COUNTS]
        + [
            vmem((COUNT, SHARD, D), LOW),
            vmem((COUNT, SHARD, D), F32),
            dma((COUNT,)),
            dma((COUNT,)),
            dma((3,)),
            dma((len(VEC_COUNTS),)),
            vmem(VEC, F32),
            vmem(mols.shape, LOW),
            vmem(layer.shape, LOW),
        ],
        compiler_params=pltpu.CompilerParams(vmem_limit_bytes=60 << 20),
    )(mols, layer, vec, *sums)
    return out[0], out[1], out[2:7], out[7:]


def body(
    chars,
    char_codes,
    mol_cotangent,
    attn_norm_gain,
    attn_norm_bias,
    qkv_weight,
    qv_bias,
    out_weight,
    out_bias,
    ffn_norm_gain,
    ffn_norm_bias,
    ffn_in_weight,
    ffn_in_bias,
    ffn_out_weight,
    ffn_out_bias,
    conv_weight,
    conv_bias,
    down_norm_gain,
    down_norm_bias,
):
    vectors = [
        attn_norm_gain,
        attn_norm_bias,
        qv_bias,
        out_bias,
        ffn_norm_gain,
        ffn_norm_bias,
        ffn_in_bias,
        ffn_out_bias,
        conv_bias,
        down_norm_gain,
        down_norm_bias,
    ]
    result = run(
        (
            chars,
            char_codes.reshape(-1, WIN),
            mol_cotangent,
            qkv_weight,
            out_weight,
            ffn_in_weight,
            ffn_out_weight,
            conv_weight,
            *vectors,
        ),
        chars,
        (lax.axis_size("replica") // RING).bit_length() - 1,
    )
    molecules, chars_grad, big, v = finish(*result[:3], result[3:8])
    t_qkv, t_out, t_in, t_ffo, t_conv = big
    return (
        molecules,
        chars_grad,
        v[0],
        v[1],
        t_qkv,
        v[2],
        t_out,
        v[3],
        v[4],
        v[5],
        t_in,
        v[6],
        t_ffo,
        v[7],
        t_conv,
        v[8],
        v[9],
        v[10],
    )


def solution(mesh):
    return jax.shard_map(
        body,
        mesh=mesh,
        in_specs=(
            P(("group", "replica"), None),
            P(("group", "replica")),
            P(("group", "replica"), None),
            P("group"),
            P("group"),
            P("group", None),
            P("group"),
            P("group", None),
            P("group"),
            P("group"),
            P("group"),
            P("group", None),
            P("group"),
            P("group", None),
            P("group"),
            P("group", None),
            P("group"),
            P("group"),
            P("group"),
        ),
        out_specs=(
            P(("group", "replica"), "section"),
            P(("group", "replica"), "section"),
            P("group"),
            P("group"),
            P("group", None),
            P("group"),
            P("group", None),
            P("group"),
            P("group"),
            P("group"),
            P("group", None),
            P("group"),
            P("group", None),
            P("group"),
            P("group", None),
            P("group"),
            P("group"),
            P("group"),
        ),
        check_vma=False,
    )
```

```python
import functools
import math

import jax
import jax.numpy as jnp
from jax import lax
from jax.experimental import pallas as pl
from jax.experimental.pallas import tpu as pltpu
from jax.sharding import PartitionSpec as P

D = 768
HEADS = 12
HEAD_DIM = 64
FF = 3072
WIN = 128
KERNEL = 4
GROUPS = 4
RING = 4
SHARD = D // GROUPS
THIRD = SHARD // 3
EIGHTH = SHARD // 4
HALF = D // 2
TILE = 768
PAIR = 2 * HEAD_DIM
PAIRS = HEADS // 2
RUN = WIN // KERNEL
BLOCKS = FF // D
VEC = (16, 256)
VEC_COUNTS = (1, 1, 2, 1, 1, 1, 4, 1, 1, 1, 1)
SCRATCH = 30
norm_eps = 1e-06
mask_value = -10000.0
MESH = pl.DeviceIdType.MESH
F32 = jnp.float32
LOW = jnp.bfloat16

CHUNKS = (
    [(0, "col", j) for j in range(3)]
    + [(1, "col", 0)]
    + [(2, "col", j) for j in range(4)]
    + [(3, "row", j) for j in range(4)]
    + [(4, "row", j) for j in range(4)]
)
COUNT = len(CHUNKS)
QKV, OUT, FIN, FOUT, CONV = BASES = (0, 3, 4, 8, 12)
SHARD_SHAPES = [(SHARD, 3 * D), (SHARD, D), (SHARD, FF), (FF // GROUPS, D), (D, D)]

A_GAIN, A_BIAS, Q_BIAS, V_BIAS, O_BIAS, F_GAIN, F_BIAS = range(7)
IN_BIAS, FO_BIAS, C_BIAS, D_GAIN, D_BIAS = 7, 11, 12, 13, 14


def segments():
    table = {}
    for row, at in zip((A_GAIN, A_BIAS, O_BIAS, F_GAIN, F_BIAS), (0, 1, 4, 5, 6)):
        table[row] = [(q, at) for q in range(GROUPS)]
    table[Q_BIAS] = [(0, 2), (0, 3), (1, 2), (1, 3)]
    table[V_BIAS] = [(2, 2), (2, 3), (3, 2), (3, 3)]
    for n in range(BLOCKS):
        table[IN_BIAS + n] = [(n, 7 + i) for i in range(4)]
    for row, at in zip((FO_BIAS, C_BIAS, D_GAIN, D_BIAS), (11, 12, 13, 14)):
        table[row] = [(q, at) for q in range(GROUPS)]
    return table


SEGMENTS = segments()

PIECES = [
    (0, 0, 1, 3), (1, 0, 1, 3), (2, 0, 1, 3), (3, 0, 1, 3), (4, 0, 1, 3), (5, 0, 1, 3), (6,
    0, 1, 3), (7, 0, 1, 3), (8, 0, 1, 3), (9, 0, 1, 3), (10, 0, 1, 3), (11, 0, 1, 3), (12,
    0, 1, 3), (13, 0, 1, 3), (14, 0, 2, 3), (14, 1, 2, 3), (15, 0, 2, 3), (15, 1, 2, 3),
]
GATHER_PLAN = [
    -1, -1, 0, 10, 1, 20, 11, 30, 2, 21, 40, -1, 12, 31, 50, 22, 41, 60, -1, -1, 32, 51, 70,
    -1, -1, 42, 61, 80, -1, 52, 71, 90, -1, -1, 62, 81, 100, -1, 72, 91, 110, -1, 82, 101,
    120, -1, 130, 92, 111, 140, -1, 150, 102, 121, 160, 170, 112, 131, 141, -1, 122, 151,
    161, -1, 132, 142, 171, -1, 152, -1, 162, 172, -1,
]

UNITS = [
    (12, 0, 192, "line"),
    (13, 0, 192, "wide"),
    (14, 0, 192, "bounce"),
    (15, 0, 192, "bounce"),
    (8, 0, 96, "cross"),
    (8, 96, 96, "cross"),
    (9, 0, 96, "bounce"),
    (9, 96, 96, "line"),
    (10, 0, 96, "cross"),
    (10, 96, 96, "line"),
    (11, 0, 96, "line"),
    (11, 96, 96, "line"),
    (4, 0, 192, "cross"),
    (5, 0, 192, "line"),
    (6, 0, 192, "bounce"),
    (7, 0, 96, "bounce"),
    (7, 96, 96, "bounce"),
    (3, 0, 64, "line"),
    (3, 64, 64, "cross"),
    (3, 128, 64, "bounce"),
    (0, 0, 48, "cross"),
    (0, 48, 48, "cross"),
    (0, 96, 48, "cross"),
    (0, 144, 48, "cross"),
    (1, 0, 64, "line"),
    (1, 64, 64, "line"),
    (1, 128, 64, "line"),
    (2, 0, 64, "wide"),
    (2, 64, 64, "bounce"),
    (2, 128, 64, "bounce"),
]

SEM_COUNT = {"wide": 5, "cross": 5, "bounce": 5, "line": 6, "deep": 8, "deep_x": 8}
SEM_AT = [sum(SEM_COUNT[unit[3]] for unit in UNITS[:u]) for u in range(len(UNITS))]
SEMS = sum(SEM_COUNT[unit[3]] for unit in UNITS)
LINES = sorted({unit[0] for unit in UNITS if unit[3] == "line"})
SWAP_PARTS = 4
PLAN = [
    -1, -1, -2, -1, -1, -1, -1, -1, -1, -1, 2, 12, -1, 22, 32, -1, -1, -1, 60, 40, 50, 13,
    70, 100, 110, 80, 61, 90, 41, -1, 3, 23, 51, 101, 111, 71, 33, 14, 62, 81, 91, -1, 120,
    -1, 4, 130, 24, 102, 121, 42, -1, 131, 15, 34, 140, 112, 52, 63, -1, 150, 160, 141, 103,
    25, -1, 72, 16, 35, 151, 161, 92, 113, 5, 104, 64, 82, 26, 43, -1, 114, 73, 190, 36,
    180, 170, -1, 6, 181, 171, 191, 132, 93, 122, 65, 44, -1, 53, 27, 74, -1, 37, 94, 66,
    105, 115, 45, -1, 133, 182, 142, 67, 106, 75, -1, 54, 116, 152, 46, 95, -1, 200, 210,
    220, 230, 134, 162, -1, 201, 211, 221, 153, 231, 76, 83, 143, 172, 240, 250, 96, 260,
    55, -1, 154, 280, 290, 135, 192, 270, 163, 84, 281, 291, 241, 251, 202, 123, 271, 56,
    155, 183, 261, 212, 144, -1, 136, 282, 173, 222, -2, 232, -2, 292, -2, 164, -2, -1, 156,
    85, 193, -1, 242, 283, 145, 124, 252, 174, 184, 86, 203, 194, 165, 272, 243, 146, 293,
    284, 125, 262, 166, 213, 185, 223, 253, 195, 233, 204, -1, 244, 157, 294, 285, 126, 254,
    263, 186, 205, 175, 214, 196, 295, 224, 273, 286, 234, 264, 206, 147, 176, 215, 274,
    167, 296, 225, -1, 235, 245, 216, 275, 255, 226, 236, 246, 265, -1, 197, 256, 276, 287,
    266, 297, -1,
]


def at16(value):
    return pl.multiple_of(value, 16)


def at128(value):
    return pl.multiple_of(value, 128)


def spot(chunk, shard, first=0):
    mat, kind, j = CHUNKS[chunk]
    if kind == "col":
        return at16((BASES[mat] + j) * D + shard * SHARD + first)
    return at16((BASES[mat] + shard) * D + j * SHARD + first)


def shard_block(refs, chunk, first, rows, col=0, cols=D):
    mat, kind, j = CHUNKS[chunk]
    if kind == "col":
        return refs[mat].at[pl.ds(at16(first), rows), pl.ds(at128(j * D + col), cols)]
    return refs[mat].at[pl.ds(at16(j * SHARD + first), rows), pl.ds(at128(col), cols)]


def remote(src, dst, send, recv, target):
    return pltpu.make_async_remote_copy(
        src_ref=src,
        dst_ref=dst,
        send_sem=send,
        recv_sem=recv,
        device_id=target,
        device_id_type=MESH,
    )


class Tally:
    def __init__(self, sem, yard):
        self.sem, self.yard, self.size = sem, yard, 0

    def add(self, ref):
        self.size += math.prod(ref.shape)

    def wait(self):
        here = self.yard.at[pl.ds(0, self.size // D)]
        pltpu.make_async_copy(here, here, self.sem).wait()
        self.size = 0


class Move:
    def __init__(self, src, dst, sent, recv, target):
        self.src, self.dst, self.sent = src, dst, sent
        self.copy = remote(src, dst, sent.sem, recv, target)

    def start(self):
        self.sent.add(self.src)
        self.copy.start()

    def wait_recv(self):
        self.copy.wait_recv()


def add_to(dst, src):
    rows = next(n for n in (48, 32, 16) if dst.shape[0] % n == 0)

    @pl.loop(0, dst.shape[0] // rows)
    def _(i):
        here = pl.ds(at16(i * rows), rows)
        dst[here, :] = dst[here, :] + src[here, :]


def dot(left, right):
    return jnp.dot(left, right, preferred_element_type=F32)


def dot_rows(left, right):
    return lax.dot_general(left, right, (((0,), (0,)), ((), ())), preferred_element_type=F32)


def dot_turned(left, right):
    return lax.dot_general(left, right, (((1,), (1,)), ((), ())), preferred_element_type=F32)


def normalized(values):
    center = values - jnp.mean(values, axis=-1, keepdims=True)
    scale = lax.rsqrt(jnp.mean(center * center, axis=-1, keepdims=True) + norm_eps)
    return center * scale, scale


def norm_back(unit, scale, gain, grad):
    grad_unit = grad * gain
    mean_grad = jnp.mean(grad_unit, axis=-1, keepdims=True)
    mean_both = jnp.mean(grad_unit * unit, axis=-1, keepdims=True)
    return scale * (grad_unit - mean_grad - unit * mean_both)


def gelu_parts(values):
    half = 0.5 * lax.erf(values * (0.5**0.5)) + 0.5
    bell = jnp.exp(-0.5 * values * values) * 0.3989422804014327
    return values * half, half + values * bell


def column_sum(values):
    return jnp.sum(values, axis=0, keepdims=True)


def program_kernel(rows, extra, *refs):
    count = len(VEC_COUNTS)
    (chars, codes, cotangent) = refs[:3]
    shards = refs[3:8]
    vectors = refs[8 : 8 + count]
    mols_out, chars_out, vec_out = refs[8 + count : 11 + count]
    out = refs[11 + count : 16 + count]
    more_in = refs[16 + count] if extra else None
    refs = refs[16 + count + (extra > 0) :]
    flat, refs = refs[:count], refs[count:]
    (
        held,
        core_in,
        y_in,
        x_in,
        e_in,
        m_in,
        line_in,
        vec,
        vecs,
        vec_segs,
        rows_f32,
        vec_grads,
        vec_in,
        chars_v,
        cot_v,
        normed,
        projected,
        probs,
        context,
        hidden,
        normed_ffn,
        slope,
        active,
        layer,
        stacked,
        low_grad,
        total,
        mol_v,
        near_rows,
        near_grads,
    ) = refs[:SCRATCH]
    (
        w_send,
        w_recv,
        c_recv,
        g_send,
        g_recv,
        more_send,
        more_recv,
        v_send,
        v_recv,
        io_sem,
        swap_sem,
        f_send,
        f_recv,
    ) = refs[SCRATCH:]
    windows = rows // WIN
    mols = rows // KERNEL
    s, g, r = lax.axis_index("section"), lax.axis_index("group"), lax.axis_index("replica")
    near = {
        "c": (s, g ^ 1, r),
        "y": (s, g ^ 2, r),
        "x": (1 - s, g, r),
        "e": (s, g, r ^ 1),
        "m": (s, g, r ^ 3),
        "d": (s, g ^ 3, r),
        "w": (s, g, r ^ 2),
    }
    far = [(s, g, r ^ (RING << i)) for i in range(extra)]
    place = lax.rem(r, RING)
    even = lax.rem(r, 2) == 0
    middle = jnp.logical_or(place == 1, place == 2)
    border = jnp.logical_not(middle)

    barrier = pltpu.get_barrier_semaphore()
    greeted = list(near.values()) + far
    for target in greeted:
        pl.semaphore_signal(barrier, inc=1, device_id=target, device_id_type=MESH)

    flat_copies = [
        pltpu.make_async_copy(src, dst, io_sem.at[5 + i])
        for i, (src, dst) in enumerate(zip(vectors, flat))
    ]
    for copy in flat_copies:
        copy.start()
    vec[...] = jnp.zeros_like(vec)
    vec_grads[...] = jnp.zeros_like(vec_grads)
    vec_segs[...] = jnp.zeros_like(vec_segs)
    at = 0
    for copy, values, rows_held in zip(flat_copies, flat, VEC_COUNTS):
        copy.wait()
        wide = values[...].astype(F32)
        for i in range(rows_held):
            line = wide[i * SHARD : (i + 1) * SHARD].reshape(1, SHARD)
            vec[at : at + 1, pl.ds(0, SHARD)] = line
            at += 1
    pl.semaphore_wait(barrier, len(greeted))

    y_third = jnp.where(even, s, 2)
    z_third = jnp.where(even, 2, s)
    x_third = 1 - s
    other = g ^ 2

    own_vec = pltpu.make_async_copy(vec, vecs.at[g], io_sem.at[2])
    vec_copies = [
        remote(vec, vecs.at[g], v_send.at[i], v_recv.at[i], near[way])
        for i, way in enumerate("cyd")
    ]
    for copy in vec_copies + [own_vec]:
        copy.start()

    sent = Tally(w_send.at[0], held)

    def rows_by(u, way):
        k, part, parts, ways = PIECES[u]
        if ways == 2:
            count = SHARD // parts
            which = s if way == "y" else 1 - s
            return k, part * count + which * (count // 2), count // 2
        third = {"y": y_third, "z": z_third, "x": x_third}[way]
        return k, third * THIRD + part * (THIRD // parts), THIRD // parts

    def arrived(u, way):
        k, first, count = rows_by(u, way)
        return held.at[pl.ds(spot(k, other, first), count)]

    def hop(u, way, src_way):
        here = arrived(u, src_way)
        i = "yxz".index(way)
        return Move(here, here, sent, w_recv.at[i, u], near["yxe"[i]])

    def first_hop(u):
        k, first, count = rows_by(u, "y")
        src = shard_block(shards, k, first, count)
        there = held.at[pl.ds(spot(k, g, first), count)]
        return Move(src, there, sent, w_recv.at[0, u], near["y"])

    def core_own(k):
        src = shard_block(shards, k, 0, SHARD)
        there = held.at[pl.ds(spot(k, g), SHARD)]
        return Move(src, there, sent, c_recv.at[k], near["c"])

    def core_hop(u, way):
        here = arrived(u, way)
        Move(here, here, sent, c_recv.at[PIECES[u][0]], near["c"]).start()

    for u in range(len(PIECES)):
        first_hop(u).start()
    loads = [
        pltpu.make_async_copy(chars.at[pl.ds(at16(s * rows), rows)], chars_v, io_sem.at[0]),
        pltpu.make_async_copy(cotangent.at[pl.ds(at16(s * mols), mols)], cot_v, io_sem.at[1]),
    ]
    for copy in loads:
        copy.start()
    for k in range(COUNT):
        own_block = held.at[pl.ds(spot(k, g), SHARD)]
        pltpu.make_async_copy(shard_block(shards, k, 0, SHARD), own_block, c_recv.at[k]).start()
        core_own(k).start()

    def gather_step(u, n):
        two = PIECES[u][3] == 2
        if n == 0:
            hop(u, "y", "y").wait_recv()
            if two:
                hop(u, "x", "y").start()
            else:
                hop(u, "z", "y").start()

                @pl.when(even)
                def _():
                    hop(u, "x", "y").start()

            core_hop(u, "y")
        if n == 1:
            hop(u, "z", "z").wait_recv()

            @pl.when(jnp.logical_not(even))
            def _():
                hop(u, "x", "z").copy.start()

            core_hop(u, "z")
        if n == 2:
            hop(u, "x", "x").wait_recv()
            core_hop(u, "x")

    def weight_ready(k):
        here = held.at[pl.ds(0, 3 * SHARD)]
        pltpu.make_async_copy(here, here, c_recv.at[k]).wait()

    def gather_done():
        sent.wait()

    def spread_matrix(seg):
        i = lax.broadcasted_iota(jnp.int32, (VEC[1], D), 0)
        j = lax.broadcasted_iota(jnp.int32, (VEC[1], D), 1)
        hit = jnp.logical_and(j == i + seg * SHARD, i < SHARD)
        return jnp.where(hit, 1.0, 0.0).astype(LOW)

    def vectors_ready():
        own_vec.wait()
        for copy in vec_copies:
            copy.wait()
        for row, parts in SEGMENTS.items():
            for seg, (q, at) in enumerate(parts):
                vec_segs[seg, row : row + 1, :] = vecs[q, at : at + 1, :]
        full = jnp.zeros((VEC[0], D), F32)
        for seg in range(GROUPS):
            full = full + dot(vec_segs[seg].astype(LOW), spread_matrix(seg))
        rows_f32[...] = full

    def vector(row):
        return rows_f32[row : row + 1, :]

    def vector_tile(row, j):
        return rows_f32[row : row + 1, pl.ds(at128(j * TILE), TILE)]

    def block(n, j=None):
        start = n * D
        if not isinstance(n, int):
            start = at16(start)
        if j is None:
            return held[pl.ds(start, D), :]
        return held[pl.ds(start, D), pl.ds(at128(j * TILE), TILE)]

    def row_tiles(body):
        @pl.loop(0, rows // WIN)
        def _(i):
            body(pl.ds(at128(i * WIN), WIN), i)

    def col_tiles(body):
        @pl.loop(0, D // TILE)
        def _(j):
            body(pl.ds(at128(j * TILE), TILE), j)

    def norm_first():
        loads[0].wait()

        def one(here, i):
            unit, _ = normalized(chars_v[here, :].astype(F32))
            normed[here, :] = (unit * vector(A_GAIN) + vector(A_BIAS)).astype(LOW)

        row_tiles(one)

    def project_block(n):
        def one(here, j):
            value = dot(normed[...], block(QKV + n, j))
            if n == 0:
                value = value + vector_tile(Q_BIAS, j)
            if n == 2:
                value = value + vector_tile(V_BIAS, j)
            projected[n, :, here] = value.astype(LOW)

        col_tiles(one)

    def key_bias(w):
        code = codes[pl.ds(s * windows + w, 1), :]
        return jnp.where(code != 0, 0.0, mask_value).astype(F32)

    def lanes():
        return lax.broadcasted_iota(jnp.int32, (WIN, PAIR), 1) < HEAD_DIM

    def two_heads(values):
        first = lanes()
        zero = jnp.zeros_like(values)
        return jnp.concatenate(
            [jnp.where(first, values, zero), jnp.where(first, zero, values)], axis=0
        )

    def one_pair(values):
        return jnp.where(lanes(), values[:WIN], values[WIN:])

    scale_factor = HEAD_DIM ** (-0.5)

    def attend(w):
        here = pl.ds(w * WIN, WIN)
        bias = key_bias(w)
        for p in range(PAIRS):
            cols = pl.ds(p * PAIR, PAIR)
            queries = two_heads(projected[0, here, cols])
            scores = dot_turned(queries, projected[1, here, cols]) * scale_factor + bias
            top = jnp.max(scores, axis=-1, keepdims=True)
            weight = jnp.exp(scores - top)
            weight = weight / jnp.sum(weight, axis=-1, keepdims=True)
            prob = weight.astype(LOW)
            probs[w, p] = prob
            context[here, cols] = one_pair(dot(prob, projected[2, here, cols])).astype(LOW)

    def attend_out():
        def one(here, j):
            value = dot(context[...], block(OUT, j)) + vector_tile(O_BIAS, j)
            hidden[:, here] = chars_v[:, here].astype(F32) + value

        col_tiles(one)

        def norm(here, i):
            unit, _ = normalized(hidden[here, :])
            normed_ffn[here, :] = (unit * vector(F_GAIN) + vector(F_BIAS)).astype(LOW)

        row_tiles(norm)

    def inner_block(n):
        def one(here, j):
            value = dot(normed_ffn[...], block(FIN + n, j)) + vector_tile(IN_BIAS + n, j)
            gelu, grad = gelu_parts(value)
            active[n, :, here] = gelu.astype(LOW)
            slope[n, :, here] = grad.astype(LOW)

        col_tiles(one)

    def by_place():
        i = lax.broadcasted_iota(jnp.int32, (WIN, WIN), 0)
        j = lax.broadcasted_iota(jnp.int32, (WIN, WIN), 1)
        return jnp.where(j == KERNEL * lax.rem(i, RUN) + i // RUN, 1.0, 0.0).astype(LOW)

    def layer_part(side):
        cols = pl.ds(side * HALF, HALF)
        value = hidden[:, cols] + rows_f32[FO_BIAS : FO_BIAS + 1, cols]
        for n in range(BLOCKS):
            value = value + dot(active[n], held[pl.ds((FOUT + n) * D, D), cols])
        low_grad[:, cols] = value.astype(LOW)

    def layer_sort():
        order = by_place()

        def sort(here, w):
            moved = dot(order, low_grad[here, :]).astype(LOW)
            for k in range(KERNEL):
                stacked[k, pl.ds(at16(w * RUN), RUN), :] = moved[k * RUN : (k + 1) * RUN]

        row_tiles(sort)
        give_rows()

    def note(row, value):
        vec_grads[row : row + 1, :] = value

    def note_more(row, value):
        vec_grads[row : row + 1, :] = vec_grads[row : row + 1, :] + value

    factors = Tally(f_send.at[0], held)
    ways = {1: "c", 2: "y", 3: "d"}

    def slot(i):
        return pl.ds(i * mols, mols)

    def give_rows():
        near_rows[slot(0), :] = stacked[g]
        for i in (2, 3, 1):
            there = near_rows.at[slot(i)]
            move = Move(stacked.at[g ^ i], there, factors, f_recv.at[i - 1], near[ways[i]])
            move.start()

    def grads_move(i, src, way):
        there = near_grads.at[slot(i)]
        return Move(near_grads.at[slot(src)], there, factors, f_recv.at[2 + i], near[way])

    def give_grads():
        grads_move(2, 0, "y").start()
        grads_move(1, 0, "c").start()

    def pass_grads():
        grads_move(2, 0, "y").wait_recv()
        grads_move(3, 2, "c").start()

    def convolve_grad(side):
        if side == 0:
            for i in (1, 3):
                grads_move(i, 0, "c").wait_recv()
            for i in (1, 2, 3):
                here = near_rows.at[slot(i)]
                Move(here, here, factors, f_recv.at[i - 1], near["c"]).wait_recv()
        value = dot_rows(near_rows[:, side * HALF : (side + 1) * HALF], near_grads[...])
        held[pl.ds(at16((CONV + g) * D + side * HALF), HALF), :] = value.astype(LOW)

    def convolve_part(side):
        cols = pl.ds(side * HALF, HALF)
        value = 0.0
        for k in range(KERNEL):
            here = pl.ds((CONV + k) * D + side * HALF, HALF)
            value = value + dot(stacked[k, :, cols], held[here, :])
        return value

    first_mols = pl.ds(0, mols)

    def convolve_start():
        total[first_mols, :] = convolve_part(0) + vector(C_BIAS)

    def convolve():
        loads[1].wait()
        gelu, grad = gelu_parts(total[first_mols, :] + convolve_part(1))
        unit, scale = normalized(gelu)
        grad_unit = norm_back(unit, scale, vector(D_GAIN), cot_v[...].astype(F32))
        near_grads[first_mols, :] = (grad_unit * grad).astype(LOW)
        give_grads()
        layer[first_mols, :] = unit

    def convolve_end():
        unit = layer[first_mols, :]
        wide = cot_v[...].astype(F32)
        note(D_GAIN, column_sum(wide * unit))
        note(D_BIAS, column_sum(wide))
        note(C_BIAS, column_sum(near_grads[first_mols, :].astype(F32)))
        mol_v[...] = (unit * vector(D_GAIN) + vector(D_BIAS)).astype(LOW)

    def convolve_back():
        for k in range(KERNEL):
            total[slot(k), :] = dot_turned(near_grads[first_mols, :], block(CONV + k))

    def layer_back():
        convolve_end()
        order = by_place()

        def sort(here, w):
            parts = [total[pl.ds(at16(k * mols + w * RUN), RUN), :] for k in range(KERNEL)]
            value = dot_rows(order, jnp.concatenate(parts, axis=0).astype(LOW))
            layer[here, :] = value
            low_grad[here, :] = value.astype(LOW)
            note_more(FO_BIAS, column_sum(value))

        row_tiles(sort)

    def weight_grad(n, left, right):
        def one(here, j):
            value = dot_rows(left[:, here], right[...])
            held[pl.ds(at128(n * D + j * TILE), TILE), :] = value.astype(LOW)

        col_tiles(one)

    def active_back(n):
        def one(here, j):
            value = dot_turned(
                low_grad[...], held[pl.ds(at128((FOUT + n) * D + j * TILE), TILE), :]
            )
            inner = (value * slope[n, :, here].astype(F32)).astype(LOW)
            slope[n, :, here] = inner
            vec_grads[IN_BIAS + n : IN_BIAS + n + 1, here] = column_sum(inner.astype(F32))

        col_tiles(one)

    def out_grad(n):
        weight_grad(FOUT + n, active.at[n], low_grad)

    def inner_sum():
        def one(here, j):
            value = jnp.zeros((rows, TILE), F32)
            for n in range(BLOCKS):
                value = value + dot_turned(
                    slope[n], held[pl.ds(at128((FIN + n) * D + j * TILE), TILE), :]
                )
            total[:, here] = value

        col_tiles(one)

    def hidden_back():
        def one(here, i):
            unit, scale = normalized(hidden[here, :])
            grad = total[here, :]
            note_more(F_GAIN, column_sum(grad * unit))
            note_more(F_BIAS, column_sum(grad))
            value = layer[here, :] + norm_back(unit, scale, vector(F_GAIN), grad)
            layer[here, :] = value
            low = value.astype(LOW)
            low_grad[here, :] = low
            note_more(O_BIAS, column_sum(low.astype(F32)))

        row_tiles(one)

    def context_back():
        def one(here, j):
            value = dot_turned(low_grad[...], held[pl.ds(at128(OUT * D + j * TILE), TILE), :])
            normed_ffn[:, here] = value.astype(LOW)

        col_tiles(one)
        weight_grad(OUT, context, low_grad)

    def attend_back(w):
        here = pl.ds(w * WIN, WIN)
        for p in range(PAIRS):
            cols = pl.ds(p * PAIR, PAIR)
            grad_out = two_heads(normed_ffn[here, cols])
            prob = probs[w, p]
            wide = prob.astype(F32)
            grad_prob = dot_turned(grad_out, projected[2, here, cols])
            inner = jnp.sum(wide * grad_prob, axis=-1, keepdims=True)
            grad_score = (wide * (grad_prob - inner)).astype(LOW)
            grad_value = dot_rows(prob, grad_out)
            grad_query = one_pair(dot(grad_score, projected[1, here, cols])) * scale_factor
            grad_key = (
                dot_rows(grad_score, two_heads(projected[0, here, cols])) * scale_factor
            )
            low_query, low_value = grad_query.astype(LOW), grad_value.astype(LOW)
            slope[0, here, cols] = low_query
            slope[1, here, cols] = grad_key.astype(LOW)
            slope[2, here, cols] = low_value
            for row, low in ((Q_BIAS, low_query), (V_BIAS, low_value)):
                vec_grads[row : row + 1, cols] = vec_grads[row : row + 1, cols] + column_sum(
                    low.astype(F32)
                )

    def project_sum():
        def one(here, j):
            value = jnp.zeros((rows, TILE), F32)
            for n in range(3):
                value = value + dot_turned(
                    slope[n], held[pl.ds(at128((QKV + n) * D + j * TILE), TILE), :]
                )
            total[:, here] = value

        col_tiles(one)

    def chars_back():
        def one(here, i):
            unit, scale = normalized(chars_v[here, :].astype(F32))
            grad = total[here, :]
            note_more(A_GAIN, column_sum(grad * unit))
            note_more(A_BIAS, column_sum(grad))
            value = layer[here, :] + norm_back(unit, scale, vector(A_GAIN), grad)
            context[here, :] = value.astype(LOW)

        row_tiles(one)

    def swap(i, whole, dst, count, part=0, parts=1):
        here = pl.ds(part * (count // parts), count // parts)
        keep = whole.at[here, pl.ds(at128(s * HALF), HALF)]
        give = whole.at[here, pl.ds(at128((1 - s) * HALF), HALF)]
        there = dst.at[pl.ds(at16(s * count + part * (count // parts)), count // parts)]
        stay = pltpu.make_async_copy(keep, there, swap_sem.at[2 * i])
        go = remote(give, there, swap_sem.at[2 * i], swap_sem.at[2 * i + 1], near["x"])
        stay.start()
        go.start()

    def swaps_done():
        for i, whole in enumerate((mol_v, context)):
            pltpu.make_async_copy(whole, whole, swap_sem.at[2 * i]).wait()
            here = whole.at[:, pl.ds(0, HALF)]
            pltpu.make_async_copy(here, here, swap_sem.at[2 * i + 1]).wait()

    c = lax.rem(g, 2)
    y = g // 2
    mine, yours = 2 * y + c, 2 * (1 - y) + c
    z_half, w_half = lax.rem(r, 2), lax.rem(r // 2, 2)
    row_one = z_half * EIGHTH * 2
    row_two = row_one + w_half * EIGHTH

    to_core, to_all = Tally(g_send.at[0], held), Tally(g_send.at[1], held)
    from_border, from_middle = Tally(g_send.at[2], held), Tally(g_send.at[3], held)
    kept = Tally(g_send.at[4], held)
    done, done_border = Tally(g_send.at[5], held), Tally(g_send.at[6], held)
    done_middle = Tally(g_send.at[7], held)

    def send(u, i, src, dst, way, sender=to_all):
        return Move(src, dst, sender, g_recv.at[SEM_AT[u] + i], near[way])

    def send_last(src, dst, way, sender=to_all, ends=done):
        move = Move(src, dst, sender, ends.sem, near[way])
        move.start()

    def cut(k, q, row, count, col=0, cols=D):
        return held.at[pl.ds(spot(k, q, row), count), pl.ds(at128(col), cols)]

    def final(k, row, count, col=None, cols=HALF):
        return shard_block(out, k, row, count, s * HALF if col is None else col, cols)

    def add_far(u, row, here):
        k = UNITS[u][0]
        count, cols = here.shape
        for i in range(extra):
            there = more_in.at[u, i, pl.ds(0, count), pl.ds(0, cols)]
            near_by = core_in.at[k, 0, pl.ds(row, count), pl.ds(0, cols)]
            copy = remote(here, there, more_send.at[u, i], more_recv.at[u, i], far[i])
            copy.start()
            copy.wait()
            copy = pltpu.make_async_copy(there, near_by, more_send.at[u, i])
            copy.start()
            copy.wait()
            add_to(here, near_by)

    def core_sum(u, i):
        k, row, count, _ = UNITS[u]
        there = core_in.at[k, i, pl.ds(row, count)]
        return send(u, 0, cut(k, 2 * i + 1 - c, row, count), there, "c", to_core)

    def wait_rows(u, i, count):
        here = held.at[pl.ds(0, count)]
        pltpu.make_async_copy(here, here, g_recv.at[SEM_AT[u] + i]).wait()

    def y_sum(u):
        k, row, count, _ = UNITS[u]
        return send(u, 1, cut(k, yours, row, count), y_in.at[k, pl.ds(row, count)], "y")

    def y_added(u):
        k, row, count, _ = UNITS[u]
        if k >= CONV:
            return
        y_sum(u).wait_recv()
        add_to(cut(k, mine, row, count), y_in.at[k, pl.ds(row, count)])

    class Wide:
        def __init__(self, u):
            self.u = u
            self.k, self.row, self.count, _ = UNITS[u]
            self.here = pl.ds(self.row, self.count)
            self.total = m_in.at[self.k, self.here]

        def part(self, side):
            return cut(self.k, mine, self.row, self.count, side * HALF, HALF)

        def done_part(self):
            return final(self.k, self.row, self.count)

        def x_sum(self):
            return send(self.u, 2, self.part(1 - s), x_in.at[self.k, self.here], "x")

        def e_sum(self):
            return send(self.u, 3, self.part(s), e_in.at[self.k, self.here], "e", from_border)

        def m_sum(self):
            return send(self.u, 4, self.part(s), self.total, "m", from_middle)

        def e_back(self):
            return send(self.u, 3, self.total, self.done_part(), "e", from_middle)

        def step(self, n):
            if n == 1:
                y_sum(self.u).start()
            if n == 2:
                y_added(self.u)
                self.x_sum().start()
            if n == 3:
                self.x_sum().wait_recv()
                add_to(self.part(s), x_in.at[self.k, self.here])

                @pl.when(border)
                def _():
                    self.e_sum().start()

            if n == 4:

                @pl.when(middle)
                def _():
                    self.e_sum().wait_recv()
                    add_to(self.part(s), e_in.at[self.k, self.here])
                    self.m_sum().start()

            if n == 5:

                @pl.when(middle)
                def _():
                    self.m_sum().wait_recv()
                    add_to(self.total, self.part(s))
                    add_far(self.u, self.row, self.total)
                    kept.add(self.total)
                    pltpu.make_async_copy(self.total, self.done_part(), kept.sem).start()
                    self.e_back().start()
                    send_last(self.total, self.done_part(), "x", from_middle)

            if n == 6:

                @pl.when(border)
                def _():
                    self.e_back().wait_recv()
                    send_last(self.done_part(), self.done_part(), "x", from_border)

                done.add(self.total)

    class Cross(Wide):
        def both_in(self, i):
            return y_in.at[self.k, self.here, pl.ds(i * HALF, HALF)]

        def both_part(self, i, side):
            return cut(self.k, 2 * i + c, self.row, self.count, side * HALF, HALF)

        def y_sum(self):
            src = cut(self.k, yours, self.row, self.count, s * HALF, HALF)
            return send(self.u, 2, src, x_in.at[self.k, self.here], "y")

        def step(self, n):
            if n == 1:
                for i in range(2):
                    send(self.u, 1, self.both_part(i, 1 - s), self.both_in(i), "x").start()
            elif n == 2:
                wait_rows(self.u, 1, self.count)
                for i in range(2):
                    add_to(self.both_part(i, s), self.both_in(i))
                self.y_sum().start()
            elif n == 3:
                self.y_sum().wait_recv()
                add_to(self.part(s), x_in.at[self.k, self.here])

                @pl.when(border)
                def _():
                    self.e_sum().start()

            else:
                super().step(n)

    class Bounce(Wide):
        def step(self, n):
            if n == 5:

                @pl.when(middle)
                def _():
                    self.m_sum().wait_recv()
                    add_to(self.total, self.part(s))
                    add_far(self.u, self.row, self.total)
                    kept.add(self.total)
                    pltpu.make_async_copy(self.total, self.done_part(), kept.sem).start()
                    self.e_back().start()

            elif n == 6:

                @pl.when(border)
                def _():
                    self.e_back().wait_recv()
                    here = self.done_part()
                    send(self.u, 4, here, here, "x", from_border).start()

            elif n == 7:

                @pl.when(border)
                def _():
                    there = final(self.k, self.row, self.count, (1 - s) * HALF)
                    send(self.u, 4, there, there, "x").wait_recv()
                    send_last(there, there, "e", from_border, done_middle)

                done_middle.add(self.total)
            else:
                super().step(n)

    class Line(Wide):
        def half(self, which):
            return self.row + which * (self.count // 2)

        def rows_of(self, which, side=None):
            col, cols = (0, D) if side is None else (side * HALF, HALF)
            return cut(self.k, mine, self.half(which), self.count // 2, col, cols)

        def done_rows(self, which):
            return final(self.k, self.half(which), self.count // 2, 0, D)

        def e_in(self, side):
            return (x_in, e_in)[side].at[self.k, self.here]

        def m_in(self, side):
            return m_in.at[self.k, pl.ds(self.row + side * (self.count // 2), self.count // 2)]

        def sum_line(self):
            return line_in.at[LINES.index(self.k), pl.ds(self.row // 2, self.count // 2)]

        def x_sum(self):
            return send(self.u, 4, self.rows_of(w_half), self.sum_line(), "x", from_middle)

        def m_back(self):
            return send(self.u, 5, self.sum_line(), self.done_rows(w_half), "m", from_middle)

        def step(self, n):
            if n == 1:
                y_sum(self.u).start()
            if n == 2:
                y_added(self.u)

                @pl.when(border)
                def _():
                    for side in range(2):
                        send(
                            self.u, 2, self.part(side), self.e_in(side), "e", from_border
                        ).start()

            if n == 3:

                @pl.when(middle)
                def _():
                    wait_rows(self.u, 2, self.count)
                    for side in range(2):
                        add_to(self.part(side), self.e_in(side))
                    for side in range(2):
                        src = self.rows_of(1 - w_half, side)
                        send(self.u, 3, src, self.m_in(side), "m", from_middle).start()

            if n == 4:

                @pl.when(middle)
                def _():
                    wait_rows(self.u, 3, self.count // 2)
                    for side in range(2):
                        add_to(self.rows_of(w_half, side), self.m_in(side))
                    self.x_sum().start()

            if n == 5:

                @pl.when(middle)
                def _():
                    self.x_sum().wait_recv()
                    add_to(self.sum_line(), self.rows_of(w_half))
                    add_far(self.u, self.row, self.sum_line())
                    kept.add(self.sum_line())
                    pltpu.make_async_copy(
                        self.sum_line(), self.done_rows(w_half), kept.sem
                    ).start()
                    self.m_back().start()
                    there = self.done_rows(w_half)
                    send_last(self.sum_line(), there, "e", from_middle, done_border)

            if n == 6:

                @pl.when(middle)
                def _():
                    self.m_back().wait_recv()
                    there = self.done_rows(1 - w_half)
                    send_last(there, there, "e", from_middle, done_border)

                for _ in range(2):
                    done_border.add(self.sum_line())

    class Deep:
        first_x = False

        def __init__(self, u):
            self.u = u
            self.k = UNITS[u][0]

        def one(self, i):
            src = cut(self.k, 2 * i + c, (1 - z_half) * EIGHTH * 2, 2 * EIGHTH)
            return send(self.u, 1, src, self.one_in(i), "e")

        def one_in(self, i):
            return y_in.at[self.k, pl.ds(i * 2 * EIGHTH, 2 * EIGHTH)]

        def two(self, i, side):
            row = row_one + (1 - w_half) * EIGHTH
            src = cut(self.k, 2 * i + c, row, EIGHTH, side * HALF, HALF)
            return send(self.u, 2, src, self.two_in(i, side), "w")

        def two_in(self, i, side):
            return x_in.at[self.k, pl.ds((2 * i + side) * EIGHTH, EIGHTH)]

        def x_sum(self, i):
            src = cut(self.k, 2 * i + c, row_two, EIGHTH, (1 - s) * HALF, HALF)
            return send(self.u, 3, src, self.x_in(i), "x")

        def x_in(self, i):
            return e_in.at[self.k, pl.ds(i * EIGHTH, EIGHTH)]

        def last(self):
            src = cut(self.k, yours, row_two, EIGHTH, s * HALF, HALF)
            return send(self.u, 4, src, self.x_in(2), "y")

        def piece(self):
            return cut(self.k, mine, row_two, EIGHTH, s * HALF, HALF)

        def own(self):
            there = final(self.k, row_two, EIGHTH)
            return pltpu.make_async_copy(self.piece(), there, g_recv.at[SEM_AT[self.u] + 7])

        def back(self, n):
            if n == 0:
                way = "x" if self.first_x else "w"
                return send(self.u, 5, self.piece(), final(self.k, row_two, EIGHTH), way)
            if self.first_x:
                here = final(self.k, row_two, EIGHTH, 0, D)
            else:
                here = final(self.k, row_one, 2 * EIGHTH)
            return send(self.u, 6, here, here, "w" if self.first_x else "e")

        def back_last(self):
            if self.first_x:
                here = final(self.k, row_one, 2 * EIGHTH, 0, D)
            else:
                here = final(self.k, 0, SHARD)
            send_last(here, here, "e" if self.first_x else "x")
            done.add(here)

        def step(self, n):
            if n == 1:
                for i in range(2):
                    self.one(i).start()
            if n == 2:
                wait_rows(self.u, 1, 4 * EIGHTH)
                for i in range(2):
                    add_to(cut(self.k, 2 * i + c, row_one, 2 * EIGHTH), self.one_in(i))
                    for side in range(2):
                        self.two(i, side).start()
            if n == 3:
                wait_rows(self.u, 2, 2 * EIGHTH)
                for i in range(2):
                    for side in range(2):
                        here = cut(self.k, 2 * i + c, row_two, EIGHTH, side * HALF, HALF)
                        add_to(here, self.two_in(i, side))
                    self.x_sum(i).start()
            if n == 4:
                wait_rows(self.u, 3, EIGHTH)
                for i in range(2):
                    here = cut(self.k, 2 * i + c, row_two, EIGHTH, s * HALF, HALF)
                    add_to(here, self.x_in(i))
                self.last().start()
            if n == 5:
                self.last().wait_recv()
                add_to(self.piece(), self.x_in(2))
                add_far(self.u, 0, self.piece())
                self.own().start()
                self.back(0).start()
            if n == 6:
                self.own().wait()
                self.back(0).wait_recv()
                self.back(1).start()
            if n == 7:
                self.back(1).wait_recv()
                self.back_last()

    class DeepX(Deep):
        first_x = True

    kinds = {"wide": Wide, "cross": Cross, "bounce": Bounce, "line": Line, "deep": Deep, "deep_x": DeepX}
    sums = [kinds[unit[3]](u) for u, unit in enumerate(UNITS)]

    def sum_step(u, n):
        if n == 0:
            for i in range(2):
                core_sum(u, i).start()
            return
        if n == 1:
            k, row, count, _ = UNITS[u]
            wait_rows(u, 0, 2 * count)
            for i in range(2):
                add_to(cut(k, 2 * i + c, row, count), core_in.at[k, i, pl.ds(row, count)])
        sums[u].step(n)

    def sums_done():
        factors.wait()
        to_core.wait()
        to_all.wait()
        if done.size:
            done.wait()

        @pl.when(border)
        def _():
            from_border.wait()
            if done_border.size:
                done_border.wait()

        @pl.when(middle)
        def _():
            from_middle.wait()
            kept.wait()
            if done_middle.size:
                done_middle.wait()

    vec_steps = 6 + extra
    vec_moves = []

    def vec_step(n):
        if n == 0:
            top = vec_grads[...]
            high = top.astype(LOW)
            low = (top - high.astype(F32)).astype(LOW)
            for seg in range(GROUPS):
                spread = spread_matrix(seg)
                vec_segs[seg] = dot_turned(high, spread) + dot_turned(low, spread)
            for row, parts in SEGMENTS.items():
                for seg, (q, at) in enumerate(parts):
                    vecs[q, at : at + 1, :] = vec_segs[seg, row : row + 1, :]
            for i in range(2):
                copy = remote(
                    vecs.at[2 * i + 1 - c], vec_in.at[i], v_send.at[3 + i], v_recv.at[3 + i], near["c"]
                )
                copy.start()
                vec_moves.append(copy)
            return
        if n == 1:
            for i in range(2):
                vec_moves[i].wait()
                vecs[2 * i + c] = vecs[2 * i + c] + vec_in[i]
        else:
            vec_moves[-1].wait()
            vecs[mine] = vecs[mine] + vec_in[n]
        steps = [near["y"], near["x"], near["e"], near["w"]] + far
        if n <= len(steps):
            copy = remote(
                vecs.at[yours if n == 1 else mine],
                vec_in.at[1 + n],
                v_send.at[4 + n],
                v_recv.at[4 + n],
                steps[n - 1],
            )
            copy.start()
            vec_moves.append(copy)
        else:
            copy = pltpu.make_async_copy(vecs.at[mine], vec_out, io_sem.at[2])
            copy.start()
            copy.wait()

    forward = [([], vectors_ready), ([], norm_first)]
    forward += [([QKV + n], functools.partial(project_block, n)) for n in range(3)]
    forward += [([], functools.partial(attend, w)) for w in range(windows)]
    forward += [([OUT], attend_out)]
    forward += [([FIN + n], functools.partial(inner_block, n)) for n in range(BLOCKS)]
    forward += [([8, 9, 10, 11], functools.partial(layer_part, 0))]
    forward += [([], functools.partial(layer_part, 1)), ([], layer_sort)]
    forward += [([12, 13], convolve_start), ([14, 15], convolve)]
    for item in GATHER_PLAN:
        if item < 0:
            need, work = forward.pop(0)
            for k in need:
                weight_ready(k)
            work()
        else:
            gather_step(item // 10, item % 10)
    gather_done()

    backward = [convolve_back, layer_back]
    for n in range(BLOCKS):
        backward += [functools.partial(active_back, n), functools.partial(out_grad, n)]
    backward.insert(5, pass_grads)
    backward[8:8] = [functools.partial(convolve_grad, side) for side in range(2)]
    backward += [inner_sum]
    backward += [
        functools.partial(weight_grad, FIN + n, normed_ffn, slope.at[n]) for n in range(BLOCKS)
    ]
    backward += [hidden_back, context_back]
    backward += [functools.partial(attend_back, w) for w in range(windows)]
    backward += [project_sum]
    backward += [functools.partial(weight_grad, QKV + n, normed, slope.at[n]) for n in range(3)]
    backward += [chars_back]
    backward += [functools.partial(vec_step, n) for n in range(vec_steps)]
    swaps = [functools.partial(swap, 0, mol_v, mols_out, mols)]
    for part in range(SWAP_PARTS):
        swaps.append(functools.partial(swap, 1, context, chars_out, rows, part, SWAP_PARTS))
    for item in PLAN:
        if item == -1:
            backward.pop(0)()
        elif item == -2:
            swaps.pop(0)()
        else:
            sum_step(item // 10, item % 10)
    for work in backward:
        work()
    sums_done()
    swaps_done()


def run(args, chars, extra):
    rows = chars.shape[0] // 2
    mols = rows // KERNEL
    anywhere = pl.BlockSpec(memory_space=pl.ANY)
    dma = pltpu.SemaphoreType.DMA
    vmem = pltpu.VMEM
    windows = rows // WIN
    return pl.pallas_call(
        functools.partial(program_kernel, rows, extra),
        name="layer_and_sums",
        out_shape=[
            jax.ShapeDtypeStruct((2 * mols, HALF), LOW),
            jax.ShapeDtypeStruct((2 * rows, HALF), LOW),
            jax.ShapeDtypeStruct(VEC, F32),
        ]
        + [jax.ShapeDtypeStruct(shape, LOW) for shape in SHARD_SHAPES]
        + [jax.ShapeDtypeStruct((len(UNITS), extra, SHARD, D), LOW)] * (extra > 0),
        in_specs=[anywhere, pl.BlockSpec(memory_space=vmem)] + [anywhere] * (len(args) - 2),
        out_specs=[anywhere] * (8 + (extra > 0)),
        scratch_shapes=[vmem((n * SHARD,), LOW) for n in VEC_COUNTS]
        + [
            vmem((COUNT * D, D), LOW),
            vmem((COUNT, 2, SHARD, D), LOW),
            vmem((CONV, SHARD, D), LOW),
            vmem((COUNT, SHARD, HALF), LOW),
            vmem((COUNT, SHARD, HALF), LOW),
            vmem((COUNT, SHARD, HALF), LOW),
            vmem((max(len(LINES), 1), SHARD // 2, D), LOW),
            vmem(VEC, F32),
            vmem((GROUPS,) + VEC, F32),
            vmem((GROUPS,) + VEC, F32),
            vmem((VEC[0], D), F32),
            vmem((VEC[0], D), F32),
            vmem((7 + extra,) + VEC, F32),
            vmem((rows, D), LOW),
            vmem((mols, D), LOW),
            vmem((rows, D), LOW),
            vmem((3, rows, D), LOW),
            vmem((windows, PAIRS, 2 * WIN, WIN), LOW),
            vmem((rows, D), LOW),
            vmem((rows, D), F32),
            vmem((rows, D), LOW),
            vmem((BLOCKS, rows, D), LOW),
            vmem((BLOCKS, rows, D), LOW),
            vmem((rows, D), F32),
            vmem((KERNEL, mols, D), LOW),
            vmem((rows, D), LOW),
            vmem((rows, D), F32),
            vmem((mols, D), LOW),
            vmem((GROUPS * mols, D), LOW),
            vmem((GROUPS * mols, D), LOW),
            dma((1,)),
            dma((3, len(PIECES))),
            dma((COUNT,)),
            dma((8,)),
            dma((SEMS,)),
            dma((len(UNITS), extra) if extra else (1, 1)),
            dma((len(UNITS), extra) if extra else (1, 1)),
            dma((9 + extra,)),
            dma((9 + extra,)),
            dma((5 + len(VEC_COUNTS),)),
            dma((4,)),
            dma((1,)),
            dma((6,)),
        ],
        compiler_params=pltpu.CompilerParams(
            collective_id=0, has_side_effects=True, vmem_limit_bytes=63 << 20
        ),
    )(*args)


def finish_kernel(mols, layer, vec, *refs):
    count = len(VEC_COUNTS)
    sums, (mols_out, layer_out), refs = refs[:5], refs[5:7], refs[7:]
    outs, vec_outs, flat, refs = refs[:5], refs[5 : 5 + count], refs[5 + count : 5 + 2 * count], refs[5 + 2 * count :]
    low, wide, load, store, whole, vec_sem, vec_held, mols_held, layer_held = refs
    loads = [
        pltpu.make_async_copy(shard_block(sums, k, 0, SHARD), low.at[k], load.at[k])
        for k in range(COUNT)
    ]
    through = [
        pltpu.make_async_copy(vec, vec_held, whole.at[2]),
        pltpu.make_async_copy(mols, mols_held, whole.at[0]),
        pltpu.make_async_copy(layer, layer_held, whole.at[1]),
    ]
    for copy in through + loads:
        copy.start()
    through[0].wait()
    at = 0
    copies = []
    for i, (ref, there, rows_held) in enumerate(zip(flat, vec_outs, VEC_COUNTS)):
        for j in range(rows_held):
            line = vec_held[at : at + 1, :][:, :SHARD].reshape(SHARD)
            ref[j * SHARD : (j + 1) * SHARD] = line
            at += 1
        copies.append(pltpu.make_async_copy(ref, there, vec_sem.at[i]))
        copies[-1].start()
    backs = [
        pltpu.make_async_copy(mols_held, mols_out, whole.at[0]),
        pltpu.make_async_copy(layer_held, layer_out, whole.at[1]),
    ]
    for before, after in zip(through[1:], backs):
        before.wait()
        after.start()
    for k in range(COUNT):
        loads[k].wait()
        wide[k] = low[k].astype(F32)
        copy = pltpu.make_async_copy(wide.at[k], shard_block(outs, k, 0, SHARD), store.at[k])
        copy.start()
        copies.append(copy)
    for copy in copies + backs:
        copy.wait()


def finish(mols, layer, vec, sums):
    anywhere = pl.BlockSpec(memory_space=pltpu.HBM)
    shape = jax.ShapeDtypeStruct
    vmem, dma = pltpu.VMEM, pltpu.SemaphoreType.DMA
    out = pl.pallas_call(
        finish_kernel,
        name="widen_sums",
        out_shape=[shape(mols.shape, LOW), shape(layer.shape, LOW)]
        + [shape(w.shape, F32) for w in sums]
        + [shape((n * SHARD,), F32) for n in VEC_COUNTS],
        in_specs=[anywhere] * 8,
        out_specs=[anywhere] * (7 + len(VEC_COUNTS)),
        scratch_shapes=[vmem((n * SHARD,), F32) for n in VEC_COUNTS]
        + [
            vmem((COUNT, SHARD, D), LOW),
            vmem((COUNT, SHARD, D), F32),
            dma((COUNT,)),
            dma((COUNT,)),
            dma((3,)),
            dma((len(VEC_COUNTS),)),
            vmem(VEC, F32),
            vmem(mols.shape, LOW),
            vmem(layer.shape, LOW),
        ],
        compiler_params=pltpu.CompilerParams(vmem_limit_bytes=60 << 20),
    )(mols, layer, vec, *sums)
    return out[0], out[1], out[2:7], out[7:]


def body(
    chars,
    char_codes,
    mol_cotangent,
    attn_norm_gain,
    attn_norm_bias,
    qkv_weight,
    qv_bias,
    out_weight,
    out_bias,
    ffn_norm_gain,
    ffn_norm_bias,
    ffn_in_weight,
    ffn_in_bias,
    ffn_out_weight,
    ffn_out_bias,
    conv_weight,
    conv_bias,
    down_norm_gain,
    down_norm_bias,
):
    vectors = [
        attn_norm_gain,
        attn_norm_bias,
        qv_bias,
        out_bias,
        ffn_norm_gain,
        ffn_norm_bias,
        ffn_in_bias,
        ffn_out_bias,
        conv_bias,
        down_norm_gain,
        down_norm_bias,
    ]
    result = run(
        (
            chars,
            char_codes.reshape(-1, WIN),
            mol_cotangent,
            qkv_weight,
            out_weight,
            ffn_in_weight,
            ffn_out_weight,
            conv_weight,
            *vectors,
        ),
        chars,
        (lax.axis_size("replica") // RING).bit_length() - 1,
    )
    molecules, chars_grad, big, v = finish(*result[:3], result[3:8])
    t_qkv, t_out, t_in, t_ffo, t_conv = big
    return (
        molecules,
        chars_grad,
        v[0],
        v[1],
        t_qkv,
        v[2],
        t_out,
        v[3],
        v[4],
        v[5],
        t_in,
        v[6],
        t_ffo,
        v[7],
        t_conv,
        v[8],
        v[9],
        v[10],
    )


def solution(mesh):
    return jax.shard_map(
        body,
        mesh=mesh,
        in_specs=(
            P(("group", "replica"), None),
            P(("group", "replica")),
            P(("group", "replica"), None),
            P("group"),
            P("group"),
            P("group", None),
            P("group"),
            P("group", None),
            P("group"),
            P("group"),
            P("group"),
            P("group", None),
            P("group"),
            P("group", None),
            P("group"),
            P("group", None),
            P("group"),
            P("group"),
            P("group"),
        ),
        out_specs=(
            P(("group", "replica"), "section"),
            P(("group", "replica"), "section"),
            P("group"),
            P("group"),
            P("group", None),
            P("group"),
            P("group", None),
            P("group"),
            P("group"),
            P("group"),
            P("group", None),
            P("group"),
            P("group", None),
            P("group"),
            P("group", None),
            P("group"),
            P("group"),
            P("group"),
        ),
        check_vma=False,
    )
```

```python
import functools
import math

import jax
import jax.numpy as jnp
from jax import lax
from jax.experimental import pallas as pl
from jax.experimental.pallas import tpu as pltpu
from jax.sharding import PartitionSpec as P

D = 768
HEADS = 12
HEAD_DIM = 64
FF = 3072
WIN = 128
KERNEL = 4
GROUPS = 4
RING = 4
SHARD = D // GROUPS
THIRD = SHARD // 3
EIGHTH = SHARD // 4
HALF = D // 2
TILE = 768
PAIR = 2 * HEAD_DIM
PAIRS = HEADS // 2
RUN = WIN // KERNEL
BLOCKS = FF // D
VEC = (16, 256)
VEC_COUNTS = (1, 1, 2, 1, 1, 1, 4, 1, 1, 1, 1)
SCRATCH = 30
norm_eps = 1e-06
mask_value = -10000.0
MESH = pl.DeviceIdType.MESH
F32 = jnp.float32
LOW = jnp.bfloat16

CHUNKS = (
    [(0, "col", j) for j in range(3)]
    + [(1, "col", 0)]
    + [(2, "col", j) for j in range(4)]
    + [(3, "row", j) for j in range(4)]
    + [(4, "row", j) for j in range(4)]
)
COUNT = len(CHUNKS)
QKV, OUT, FIN, FOUT, CONV = BASES = (0, 3, 4, 8, 12)
SHARD_SHAPES = [(SHARD, 3 * D), (SHARD, D), (SHARD, FF), (FF // GROUPS, D), (D, D)]

A_GAIN, A_BIAS, Q_BIAS, V_BIAS, O_BIAS, F_GAIN, F_BIAS = range(7)
IN_BIAS, FO_BIAS, C_BIAS, D_GAIN, D_BIAS = 7, 11, 12, 13, 14


def segments():
    table = {}
    for row, at in zip((A_GAIN, A_BIAS, O_BIAS, F_GAIN, F_BIAS), (0, 1, 4, 5, 6)):
        table[row] = [(q, at) for q in range(GROUPS)]
    table[Q_BIAS] = [(0, 2), (0, 3), (1, 2), (1, 3)]
    table[V_BIAS] = [(2, 2), (2, 3), (3, 2), (3, 3)]
    for n in range(BLOCKS):
        table[IN_BIAS + n] = [(n, 7 + i) for i in range(4)]
    for row, at in zip((FO_BIAS, C_BIAS, D_GAIN, D_BIAS), (11, 12, 13, 14)):
        table[row] = [(q, at) for q in range(GROUPS)]
    return table


SEGMENTS = segments()

PIECES = [
    (0, 0, 1, 3), (1, 0, 1, 3), (2, 0, 1, 3), (3, 0, 1, 3), (4, 0, 1, 3), (5, 0, 1, 3), (6,
    0, 1, 3), (7, 0, 1, 3), (8, 0, 2, 3), (8, 1, 2, 3), (9, 0, 2, 3), (9, 1, 2, 3), (10, 0,
    2, 3), (10, 1, 2, 3), (11, 0, 2, 3), (11, 1, 2, 3), (12, 0, 2, 3), (12, 1, 2, 3), (13,
    0, 2, 3), (13, 1, 2, 3), (14, 0, 2, 3), (14, 1, 2, 3), (15, 0, 2, 3), (15, 1, 2, 3),
]
GATHER_PLAN = [
    -1, -1, 0, 10, 1, 20, 11, 30, 2, 21, 40, -1, 12, 31, 50, 22, 41, 60, -1, -1, 32, 51, 70,
    -1, 80, 42, 61, 90, -1, 100, -1, 52, 71, 110, 120, -1, 81, 62, 91, 130, -1, 101, 72,
    111, 140, 150, 160, -1, 82, 92, 121, 131, 170, 180, 102, 141, -1, 112, 151, 122, 161,
    190, 200, 210, -1, 132, 142, 171, 181, 220, 191, 152, 230, -1, 162, 201, 172, 211, -1,
    182, 221, 231, 192, -1, 202, -1, 212, -1, 222, 232, -1,
]

UNITS = [
    (12, 0, 192, "line"),
    (13, 0, 192, "wide"),
    (14, 0, 192, "bounce"),
    (15, 0, 192, "bounce"),
    (8, 0, 96, "cross"),
    (8, 96, 96, "cross"),
    (9, 0, 96, "bounce"),
    (9, 96, 96, "line"),
    (10, 0, 96, "cross"),
    (10, 96, 96, "line"),
    (11, 0, 96, "line"),
    (11, 96, 96, "line"),
    (4, 0, 192, "cross"),
    (5, 0, 192, "line"),
    (6, 0, 192, "bounce"),
    (7, 0, 96, "bounce"),
    (7, 96, 96, "bounce"),
    (3, 0, 64, "line"),
    (3, 64, 64, "cross"),
    (3, 128, 64, "bounce"),
    (0, 0, 48, "cross"),
    (0, 48, 48, "cross"),
    (0, 96, 48, "cross"),
    (0, 144, 48, "cross"),
    (1, 0, 64, "line"),
    (1, 64, 64, "line"),
    (1, 128, 64, "line"),
    (2, 0, 64, "wide"),
    (2, 64, 64, "bounce"),
    (2, 128, 64, "bounce"),
]

SEM_COUNT = {"wide": 5, "cross": 5, "bounce": 5, "line": 6, "deep": 8, "deep_x": 8}
SEM_AT = [sum(SEM_COUNT[unit[3]] for unit in UNITS[:u]) for u in range(len(UNITS))]
SEMS = sum(SEM_COUNT[unit[3]] for unit in UNITS)
LINES = sorted({unit[0] for unit in UNITS if unit[3] == "line"})
SWAP_PARTS = 4
PLAN = [
    -1, -1, -2, -1, -1, -1, -1, -1, -1, -1, 2, 12, -1, 22, 32, -1, -1, -1, 60, 40, 50, 13,
    70, 100, 110, 80, 61, 90, 41, -1, 3, 23, 51, 101, 111, 71, 33, 14, 62, 81, 91, -1, 120,
    -1, 4, 130, 24, 102, 121, 42, -1, 131, 15, 34, 140, 112, 52, 63, -1, 150, 160, 141, 103,
    25, -1, 72, 16, 35, 151, 161, 92, 113, 5, 104, 64, 82, 26, 43, -1, 114, 73, 190, 36,
    180, 170, -1, 6, 181, 171, 191, 132, 93, 122, 65, 44, -1, 53, 27, 74, -1, 37, 94, 66,
    105, 115, 45, -1, 133, 182, 142, 67, 106, 75, -1, 54, 116, 152, 46, 95, -1, 200, 210,
    220, 230, 134, 162, -1, 201, 211, 221, 153, 231, 76, 83, 143, 172, 240, 250, 96, 260,
    55, -1, 154, 280, 290, 135, 192, 270, 163, 84, 281, 291, 241, 251, 202, 123, 271, 56,
    155, 183, 261, 212, 144, -1, 136, 282, 173, 222, -2, 232, -2, 292, -2, 164, -2, -1, 156,
    85, 193, -1, 242, 283, 145, 124, 252, 174, 184, 86, 203, 194, 165, 272, 243, 146, 293,
    284, 125, 262, 166, 213, 185, 223, 253, 195, 233, 204, -1, 244, 157, 294, 285, 126, 254,
    263, 186, 205, 175, 214, 196, 295, 224, 273, 286, 234, 264, 206, 147, 176, 215, 274,
    167, 296, 225, -1, 235, 245, 216, 275, 255, 226, 236, 246, 265, -1, 197, 256, 276, 287,
    266, 297, -1,
]


def at16(value):
    return pl.multiple_of(value, 16)


def at128(value):
    return pl.multiple_of(value, 128)


def spot(chunk, shard, first=0):
    mat, kind, j = CHUNKS[chunk]
    if kind == "col":
        return at16((BASES[mat] + j) * D + shard * SHARD + first)
    return at16((BASES[mat] + shard) * D + j * SHARD + first)


def shard_block(refs, chunk, first, rows, col=0, cols=D):
    mat, kind, j = CHUNKS[chunk]
    if kind == "col":
        return refs[mat].at[pl.ds(at16(first), rows), pl.ds(at128(j * D + col), cols)]
    return refs[mat].at[pl.ds(at16(j * SHARD + first), rows), pl.ds(at128(col), cols)]


def remote(src, dst, send, recv, target):
    return pltpu.make_async_remote_copy(
        src_ref=src,
        dst_ref=dst,
        send_sem=send,
        recv_sem=recv,
        device_id=target,
        device_id_type=MESH,
    )


class Tally:
    def __init__(self, sem, yard):
        self.sem, self.yard, self.size = sem, yard, 0

    def add(self, ref):
        self.size += math.prod(ref.shape)

    def wait(self):
        here = self.yard.at[pl.ds(0, self.size // D)]
        pltpu.make_async_copy(here, here, self.sem).wait()
        self.size = 0


class Move:
    def __init__(self, src, dst, sent, recv, target):
        self.src, self.dst, self.sent = src, dst, sent
        self.copy = remote(src, dst, sent.sem, recv, target)

    def start(self):
        self.sent.add(self.src)
        self.copy.start()

    def wait_recv(self):
        self.copy.wait_recv()


def add_to(dst, src):
    rows = next(n for n in (48, 32, 16) if dst.shape[0] % n == 0)

    @pl.loop(0, dst.shape[0] // rows)
    def _(i):
        here = pl.ds(at16(i * rows), rows)
        dst[here, :] = dst[here, :] + src[here, :]


def dot(left, right):
    return jnp.dot(left, right, preferred_element_type=F32)


def dot_rows(left, right):
    return lax.dot_general(left, right, (((0,), (0,)), ((), ())), preferred_element_type=F32)


def dot_turned(left, right):
    return lax.dot_general(left, right, (((1,), (1,)), ((), ())), preferred_element_type=F32)


def normalized(values):
    center = values - jnp.mean(values, axis=-1, keepdims=True)
    scale = lax.rsqrt(jnp.mean(center * center, axis=-1, keepdims=True) + norm_eps)
    return center * scale, scale


def norm_back(unit, scale, gain, grad):
    grad_unit = grad * gain
    mean_grad = jnp.mean(grad_unit, axis=-1, keepdims=True)
    mean_both = jnp.mean(grad_unit * unit, axis=-1, keepdims=True)
    return scale * (grad_unit - mean_grad - unit * mean_both)


def gelu_parts(values):
    half = 0.5 * lax.erf(values * (0.5**0.5)) + 0.5
    bell = jnp.exp(-0.5 * values * values) * 0.3989422804014327
    return values * half, half + values * bell


def column_sum(values):
    return jnp.sum(values, axis=0, keepdims=True)


def program_kernel(rows, extra, *refs):
    count = len(VEC_COUNTS)
    (chars, codes, cotangent) = refs[:3]
    shards = refs[3:8]
    vectors = refs[8 : 8 + count]
    mols_out, chars_out, vec_out = refs[8 + count : 11 + count]
    out = refs[11 + count : 16 + count]
    more_in = refs[16 + count] if extra else None
    refs = refs[16 + count + (extra > 0) :]
    flat, refs = refs[:count], refs[count:]
    (
        held,
        core_in,
        y_in,
        x_in,
        e_in,
        m_in,
        line_in,
        vec,
        vecs,
        vec_segs,
        rows_f32,
        vec_grads,
        vec_in,
        chars_v,
        cot_v,
        normed,
        projected,
        probs,
        context,
        hidden,
        normed_ffn,
        slope,
        active,
        layer,
        stacked,
        low_grad,
        total,
        mol_v,
        near_rows,
        near_grads,
    ) = refs[:SCRATCH]
    (
        w_send,
        w_recv,
        c_recv,
        g_send,
        g_recv,
        more_send,
        more_recv,
        v_send,
        v_recv,
        io_sem,
        swap_sem,
        f_send,
        f_recv,
    ) = refs[SCRATCH:]
    windows = rows // WIN
    mols = rows // KERNEL
    s, g, r = lax.axis_index("section"), lax.axis_index("group"), lax.axis_index("replica")
    near = {
        "c": (s, g ^ 1, r),
        "y": (s, g ^ 2, r),
        "x": (1 - s, g, r),
        "e": (s, g, r ^ 1),
        "m": (s, g, r ^ 3),
        "d": (s, g ^ 3, r),
        "w": (s, g, r ^ 2),
    }
    far = [(s, g, r ^ (RING << i)) for i in range(extra)]
    place = lax.rem(r, RING)
    even = lax.rem(r, 2) == 0
    middle = jnp.logical_or(place == 1, place == 2)
    border = jnp.logical_not(middle)

    barrier = pltpu.get_barrier_semaphore()
    greeted = list(near.values()) + far
    for target in greeted:
        pl.semaphore_signal(barrier, inc=1, device_id=target, device_id_type=MESH)

    flat_copies = [
        pltpu.make_async_copy(src, dst, io_sem.at[5 + i])
        for i, (src, dst) in enumerate(zip(vectors, flat))
    ]
    for copy in flat_copies:
        copy.start()
    vec[...] = jnp.zeros_like(vec)
    vec_grads[...] = jnp.zeros_like(vec_grads)
    vec_segs[...] = jnp.zeros_like(vec_segs)
    at = 0
    for copy, values, rows_held in zip(flat_copies, flat, VEC_COUNTS):
        copy.wait()
        wide = values[...].astype(F32)
        for i in range(rows_held):
            line = wide[i * SHARD : (i + 1) * SHARD].reshape(1, SHARD)
            vec[at : at + 1, pl.ds(0, SHARD)] = line
            at += 1
    pl.semaphore_wait(barrier, len(greeted))

    y_third = jnp.where(even, s, 2)
    z_third = jnp.where(even, 2, s)
    x_third = 1 - s
    other = g ^ 2

    own_vec = pltpu.make_async_copy(vec, vecs.at[g], io_sem.at[2])
    vec_copies = [
        remote(vec, vecs.at[g], v_send.at[i], v_recv.at[i], near[way])
        for i, way in enumerate("cyd")
    ]
    for copy in vec_copies + [own_vec]:
        copy.start()

    sent = Tally(w_send.at[0], held)

    def rows_by(u, way):
        k, part, parts, ways = PIECES[u]
        if ways == 2:
            count = SHARD // parts
            which = s if way == "y" else 1 - s
            return k, part * count + which * (count // 2), count // 2
        third = {"y": y_third, "z": z_third, "x": x_third}[way]
        return k, third * THIRD + part * (THIRD // parts), THIRD // parts

    def arrived(u, way):
        k, first, count = rows_by(u, way)
        return held.at[pl.ds(spot(k, other, first), count)]

    def hop(u, way, src_way):
        here = arrived(u, src_way)
        i = "yxz".index(way)
        return Move(here, here, sent, w_recv.at[i, u], near["yxe"[i]])

    def first_hop(u):
        k, first, count = rows_by(u, "y")
        src = shard_block(shards, k, first, count)
        there = held.at[pl.ds(spot(k, g, first), count)]
        return Move(src, there, sent, w_recv.at[0, u], near["y"])

    def core_own(k):
        src = shard_block(shards, k, 0, SHARD)
        there = held.at[pl.ds(spot(k, g), SHARD)]
        return Move(src, there, sent, c_recv.at[k], near["c"])

    def core_hop(u, way):
        here = arrived(u, way)
        Move(here, here, sent, c_recv.at[PIECES[u][0]], near["c"]).start()

    for u in range(len(PIECES)):
        first_hop(u).start()
    loads = [
        pltpu.make_async_copy(chars.at[pl.ds(at16(s * rows), rows)], chars_v, io_sem.at[0]),
        pltpu.make_async_copy(cotangent.at[pl.ds(at16(s * mols), mols)], cot_v, io_sem.at[1]),
    ]
    for copy in loads:
        copy.start()
    for k in range(COUNT):
        own_block = held.at[pl.ds(spot(k, g), SHARD)]
        pltpu.make_async_copy(shard_block(shards, k, 0, SHARD), own_block, c_recv.at[k]).start()
        core_own(k).start()

    def gather_step(u, n):
        two = PIECES[u][3] == 2
        if n == 0:
            hop(u, "y", "y").wait_recv()
            if two:
                hop(u, "x", "y").start()
            else:
                hop(u, "z", "y").start()

                @pl.when(even)
                def _():
                    hop(u, "x", "y").start()

            core_hop(u, "y")
        if n == 1:
            hop(u, "z", "z").wait_recv()

            @pl.when(jnp.logical_not(even))
            def _():
                hop(u, "x", "z").copy.start()

            core_hop(u, "z")
        if n == 2:
            hop(u, "x", "x").wait_recv()
            core_hop(u, "x")

    def weight_ready(k):
        here = held.at[pl.ds(0, 3 * SHARD)]
        pltpu.make_async_copy(here, here, c_recv.at[k]).wait()

    def gather_done():
        sent.wait()

    def spread_matrix(seg):
        i = lax.broadcasted_iota(jnp.int32, (VEC[1], D), 0)
        j = lax.broadcasted_iota(jnp.int32, (VEC[1], D), 1)
        hit = jnp.logical_and(j == i + seg * SHARD, i < SHARD)
        return jnp.where(hit, 1.0, 0.0).astype(LOW)

    def vectors_ready():
        own_vec.wait()
        for copy in vec_copies:
            copy.wait()
        for row, parts in SEGMENTS.items():
            for seg, (q, at) in enumerate(parts):
                vec_segs[seg, row : row + 1, :] = vecs[q, at : at + 1, :]
        full = jnp.zeros((VEC[0], D), F32)
        for seg in range(GROUPS):
            full = full + dot(vec_segs[seg].astype(LOW), spread_matrix(seg))
        rows_f32[...] = full

    def vector(row):
        return rows_f32[row : row + 1, :]

    def vector_tile(row, j):
        return rows_f32[row : row + 1, pl.ds(at128(j * TILE), TILE)]

    def block(n, j=None):
        start = n * D
        if not isinstance(n, int):
            start = at16(start)
        if j is None:
            return held[pl.ds(start, D), :]
        return held[pl.ds(start, D), pl.ds(at128(j * TILE), TILE)]

    def row_tiles(body):
        @pl.loop(0, rows // WIN)
        def _(i):
            body(pl.ds(at128(i * WIN), WIN), i)

    def col_tiles(body):
        @pl.loop(0, D // TILE)
        def _(j):
            body(pl.ds(at128(j * TILE), TILE), j)

    def norm_first():
        loads[0].wait()

        def one(here, i):
            unit, _ = normalized(chars_v[here, :].astype(F32))
            normed[here, :] = (unit * vector(A_GAIN) + vector(A_BIAS)).astype(LOW)

        row_tiles(one)

    def project_block(n):
        def one(here, j):
            value = dot(normed[...], block(QKV + n, j))
            if n == 0:
                value = value + vector_tile(Q_BIAS, j)
            if n == 2:
                value = value + vector_tile(V_BIAS, j)
            projected[n, :, here] = value.astype(LOW)

        col_tiles(one)

    def key_bias(w):
        code = codes[pl.ds(s * windows + w, 1), :]
        return jnp.where(code != 0, 0.0, mask_value).astype(F32)

    def lanes():
        return lax.broadcasted_iota(jnp.int32, (WIN, PAIR), 1) < HEAD_DIM

    def two_heads(values):
        first = lanes()
        zero = jnp.zeros_like(values)
        return jnp.concatenate(
            [jnp.where(first, values, zero), jnp.where(first, zero, values)], axis=0
        )

    def one_pair(values):
        return jnp.where(lanes(), values[:WIN], values[WIN:])

    scale_factor = HEAD_DIM ** (-0.5)

    def attend(w):
        here = pl.ds(w * WIN, WIN)
        bias = key_bias(w)
        for p in range(PAIRS):
            cols = pl.ds(p * PAIR, PAIR)
            queries = two_heads(projected[0, here, cols])
            scores = dot_turned(queries, projected[1, here, cols]) * scale_factor + bias
            top = jnp.max(scores, axis=-1, keepdims=True)
            weight = jnp.exp(scores - top)
            weight = weight / jnp.sum(weight, axis=-1, keepdims=True)
            prob = weight.astype(LOW)
            probs[w, p] = prob
            context[here, cols] = one_pair(dot(prob, projected[2, here, cols])).astype(LOW)

    def attend_out():
        def one(here, j):
            value = dot(context[...], block(OUT, j)) + vector_tile(O_BIAS, j)
            hidden[:, here] = chars_v[:, here].astype(F32) + value

        col_tiles(one)

        def norm(here, i):
            unit, _ = normalized(hidden[here, :])
            normed_ffn[here, :] = (unit * vector(F_GAIN) + vector(F_BIAS)).astype(LOW)

        row_tiles(norm)

    def inner_block(n):
        def one(here, j):
            value = dot(normed_ffn[...], block(FIN + n, j)) + vector_tile(IN_BIAS + n, j)
            gelu, grad = gelu_parts(value)
            active[n, :, here] = gelu.astype(LOW)
            slope[n, :, here] = grad.astype(LOW)

        col_tiles(one)

    def by_place():
        i = lax.broadcasted_iota(jnp.int32, (WIN, WIN), 0)
        j = lax.broadcasted_iota(jnp.int32, (WIN, WIN), 1)
        return jnp.where(j == KERNEL * lax.rem(i, RUN) + i // RUN, 1.0, 0.0).astype(LOW)

    def layer_part(side):
        cols = pl.ds(side * HALF, HALF)
        value = hidden[:, cols] + rows_f32[FO_BIAS : FO_BIAS + 1, cols]
        for n in range(BLOCKS):
            value = value + dot(active[n], held[pl.ds((FOUT + n) * D, D), cols])
        low_grad[:, cols] = value.astype(LOW)

    def layer_sort():
        order = by_place()

        def sort(here, w):
            moved = dot(order, low_grad[here, :]).astype(LOW)
            for k in range(KERNEL):
                stacked[k, pl.ds(at16(w * RUN), RUN), :] = moved[k * RUN : (k + 1) * RUN]

        row_tiles(sort)
        give_rows()

    def note(row, value):
        vec_grads[row : row + 1, :] = value

    def note_more(row, value):
        vec_grads[row : row + 1, :] = vec_grads[row : row + 1, :] + value

    factors = Tally(f_send.at[0], held)
    ways = {1: "c", 2: "y", 3: "d"}

    def slot(i):
        return pl.ds(i * mols, mols)

    def give_rows():
        near_rows[slot(0), :] = stacked[g]
        for i in (2, 3, 1):
            there = near_rows.at[slot(i)]
            move = Move(stacked.at[g ^ i], there, factors, f_recv.at[i - 1], near[ways[i]])
            move.start()

    def grads_move(i, src, way):
        there = near_grads.at[slot(i)]
        return Move(near_grads.at[slot(src)], there, factors, f_recv.at[2 + i], near[way])

    def give_grads():
        grads_move(2, 0, "y").start()
        grads_move(1, 0, "c").start()

    def pass_grads():
        grads_move(2, 0, "y").wait_recv()
        grads_move(3, 2, "c").start()

    def convolve_grad(side):
        if side == 0:
            for i in (1, 3):
                grads_move(i, 0, "c").wait_recv()
            for i in (1, 2, 3):
                here = near_rows.at[slot(i)]
                Move(here, here, factors, f_recv.at[i - 1], near["c"]).wait_recv()
        value = dot_rows(near_rows[:, side * HALF : (side + 1) * HALF], near_grads[...])
        held[pl.ds(at16((CONV + g) * D + side * HALF), HALF), :] = value.astype(LOW)

    def convolve_part(side):
        cols = pl.ds(side * HALF, HALF)
        value = 0.0
        for k in range(KERNEL):
            here = pl.ds((CONV + k) * D + side * HALF, HALF)
            value = value + dot(stacked[k, :, cols], held[here, :])
        return value

    first_mols = pl.ds(0, mols)

    def convolve_start():
        total[first_mols, :] = convolve_part(0) + vector(C_BIAS)

    def convolve():
        loads[1].wait()
        gelu, grad = gelu_parts(total[first_mols, :] + convolve_part(1))
        unit, scale = normalized(gelu)
        grad_unit = norm_back(unit, scale, vector(D_GAIN), cot_v[...].astype(F32))
        near_grads[first_mols, :] = (grad_unit * grad).astype(LOW)
        give_grads()
        layer[first_mols, :] = unit

    def convolve_end():
        unit = layer[first_mols, :]
        wide = cot_v[...].astype(F32)
        note(D_GAIN, column_sum(wide * unit))
        note(D_BIAS, column_sum(wide))
        note(C_BIAS, column_sum(near_grads[first_mols, :].astype(F32)))
        mol_v[...] = (unit * vector(D_GAIN) + vector(D_BIAS)).astype(LOW)

    def convolve_back():
        for k in range(KERNEL):
            total[slot(k), :] = dot_turned(near_grads[first_mols, :], block(CONV + k))

    def layer_back():
        convolve_end()
        order = by_place()

        def sort(here, w):
            parts = [total[pl.ds(at16(k * mols + w * RUN), RUN), :] for k in range(KERNEL)]
            value = dot_rows(order, jnp.concatenate(parts, axis=0).astype(LOW))
            layer[here, :] = value
            low_grad[here, :] = value.astype(LOW)
            note_more(FO_BIAS, column_sum(value))

        row_tiles(sort)

    def weight_grad(n, left, right):
        def one(here, j):
            value = dot_rows(left[:, here], right[...])
            held[pl.ds(at128(n * D + j * TILE), TILE), :] = value.astype(LOW)

        col_tiles(one)

    def active_back(n):
        def one(here, j):
            value = dot_turned(
                low_grad[...], held[pl.ds(at128((FOUT + n) * D + j * TILE), TILE), :]
            )
            inner = (value * slope[n, :, here].astype(F32)).astype(LOW)
            slope[n, :, here] = inner
            vec_grads[IN_BIAS + n : IN_BIAS + n + 1, here] = column_sum(inner.astype(F32))

        col_tiles(one)

    def out_grad(n):
        weight_grad(FOUT + n, active.at[n], low_grad)

    def inner_sum():
        def one(here, j):
            value = jnp.zeros((rows, TILE), F32)
            for n in range(BLOCKS):
                value = value + dot_turned(
                    slope[n], held[pl.ds(at128((FIN + n) * D + j * TILE), TILE), :]
                )
            total[:, here] = value

        col_tiles(one)

    def hidden_back():
        def one(here, i):
            unit, scale = normalized(hidden[here, :])
            grad = total[here, :]
            note_more(F_GAIN, column_sum(grad * unit))
            note_more(F_BIAS, column_sum(grad))
            value = layer[here, :] + norm_back(unit, scale, vector(F_GAIN), grad)
            layer[here, :] = value
            low = value.astype(LOW)
            low_grad[here, :] = low
            note_more(O_BIAS, column_sum(low.astype(F32)))

        row_tiles(one)

    def context_back():
        def one(here, j):
            value = dot_turned(low_grad[...], held[pl.ds(at128(OUT * D + j * TILE), TILE), :])
            normed_ffn[:, here] = value.astype(LOW)

        col_tiles(one)
        weight_grad(OUT, context, low_grad)

    def attend_back(w):
        here = pl.ds(w * WIN, WIN)
        for p in range(PAIRS):
            cols = pl.ds(p * PAIR, PAIR)
            grad_out = two_heads(normed_ffn[here, cols])
            prob = probs[w, p]
            wide = prob.astype(F32)
            grad_prob = dot_turned(grad_out, projected[2, here, cols])
            inner = jnp.sum(wide * grad_prob, axis=-1, keepdims=True)
            grad_score = (wide * (grad_prob - inner)).astype(LOW)
            grad_value = dot_rows(prob, grad_out)
            grad_query = one_pair(dot(grad_score, projected[1, here, cols])) * scale_factor
            grad_key = (
                dot_rows(grad_score, two_heads(projected[0, here, cols])) * scale_factor
            )
            low_query, low_value = grad_query.astype(LOW), grad_value.astype(LOW)
            slope[0, here, cols] = low_query
            slope[1, here, cols] = grad_key.astype(LOW)
            slope[2, here, cols] = low_value
            for row, low in ((Q_BIAS, low_query), (V_BIAS, low_value)):
                vec_grads[row : row + 1, cols] = vec_grads[row : row + 1, cols] + column_sum(
                    low.astype(F32)
                )

    def project_sum():
        def one(here, j):
            value = jnp.zeros((rows, TILE), F32)
            for n in range(3):
                value = value + dot_turned(
                    slope[n], held[pl.ds(at128((QKV + n) * D + j * TILE), TILE), :]
                )
            total[:, here] = value

        col_tiles(one)

    def chars_back():
        def one(here, i):
            unit, scale = normalized(chars_v[here, :].astype(F32))
            grad = total[here, :]
            note_more(A_GAIN, column_sum(grad * unit))
            note_more(A_BIAS, column_sum(grad))
            value = layer[here, :] + norm_back(unit, scale, vector(A_GAIN), grad)
            context[here, :] = value.astype(LOW)

        row_tiles(one)

    def swap(i, whole, dst, count, part=0, parts=1):
        here = pl.ds(part * (count // parts), count // parts)
        keep = whole.at[here, pl.ds(at128(s * HALF), HALF)]
        give = whole.at[here, pl.ds(at128((1 - s) * HALF), HALF)]
        there = dst.at[pl.ds(at16(s * count + part * (count // parts)), count // parts)]
        stay = pltpu.make_async_copy(keep, there, swap_sem.at[2 * i])
        go = remote(give, there, swap_sem.at[2 * i], swap_sem.at[2 * i + 1], near["x"])
        stay.start()
        go.start()

    def swaps_done():
        for i, whole in enumerate((mol_v, context)):
            pltpu.make_async_copy(whole, whole, swap_sem.at[2 * i]).wait()
            here = whole.at[:, pl.ds(0, HALF)]
            pltpu.make_async_copy(here, here, swap_sem.at[2 * i + 1]).wait()

    c = lax.rem(g, 2)
    y = g // 2
    mine, yours = 2 * y + c, 2 * (1 - y) + c
    z_half, w_half = lax.rem(r, 2), lax.rem(r // 2, 2)
    row_one = z_half * EIGHTH * 2
    row_two = row_one + w_half * EIGHTH

    to_core, to_all = Tally(g_send.at[0], held), Tally(g_send.at[1], held)
    from_border, from_middle = Tally(g_send.at[2], held), Tally(g_send.at[3], held)
    kept = Tally(g_send.at[4], held)
    done, done_border = Tally(g_send.at[5], held), Tally(g_send.at[6], held)
    done_middle = Tally(g_send.at[7], held)

    def send(u, i, src, dst, way, sender=to_all):
        return Move(src, dst, sender, g_recv.at[SEM_AT[u] + i], near[way])

    def send_last(src, dst, way, sender=to_all, ends=done):
        move = Move(src, dst, sender, ends.sem, near[way])
        move.start()

    def cut(k, q, row, count, col=0, cols=D):
        return held.at[pl.ds(spot(k, q, row), count), pl.ds(at128(col), cols)]

    def final(k, row, count, col=None, cols=HALF):
        return shard_block(out, k, row, count, s * HALF if col is None else col, cols)

    def add_far(u, row, here):
        k = UNITS[u][0]
        count, cols = here.shape
        for i in range(extra):
            there = more_in.at[u, i, pl.ds(0, count), pl.ds(0, cols)]
            near_by = core_in.at[k, 0, pl.ds(row, count), pl.ds(0, cols)]
            copy = remote(here, there, more_send.at[u, i], more_recv.at[u, i], far[i])
            copy.start()
            copy.wait()
            copy = pltpu.make_async_copy(there, near_by, more_send.at[u, i])
            copy.start()
            copy.wait()
            add_to(here, near_by)

    def core_sum(u, i):
        k, row, count, _ = UNITS[u]
        there = core_in.at[k, i, pl.ds(row, count)]
        return send(u, 0, cut(k, 2 * i + 1 - c, row, count), there, "c", to_core)

    def wait_rows(u, i, count):
        here = held.at[pl.ds(0, count)]
        pltpu.make_async_copy(here, here, g_recv.at[SEM_AT[u] + i]).wait()

    def y_sum(u):
        k, row, count, _ = UNITS[u]
        return send(u, 1, cut(k, yours, row, count), y_in.at[k, pl.ds(row, count)], "y")

    def y_added(u):
        k, row, count, _ = UNITS[u]
        if k >= CONV:
            return
        y_sum(u).wait_recv()
        add_to(cut(k, mine, row, count), y_in.at[k, pl.ds(row, count)])

    class Wide:
        def __init__(self, u):
            self.u = u
            self.k, self.row, self.count, _ = UNITS[u]
            self.here = pl.ds(self.row, self.count)
            self.total = m_in.at[self.k, self.here]

        def part(self, side):
            return cut(self.k, mine, self.row, self.count, side * HALF, HALF)

        def done_part(self):
            return final(self.k, self.row, self.count)

        def x_sum(self):
            return send(self.u, 2, self.part(1 - s), x_in.at[self.k, self.here], "x")

        def e_sum(self):
            return send(self.u, 3, self.part(s), e_in.at[self.k, self.here], "e", from_border)

        def m_sum(self):
            return send(self.u, 4, self.part(s), self.total, "m", from_middle)

        def e_back(self):
            return send(self.u, 3, self.total, self.done_part(), "e", from_middle)

        def step(self, n):
            if n == 1:
                y_sum(self.u).start()
            if n == 2:
                y_added(self.u)
                self.x_sum().start()
            if n == 3:
                self.x_sum().wait_recv()
                add_to(self.part(s), x_in.at[self.k, self.here])

                @pl.when(border)
                def _():
                    self.e_sum().start()

            if n == 4:

                @pl.when(middle)
                def _():
                    self.e_sum().wait_recv()
                    add_to(self.part(s), e_in.at[self.k, self.here])
                    self.m_sum().start()

            if n == 5:

                @pl.when(middle)
                def _():
                    self.m_sum().wait_recv()
                    add_to(self.total, self.part(s))
                    add_far(self.u, self.row, self.total)
                    kept.add(self.total)
                    pltpu.make_async_copy(self.total, self.done_part(), kept.sem).start()
                    self.e_back().start()
                    send_last(self.total, self.done_part(), "x", from_middle)

            if n == 6:

                @pl.when(border)
                def _():
                    self.e_back().wait_recv()
                    send_last(self.done_part(), self.done_part(), "x", from_border)

                done.add(self.total)

    class Cross(Wide):
        def both_in(self, i):
            return y_in.at[self.k, self.here, pl.ds(i * HALF, HALF)]

        def both_part(self, i, side):
            return cut(self.k, 2 * i + c, self.row, self.count, side * HALF, HALF)

        def y_sum(self):
            src = cut(self.k, yours, self.row, self.count, s * HALF, HALF)
            return send(self.u, 2, src, x_in.at[self.k, self.here], "y")

        def step(self, n):
            if n == 1:
                for i in range(2):
                    send(self.u, 1, self.both_part(i, 1 - s), self.both_in(i), "x").start()
            elif n == 2:
                wait_rows(self.u, 1, self.count)
                for i in range(2):
                    add_to(self.both_part(i, s), self.both_in(i))
                self.y_sum().start()
            elif n == 3:
                self.y_sum().wait_recv()
                add_to(self.part(s), x_in.at[self.k, self.here])

                @pl.when(border)
                def _():
                    self.e_sum().start()

            else:
                super().step(n)

    class Bounce(Wide):
        def step(self, n):
            if n == 5:

                @pl.when(middle)
                def _():
                    self.m_sum().wait_recv()
                    add_to(self.total, self.part(s))
                    add_far(self.u, self.row, self.total)
                    kept.add(self.total)
                    pltpu.make_async_copy(self.total, self.done_part(), kept.sem).start()
                    self.e_back().start()

            elif n == 6:

                @pl.when(border)
                def _():
                    self.e_back().wait_recv()
                    here = self.done_part()
                    send(self.u, 4, here, here, "x", from_border).start()

            elif n == 7:

                @pl.when(border)
                def _():
                    there = final(self.k, self.row, self.count, (1 - s) * HALF)
                    send(self.u, 4, there, there, "x").wait_recv()
                    send_last(there, there, "e", from_border, done_middle)

                done_middle.add(self.total)
            else:
                super().step(n)

    class Line(Wide):
        def half(self, which):
            return self.row + which * (self.count // 2)

        def rows_of(self, which, side=None):
            col, cols = (0, D) if side is None else (side * HALF, HALF)
            return cut(self.k, mine, self.half(which), self.count // 2, col, cols)

        def done_rows(self, which):
            return final(self.k, self.half(which), self.count // 2, 0, D)

        def e_in(self, side):
            return (x_in, e_in)[side].at[self.k, self.here]

        def m_in(self, side):
            return m_in.at[self.k, pl.ds(self.row + side * (self.count // 2), self.count // 2)]

        def sum_line(self):
            return line_in.at[LINES.index(self.k), pl.ds(self.row // 2, self.count // 2)]

        def x_sum(self):
            return send(self.u, 4, self.rows_of(w_half), self.sum_line(), "x", from_middle)

        def m_back(self):
            return send(self.u, 5, self.sum_line(), self.done_rows(w_half), "m", from_middle)

        def step(self, n):
            if n == 1:
                y_sum(self.u).start()
            if n == 2:
                y_added(self.u)

                @pl.when(border)
                def _():
                    for side in range(2):
                        send(
                            self.u, 2, self.part(side), self.e_in(side), "e", from_border
                        ).start()

            if n == 3:

                @pl.when(middle)
                def _():
                    wait_rows(self.u, 2, self.count)
                    for side in range(2):
                        add_to(self.part(side), self.e_in(side))
                    for side in range(2):
                        src = self.rows_of(1 - w_half, side)
                        send(self.u, 3, src, self.m_in(side), "m", from_middle).start()

            if n == 4:

                @pl.when(middle)
                def _():
                    wait_rows(self.u, 3, self.count // 2)
                    for side in range(2):
                        add_to(self.rows_of(w_half, side), self.m_in(side))
                    self.x_sum().start()

            if n == 5:

                @pl.when(middle)
                def _():
                    self.x_sum().wait_recv()
                    add_to(self.sum_line(), self.rows_of(w_half))
                    add_far(self.u, self.row, self.sum_line())
                    kept.add(self.sum_line())
                    pltpu.make_async_copy(
                        self.sum_line(), self.done_rows(w_half), kept.sem
                    ).start()
                    self.m_back().start()
                    there = self.done_rows(w_half)
                    send_last(self.sum_line(), there, "e", from_middle, done_border)

            if n == 6:

                @pl.when(middle)
                def _():
                    self.m_back().wait_recv()
                    there = self.done_rows(1 - w_half)
                    send_last(there, there, "e", from_middle, done_border)

                for _ in range(2):
                    done_border.add(self.sum_line())

    class Deep:
        first_x = False

        def __init__(self, u):
            self.u = u
            self.k = UNITS[u][0]

        def one(self, i):
            src = cut(self.k, 2 * i + c, (1 - z_half) * EIGHTH * 2, 2 * EIGHTH)
            return send(self.u, 1, src, self.one_in(i), "e")

        def one_in(self, i):
            return y_in.at[self.k, pl.ds(i * 2 * EIGHTH, 2 * EIGHTH)]

        def two(self, i, side):
            row = row_one + (1 - w_half) * EIGHTH
            src = cut(self.k, 2 * i + c, row, EIGHTH, side * HALF, HALF)
            return send(self.u, 2, src, self.two_in(i, side), "w")

        def two_in(self, i, side):
            return x_in.at[self.k, pl.ds((2 * i + side) * EIGHTH, EIGHTH)]

        def x_sum(self, i):
            src = cut(self.k, 2 * i + c, row_two, EIGHTH, (1 - s) * HALF, HALF)
            return send(self.u, 3, src, self.x_in(i), "x")

        def x_in(self, i):
            return e_in.at[self.k, pl.ds(i * EIGHTH, EIGHTH)]

        def last(self):
            src = cut(self.k, yours, row_two, EIGHTH, s * HALF, HALF)
            return send(self.u, 4, src, self.x_in(2), "y")

        def piece(self):
            return cut(self.k, mine, row_two, EIGHTH, s * HALF, HALF)

        def own(self):
            there = final(self.k, row_two, EIGHTH)
            return pltpu.make_async_copy(self.piece(), there, g_recv.at[SEM_AT[self.u] + 7])

        def back(self, n):
            if n == 0:
                way = "x" if self.first_x else "w"
                return send(self.u, 5, self.piece(), final(self.k, row_two, EIGHTH), way)
            if self.first_x:
                here = final(self.k, row_two, EIGHTH, 0, D)
            else:
                here = final(self.k, row_one, 2 * EIGHTH)
            return send(self.u, 6, here, here, "w" if self.first_x else "e")

        def back_last(self):
            if self.first_x:
                here = final(self.k, row_one, 2 * EIGHTH, 0, D)
            else:
                here = final(self.k, 0, SHARD)
            send_last(here, here, "e" if self.first_x else "x")
            done.add(here)

        def step(self, n):
            if n == 1:
                for i in range(2):
                    self.one(i).start()
            if n == 2:
                wait_rows(self.u, 1, 4 * EIGHTH)
                for i in range(2):
                    add_to(cut(self.k, 2 * i + c, row_one, 2 * EIGHTH), self.one_in(i))
                    for side in range(2):
                        self.two(i, side).start()
            if n == 3:
                wait_rows(self.u, 2, 2 * EIGHTH)
                for i in range(2):
                    for side in range(2):
                        here = cut(self.k, 2 * i + c, row_two, EIGHTH, side * HALF, HALF)
                        add_to(here, self.two_in(i, side))
                    self.x_sum(i).start()
            if n == 4:
                wait_rows(self.u, 3, EIGHTH)
                for i in range(2):
                    here = cut(self.k, 2 * i + c, row_two, EIGHTH, s * HALF, HALF)
                    add_to(here, self.x_in(i))
                self.last().start()
            if n == 5:
                self.last().wait_recv()
                add_to(self.piece(), self.x_in(2))
                add_far(self.u, 0, self.piece())
                self.own().start()
                self.back(0).start()
            if n == 6:
                self.own().wait()
                self.back(0).wait_recv()
                self.back(1).start()
            if n == 7:
                self.back(1).wait_recv()
                self.back_last()

    class DeepX(Deep):
        first_x = True

    kinds = {"wide": Wide, "cross": Cross, "bounce": Bounce, "line": Line, "deep": Deep, "deep_x": DeepX}
    sums = [kinds[unit[3]](u) for u, unit in enumerate(UNITS)]

    def sum_step(u, n):
        if n == 0:
            for i in range(2):
                core_sum(u, i).start()
            return
        if n == 1:
            k, row, count, _ = UNITS[u]
            wait_rows(u, 0, 2 * count)
            for i in range(2):
                add_to(cut(k, 2 * i + c, row, count), core_in.at[k, i, pl.ds(row, count)])
        sums[u].step(n)

    def sums_done():
        factors.wait()
        to_core.wait()
        to_all.wait()
        if done.size:
            done.wait()

        @pl.when(border)
        def _():
            from_border.wait()
            if done_border.size:
                done_border.wait()

        @pl.when(middle)
        def _():
            from_middle.wait()
            kept.wait()
            if done_middle.size:
                done_middle.wait()

    vec_steps = 6 + extra
    vec_moves = []

    def vec_step(n):
        if n == 0:
            top = vec_grads[...]
            high = top.astype(LOW)
            low = (top - high.astype(F32)).astype(LOW)
            for seg in range(GROUPS):
                spread = spread_matrix(seg)
                vec_segs[seg] = dot_turned(high, spread) + dot_turned(low, spread)
            for row, parts in SEGMENTS.items():
                for seg, (q, at) in enumerate(parts):
                    vecs[q, at : at + 1, :] = vec_segs[seg, row : row + 1, :]
            for i in range(2):
                copy = remote(
                    vecs.at[2 * i + 1 - c], vec_in.at[i], v_send.at[3 + i], v_recv.at[3 + i], near["c"]
                )
                copy.start()
                vec_moves.append(copy)
            return
        if n == 1:
            for i in range(2):
                vec_moves[i].wait()
                vecs[2 * i + c] = vecs[2 * i + c] + vec_in[i]
        else:
            vec_moves[-1].wait()
            vecs[mine] = vecs[mine] + vec_in[n]
        steps = [near["y"], near["x"], near["e"], near["w"]] + far
        if n <= len(steps):
            copy = remote(
                vecs.at[yours if n == 1 else mine],
                vec_in.at[1 + n],
                v_send.at[4 + n],
                v_recv.at[4 + n],
                steps[n - 1],
            )
            copy.start()
            vec_moves.append(copy)
        else:
            copy = pltpu.make_async_copy(vecs.at[mine], vec_out, io_sem.at[2])
            copy.start()
            copy.wait()

    forward = [([], vectors_ready), ([], norm_first)]
    forward += [([QKV + n], functools.partial(project_block, n)) for n in range(3)]
    forward += [([], functools.partial(attend, w)) for w in range(windows)]
    forward += [([OUT], attend_out)]
    forward += [([FIN + n], functools.partial(inner_block, n)) for n in range(BLOCKS)]
    forward += [([8, 9, 10, 11], functools.partial(layer_part, 0))]
    forward += [([], functools.partial(layer_part, 1)), ([], layer_sort)]
    forward += [([12, 13], convolve_start), ([14, 15], convolve)]
    for item in GATHER_PLAN:
        if item < 0:
            need, work = forward.pop(0)
            for k in need:
                weight_ready(k)
            work()
        else:
            gather_step(item // 10, item % 10)
    gather_done()

    backward = [convolve_back, layer_back]
    for n in range(BLOCKS):
        backward += [functools.partial(active_back, n), functools.partial(out_grad, n)]
    backward.insert(5, pass_grads)
    backward[8:8] = [functools.partial(convolve_grad, side) for side in range(2)]
    backward += [inner_sum]
    backward += [
        functools.partial(weight_grad, FIN + n, normed_ffn, slope.at[n]) for n in range(BLOCKS)
    ]
    backward += [hidden_back, context_back]
    backward += [functools.partial(attend_back, w) for w in range(windows)]
    backward += [project_sum]
    backward += [functools.partial(weight_grad, QKV + n, normed, slope.at[n]) for n in range(3)]
    backward += [chars_back]
    backward += [functools.partial(vec_step, n) for n in range(vec_steps)]
    swaps = [functools.partial(swap, 0, mol_v, mols_out, mols)]
    for part in range(SWAP_PARTS):
        swaps.append(functools.partial(swap, 1, context, chars_out, rows, part, SWAP_PARTS))
    for item in PLAN:
        if item == -1:
            backward.pop(0)()
        elif item == -2:
            swaps.pop(0)()
        else:
            sum_step(item // 10, item % 10)
    for work in backward:
        work()
    sums_done()
    swaps_done()


def run(args, chars, extra):
    rows = chars.shape[0] // 2
    mols = rows // KERNEL
    anywhere = pl.BlockSpec(memory_space=pl.ANY)
    dma = pltpu.SemaphoreType.DMA
    vmem = pltpu.VMEM
    windows = rows // WIN
    return pl.pallas_call(
        functools.partial(program_kernel, rows, extra),
        name="layer_and_sums",
        out_shape=[
            jax.ShapeDtypeStruct((2 * mols, HALF), LOW),
            jax.ShapeDtypeStruct((2 * rows, HALF), LOW),
            jax.ShapeDtypeStruct(VEC, F32),
        ]
        + [jax.ShapeDtypeStruct(shape, LOW) for shape in SHARD_SHAPES]
        + [jax.ShapeDtypeStruct((len(UNITS), extra, SHARD, D), LOW)] * (extra > 0),
        in_specs=[anywhere, pl.BlockSpec(memory_space=vmem)] + [anywhere] * (len(args) - 2),
        out_specs=[anywhere] * (8 + (extra > 0)),
        scratch_shapes=[vmem((n * SHARD,), LOW) for n in VEC_COUNTS]
        + [
            vmem((COUNT * D, D), LOW),
            vmem((COUNT, 2, SHARD, D), LOW),
            vmem((CONV, SHARD, D), LOW),
            vmem((COUNT, SHARD, HALF), LOW),
            vmem((COUNT, SHARD, HALF), LOW),
            vmem((COUNT, SHARD, HALF), LOW),
            vmem((max(len(LINES), 1), SHARD // 2, D), LOW),
            vmem(VEC, F32),
            vmem((GROUPS,) + VEC, F32),
            vmem((GROUPS,) + VEC, F32),
            vmem((VEC[0], D), F32),
            vmem((VEC[0], D), F32),
            vmem((7 + extra,) + VEC, F32),
            vmem((rows, D), LOW),
            vmem((mols, D), LOW),
            vmem((rows, D), LOW),
            vmem((3, rows, D), LOW),
            vmem((windows, PAIRS, 2 * WIN, WIN), LOW),
            vmem((rows, D), LOW),
            vmem((rows, D), F32),
            vmem((rows, D), LOW),
            vmem((BLOCKS, rows, D), LOW),
            vmem((BLOCKS, rows, D), LOW),
            vmem((rows, D), F32),
            vmem((KERNEL, mols, D), LOW),
            vmem((rows, D), LOW),
            vmem((rows, D), F32),
            vmem((mols, D), LOW),
            vmem((GROUPS * mols, D), LOW),
            vmem((GROUPS * mols, D), LOW),
            dma((1,)),
            dma((3, len(PIECES))),
            dma((COUNT,)),
            dma((8,)),
            dma((SEMS,)),
            dma((len(UNITS), extra) if extra else (1, 1)),
            dma((len(UNITS), extra) if extra else (1, 1)),
            dma((9 + extra,)),
            dma((9 + extra,)),
            dma((5 + len(VEC_COUNTS),)),
            dma((4,)),
            dma((1,)),
            dma((6,)),
        ],
        compiler_params=pltpu.CompilerParams(
            collective_id=0, has_side_effects=True, vmem_limit_bytes=63 << 20
        ),
    )(*args)


def finish_kernel(mols, layer, vec, *refs):
    count = len(VEC_COUNTS)
    sums, (mols_out, layer_out), refs = refs[:5], refs[5:7], refs[7:]
    outs, vec_outs, flat, refs = refs[:5], refs[5 : 5 + count], refs[5 + count : 5 + 2 * count], refs[5 + 2 * count :]
    low, wide, load, store, whole, vec_sem, vec_held, mols_held, layer_held = refs
    loads = [
        pltpu.make_async_copy(shard_block(sums, k, 0, SHARD), low.at[k], load.at[k])
        for k in range(COUNT)
    ]
    through = [
        pltpu.make_async_copy(vec, vec_held, whole.at[2]),
        pltpu.make_async_copy(mols, mols_held, whole.at[0]),
        pltpu.make_async_copy(layer, layer_held, whole.at[1]),
    ]
    for copy in through + loads:
        copy.start()
    through[0].wait()
    at = 0
    copies = []
    for i, (ref, there, rows_held) in enumerate(zip(flat, vec_outs, VEC_COUNTS)):
        for j in range(rows_held):
            line = vec_held[at : at + 1, :][:, :SHARD].reshape(SHARD)
            ref[j * SHARD : (j + 1) * SHARD] = line
            at += 1
        copies.append(pltpu.make_async_copy(ref, there, vec_sem.at[i]))
        copies[-1].start()
    backs = [
        pltpu.make_async_copy(mols_held, mols_out, whole.at[0]),
        pltpu.make_async_copy(layer_held, layer_out, whole.at[1]),
    ]
    for before, after in zip(through[1:], backs):
        before.wait()
        after.start()
    for k in range(COUNT):
        loads[k].wait()
        wide[k] = low[k].astype(F32)
        copy = pltpu.make_async_copy(wide.at[k], shard_block(outs, k, 0, SHARD), store.at[k])
        copy.start()
        copies.append(copy)
    for copy in copies + backs:
        copy.wait()


def finish(mols, layer, vec, sums):
    anywhere = pl.BlockSpec(memory_space=pltpu.HBM)
    shape = jax.ShapeDtypeStruct
    vmem, dma = pltpu.VMEM, pltpu.SemaphoreType.DMA
    out = pl.pallas_call(
        finish_kernel,
        name="widen_sums",
        out_shape=[shape(mols.shape, LOW), shape(layer.shape, LOW)]
        + [shape(w.shape, F32) for w in sums]
        + [shape((n * SHARD,), F32) for n in VEC_COUNTS],
        in_specs=[anywhere] * 8,
        out_specs=[anywhere] * (7 + len(VEC_COUNTS)),
        scratch_shapes=[vmem((n * SHARD,), F32) for n in VEC_COUNTS]
        + [
            vmem((COUNT, SHARD, D), LOW),
            vmem((COUNT, SHARD, D), F32),
            dma((COUNT,)),
            dma((COUNT,)),
            dma((3,)),
            dma((len(VEC_COUNTS),)),
            vmem(VEC, F32),
            vmem(mols.shape, LOW),
            vmem(layer.shape, LOW),
        ],
        compiler_params=pltpu.CompilerParams(vmem_limit_bytes=60 << 20),
    )(mols, layer, vec, *sums)
    return out[0], out[1], out[2:7], out[7:]


def body(
    chars,
    char_codes,
    mol_cotangent,
    attn_norm_gain,
    attn_norm_bias,
    qkv_weight,
    qv_bias,
    out_weight,
    out_bias,
    ffn_norm_gain,
    ffn_norm_bias,
    ffn_in_weight,
    ffn_in_bias,
    ffn_out_weight,
    ffn_out_bias,
    conv_weight,
    conv_bias,
    down_norm_gain,
    down_norm_bias,
):
    vectors = [
        attn_norm_gain,
        attn_norm_bias,
        qv_bias,
        out_bias,
        ffn_norm_gain,
        ffn_norm_bias,
        ffn_in_bias,
        ffn_out_bias,
        conv_bias,
        down_norm_gain,
        down_norm_bias,
    ]
    result = run(
        (
            chars,
            char_codes.reshape(-1, WIN),
            mol_cotangent,
            qkv_weight,
            out_weight,
            ffn_in_weight,
            ffn_out_weight,
            conv_weight,
            *vectors,
        ),
        chars,
        (lax.axis_size("replica") // RING).bit_length() - 1,
    )
    molecules, chars_grad, big, v = finish(*result[:3], result[3:8])
    t_qkv, t_out, t_in, t_ffo, t_conv = big
    return (
        molecules,
        chars_grad,
        v[0],
        v[1],
        t_qkv,
        v[2],
        t_out,
        v[3],
        v[4],
        v[5],
        t_in,
        v[6],
        t_ffo,
        v[7],
        t_conv,
        v[8],
        v[9],
        v[10],
    )


def solution(mesh):
    return jax.shard_map(
        body,
        mesh=mesh,
        in_specs=(
            P(("group", "replica"), None),
            P(("group", "replica")),
            P(("group", "replica"), None),
            P("group"),
            P("group"),
            P("group", None),
            P("group"),
            P("group", None),
            P("group"),
            P("group"),
            P("group"),
            P("group", None),
            P("group"),
            P("group", None),
            P("group"),
            P("group", None),
            P("group"),
            P("group"),
            P("group"),
        ),
        out_specs=(
            P(("group", "replica"), "section"),
            P(("group", "replica"), "section"),
            P("group"),
            P("group"),
            P("group", None),
            P("group"),
            P("group", None),
            P("group"),
            P("group"),
            P("group"),
            P("group", None),
            P("group"),
            P("group", None),
            P("group"),
            P("group", None),
            P("group"),
            P("group"),
            P("group"),
        ),
        check_vma=False,
    )
```
